32 devices in a mesh: batch: 2 (over x), seq: 4 (over y, core), head: 4 (over z).
Axes of the slice: x: 2, y: 2, z: 4, core: 2. Of those that a mesh axis runs over, the one named last changes fastest.
Arguments:
- inputs: bfloat16 [16, 1024, 1024], P('batch', ('seq', 'head')), may hold values from -6 to 6
- memory: bfloat16 [16, 1024, 1024], P('batch', ('seq', 'head')), may hold values from -6 to 6
- cotangent: bfloat16 [16, 1024, 1024], P('batch', ('seq', 'head')), may hold values from -6 to 6
- tgt_lengths: int32 [16, 16], P('batch'), may hold values from 1 to 1009, as said below
- src_ids: int32 [16, 1024], P('batch'), may hold values from 0 to 15, as said below
- gain_one: float32 [1024], replicated, may hold values from 0.5 to 1.5
- w_query: bfloat16 [1024, 1024], P(None, 'head'), may hold values from -0.1875 to 0.1875
- w_key: bfloat16 [1024, 1024], P(None, 'head'), may hold values from -0.1875 to 0.1875
- w_value: bfloat16 [1024, 1024], P(None, 'head'), may hold values from -0.1875 to 0.1875
- w_out: bfloat16 [1024, 1024], P('head'), may hold values from -0.75 to 0.75
- gain_two: float32 [1024], replicated, may hold values from 0.5 to 1.5
- w_cross_query: bfloat16 [1024, 1024], P(None, 'head'), may hold values from -0.1875 to 0.1875
- w_mem_key: bfloat16 [1024, 1024], P(None, 'head'), may hold values from -0.1875 to 0.1875
- w_mem_value: bfloat16 [1024, 1024], P(None, 'head'), may hold values from -0.1875 to 0.1875
- w_cross_out: bfloat16 [1024, 1024], P('head'), may hold values from -0.75 to 0.75
- gain_three: float32 [1024], replicated, may hold values from 0.5 to 1.5
- w_up: bfloat16 [1024, 4096], P(None, 'head'), may hold values from -0.1875 to 0.1875
- w_down: bfloat16 [4096, 1024], P('head'), may hold values from -0.09375 to 0.09375
Outputs:
- output: bfloat16 [16, 1024, 1024], P('batch', ('seq', 'head'))
- grad_inputs: float32 [16, 1024, 1024], P('batch', ('seq', 'head'))
- grad_memory: float32 [16, 1024, 1024], P('batch', ('seq', 'head'))
- grad_gain_one: float32 [1024], replicated
- grad_w_query: float32 [1024, 1024], P(None, 'head')
- grad_w_key: float32 [1024, 1024], P(None, 'head')
- grad_w_value: float32 [1024, 1024], P(None, 'head')
- grad_w_out: float32 [1024, 1024], P('head')
- grad_gain_two: float32 [1024], replicated
- grad_w_cross_query: float32 [1024, 1024], P(None, 'head')
- grad_w_mem_key: float32 [1024, 1024], P(None, 'head')
- grad_w_mem_value: float32 [1024, 1024], P(None, 'head')
- grad_w_cross_out: float32 [1024, 1024], P('head')
- grad_gain_three: float32 [1024], replicated
- grad_w_up: float32 [1024, 4096], P(None, 'head')
- grad_w_down: float32 [4096, 1024], P('head')
The draws below stay inside these ranges and needn't reach their ends.
Inputs may be any that keep to these rules, and one draw needn't show every extreme that they name: `tgt_lengths`: each row's lengths are positive and add up to 1024. `src_ids`: non-decreasing along each row; every value from 0 to 15 occurs in every row.
All inputs are finite; a program needn't handle non-finite values.
Results may differ from the reference program's by a relative error of at most 0.02.
Values may be sent and summed in bfloat16 or wider, within the bound.
No kernel may reach another device: no remote copies, remote signals or barrier semaphores. Data moves between devices by JAX's collectives and lax.ppermute only.
A program may use at most 512 MiB of HBM per device.

```python
import jax
import jax.numpy as jnp
from jax import lax

D = 1024
HEADS = 16
HEAD_DIM = 64
FF = 4096
LEN = 1024
NSEG = 16
ROWS_B = 8
ROWS = 16


def long_rows(key):
    pick_key = jax.random.fold_in(key, 11)
    place_key = jax.random.fold_in(key, 12)
    groups = ROWS // ROWS_B
    chosen = jax.random.randint(pick_key, (groups,), 0, ROWS_B)
    row_index = jnp.arange(ROWS, dtype=jnp.int32)
    is_long = row_index % ROWS_B == jnp.repeat(chosen, ROWS_B)
    long_slot = jax.random.randint(place_key, (ROWS,), 0, NSEG)
    return (is_long, long_slot)


def row_lengths(key, is_long, long_slot):

    def one_row(row_key):
        cut_points = jax.random.permutation(row_key, LEN - 1)[:NSEG - 1] + 1
        bounds = jnp.concatenate([jnp.zeros((1,), jnp.int32), jnp.sort(cut_points).astype(jnp.int32), jnp.full((1,), LEN, jnp.int32)])
        return bounds[1:] - bounds[:-1]
    drawn_rows = jax.vmap(one_row)(jax.random.split(key, ROWS))
    places = jnp.arange(NSEG, dtype=jnp.int32)
    stretched = jnp.where(places[None, :] == long_slot[:, None], LEN - NSEG + 1, 1).astype(jnp.int32)
    return jnp.where(is_long[:, None], stretched, drawn_rows).astype(jnp.int32)


def draw_tgt_lengths(key, part):
    is_long, long_slot = long_rows(key)
    key = jax.random.fold_in(key, 3)
    return row_lengths(key, is_long, long_slot)


def draw_src_ids(key, part):
    is_long, long_slot = long_rows(key)
    key = jax.random.fold_in(key, 5)
    lengths = row_lengths(key, is_long, long_slot)
    segment_ends = jnp.cumsum(lengths, -1)[:, :-1]
    positions = jnp.arange(LEN, dtype=jnp.int32)
    return jnp.sum((positions[None, :, None] >= segment_ends[:, None, :]).astype(jnp.int32), -1).astype(jnp.int32)


def level_of(stream_key, dims, shards, least, largest):
    loudness = 1.0
    for position, parts in shards:
        draws = jax.random.uniform(jax.random.fold_in(jax.random.fold_in(stream_key, 6), position), (parts,), jnp.float32, least / len(shards), largest / len(shards))
        loudness = loudness * jnp.repeat(jnp.exp(draws), dims[position] // parts).reshape((-1,) + (1,) * (len(dims) - 1 - position))
    return loudness


def normal_values(stream_key, shape, width, most, cuts=(), held_as=jnp.bfloat16):
    level = level_of(stream_key, shape, cuts, -0.22, 0.18) if cuts else 1.0
    values = jax.random.normal(stream_key, shape, jnp.float32) * width * level
    return jnp.minimum(jnp.maximum(values, -most), most).astype(held_as)


def setup_inputs(seed: int = 0) -> dict:
    key_of = jax.random.split(jax.random.key(seed), 19)
    inputs = normal_values(key_of[0], (ROWS, LEN, D), 1.0, 6.0, ((0, 2), (1, 16)))
    memory = normal_values(key_of[1], (ROWS, LEN, D), 1.0, 6.0, ((0, 2), (1, 16)))
    cotangent = normal_values(key_of[2], (ROWS, LEN, D), 1.0, 6.0, ((0, 2), (1, 16)))
    tgt_lengths = draw_tgt_lengths(jax.random.fold_in(key_of[18], 71), 0)
    src_ids = draw_src_ids(jax.random.fold_in(key_of[18], 71), 0)
    gain_one = jnp.clip(1.0 + 0.1 * jax.random.normal(key_of[5], (D,), jnp.float32), 0.5, 1.5)
    w_query = normal_values(key_of[6], (D, HEADS * HEAD_DIM), D ** -0.5, 0.1875, ((1, 4),))
    w_key = normal_values(key_of[7], (D, HEADS * HEAD_DIM), D ** -0.5, 0.1875, ((1, 4),))
    w_value = normal_values(key_of[8], (D, HEADS * HEAD_DIM), D ** -0.5, 0.1875, ((1, 4),))
    w_out = normal_values(key_of[9], (HEADS * HEAD_DIM, D), (HEADS * HEAD_DIM // 16) ** -0.5, 0.75, ((0, 4),))
    gain_two = jnp.clip(1.0 + 0.1 * jax.random.normal(key_of[10], (D,), jnp.float32), 0.5, 1.5)
    w_cross_query = normal_values(key_of[11], (D, HEADS * HEAD_DIM), D ** -0.5, 0.1875, ((1, 4),))
    w_mem_key = normal_values(key_of[12], (D, HEADS * HEAD_DIM), D ** -0.5, 0.1875, ((1, 4),))
    w_mem_value = normal_values(key_of[13], (D, HEADS * HEAD_DIM), D ** -0.5, 0.1875, ((1, 4),))
    w_cross_out = normal_values(key_of[14], (HEADS * HEAD_DIM, D), (HEADS * HEAD_DIM // 16) ** -0.5, 0.75, ((0, 4),))
    gain_three = jnp.clip(1.0 + 0.1 * jax.random.normal(key_of[15], (D,), jnp.float32), 0.5, 1.5)
    w_up = normal_values(key_of[16], (D, FF), D ** -0.5, 0.1875, ((1, 4),))
    w_down = normal_values(key_of[17], (FF, D), FF ** -0.5, 0.09375, ((0, 4),))
    return dict(inputs=inputs, memory=memory, cotangent=cotangent, tgt_lengths=tgt_lengths, src_ids=src_ids, gain_one=gain_one, w_query=w_query, w_key=w_key, w_value=w_value, w_out=w_out, gain_two=gain_two, w_cross_query=w_cross_query, w_mem_key=w_mem_key, w_mem_value=w_mem_value, w_cross_out=w_cross_out, gain_three=gain_three, w_up=w_up, w_down=w_down)


@jax.custom_vjp
def low(v):
    return lax.optimization_barrier(v.astype(jnp.bfloat16)).astype(jnp.float32)

@jax.custom_vjp
def low_back(v):
    return v

def low_keep(v):
    return (low(v), None)

def low_pass(kept, grad):
    return (grad,)

def back_keep(v):
    return (v, None)

def back_low(kept, grad):
    return (low(grad),)
low.defvjp(low_keep, low_pass)
low_back.defvjp(back_keep, back_low)
EPSILON = 1e-05
MASKED = -1000000000.0

def product(left, right):
    return jnp.matmul(left, right, precision=lax.Precision.HIGHEST)

def normalize(activity, gain_vector):
    centre = lax.optimization_barrier(jnp.mean(activity, -1, keepdims=True))
    shifted = activity - centre
    variance = lax.optimization_barrier(jnp.mean(shifted * shifted, -1, keepdims=True))
    return shifted * lax.rsqrt(variance + EPSILON) * gain_vector

def segment_ids(lengths):
    segment_ends = jnp.cumsum(lengths, -1)[:-1]
    positions = jnp.arange(LEN, dtype=jnp.int32)
    return lax.optimization_barrier(jnp.sum((positions[:, None] >= segment_ends[None, :]).astype(jnp.int32), -1))

def attention(queries, key_rows, value_rows, allowed):
    query_len = queries.shape[0]
    key_len = key_rows.shape[0]
    query_four = queries.reshape(query_len, HEADS, HEAD_DIM)
    key_four = key_rows.reshape(key_len, HEADS, HEAD_DIM)
    value_four = value_rows.reshape(key_len, HEADS, HEAD_DIM)
    raw_scores = jnp.einsum('qhe,khe->hqk', query_four, key_four, precision=lax.Precision.HIGHEST)
    scores = low_back(raw_scores * HEAD_DIM ** (-0.5))
    scores = jnp.where(allowed[None], scores, MASKED)
    highest = lax.optimization_barrier(jnp.max(scores, -1, keepdims=True))
    weights = jnp.exp(scores - highest)
    probs_full = weights / lax.optimization_barrier(jnp.sum(weights, -1, keepdims=True))
    mixed = jnp.einsum('hqk,khe->qhe', low(probs_full), value_four, precision=lax.Precision.HIGHEST)
    return mixed.reshape(query_len, HEADS * HEAD_DIM)

def reference(inputs, memory, cotangent, tgt_lengths, src_ids, gain_one, w_query, w_key, w_value, w_out, gain_two, w_cross_query, w_mem_key, w_mem_value, w_cross_out, gain_three, w_up, w_down):

    def layer(input_all, memory_all, gain_a, weight_q, weight_k, weight_v, weight_o, gain_b, weight_cq, weight_mk, weight_mv, weight_co, gain_c, weight_up, weight_down):

        def one_row(row_items):
            residual, source, lengths, source_ids = row_items
            target_ids = segment_ids(lengths)
            positions = jnp.arange(LEN, dtype=jnp.int32)
            self_allowed = (target_ids[:, None] == target_ids[None, :]) & (positions[None, :] <= positions[:, None])
            cross_allowed = target_ids[:, None] == source_ids[None, :]
            normed_one = low(normalize(residual, gain_a))
            queries = low(low_back(product(normed_one, weight_q)))
            key_rows = low(low_back(product(normed_one, weight_k)))
            value_rows = low(low_back(product(normed_one, weight_v)))
            mem_keys = low(low_back(product(source, weight_mk)))
            mem_values = low(low_back(product(source, weight_mv)))
            self_mixed = low(low_back(attention(queries, key_rows, value_rows, self_allowed)))
            after_self = residual + low_back(product(self_mixed, weight_o))
            normed_two = low(normalize(after_self, gain_b))
            cross_queries = low(low_back(product(normed_two, weight_cq)))
            cross_mixed = low(low_back(attention(cross_queries, mem_keys, mem_values, cross_allowed)))
            after_cross = after_self + low_back(product(cross_mixed, weight_co))
            normed_three = low(normalize(after_cross, gain_c))
            hidden_pre = low_back(product(normed_three, weight_up))
            hidden_act = low(jax.nn.gelu(hidden_pre, approximate=True))
            return after_cross + low_back(product(hidden_act, weight_down))
        return lax.map(jax.checkpoint(one_row), (input_all, memory_all, tgt_lengths, src_ids))
    weight_list = (w_query, w_key, w_value, w_out)
    cross_list = (w_cross_query, w_mem_key, w_mem_value, w_cross_out)
    output, pullback = jax.vjp(layer, inputs.astype(jnp.float32), memory.astype(jnp.float32), gain_one, *[matrix.astype(jnp.float32) for matrix in weight_list], gain_two, *[matrix.astype(jnp.float32) for matrix in cross_list], gain_three, w_up.astype(jnp.float32), w_down.astype(jnp.float32))
    grads = pullback(cotangent.astype(jnp.float32))
    return (output.astype(jnp.bfloat16), grads[0], grads[1], grads[2], grads[3], grads[4], grads[5], grads[6], grads[7], grads[8], grads[9], grads[10], grads[11], grads[12], grads[13], grads[14])
```

```python
import jax
import jax.numpy as jnp
from jax import lax
from jax.sharding import Mesh
from jax.sharding import PartitionSpec as P

HEAD_DIM = 64
LEN = 1024
EPSILON = 1e-05
MASKED = -1000000000.0
BF = jnp.bfloat16
F32 = jnp.float32
SWAP = [(0, 1), (1, 0)]


def dot(left, right, left_dim, right_dim):
    return lax.dot_general(
        left, right, (((left_dim,), (right_dim,)), ((), ())), preferred_element_type=F32
    )


def normalize(activity, gain):
    centre = jnp.mean(activity, -1, keepdims=True)
    shifted = activity - centre
    variance = jnp.mean(shifted * shifted, -1, keepdims=True)
    return (shifted * lax.rsqrt(variance + EPSILON) * gain).astype(BF)


def normalize_back(activity, gain, grad):
    centre = jnp.mean(activity, -1, keepdims=True)
    shifted = activity - centre
    variance = jnp.mean(shifted * shifted, -1, keepdims=True)
    rate = lax.rsqrt(variance + EPSILON)
    unit = shifted * rate
    scaled = grad * gain
    inner = scaled - jnp.mean(scaled, -1, keepdims=True)
    grad_activity = rate * (inner - unit * jnp.mean(scaled * unit, -1, keepdims=True))
    return grad_activity, jnp.sum(grad * unit, 0)


def core_swap(piece):
    return lax.ppermute(piece, "core", SWAP)


def both(own):
    return jnp.concatenate([own, core_swap(own)], 0)


def own_sum(partial):
    half = partial.shape[0] // 2
    other = core_swap(partial[half:].astype(BF))
    return partial[:half] + other.astype(F32)


def to_row(tokens):
    rows, span, width = tokens.shape
    moved = lax.all_to_all(tokens, ("yy", "head"), 0, 0, tiled=True)
    return moved.reshape(rows * span, width)


def from_row(own, rows):
    parts = own.reshape(rows, own.shape[0] // rows, own.shape[1])
    return lax.all_to_all(parts, ("yy", "head"), 0, 0, tiled=True)


def gather_weight(piece):
    rows, width = piece.shape
    along = lax.all_gather(piece, "head", axis=0, tiled=False)
    for axis in ("yy", "batch"):
        along = lax.all_gather(along, axis, axis=1, tiled=False)
    return along.reshape(along.shape[0], -1, width)


def halve(grads, axis, dim):
    count = lax.axis_size(axis)
    if count == 2:
        index = lax.axis_index(axis)
        mine = lax.dynamic_index_in_dim(grads, index, dim, keepdims=False)
        other = lax.dynamic_index_in_dim(grads, 1 - index, dim, keepdims=False)
        return (mine.astype(F32) + lax.ppermute(other, axis, SWAP).astype(F32)).astype(BF)
    return lax.psum_scatter(grads, axis, scatter_dimension=dim, tiled=False)


def sum_weight(grads):
    heads, total, width = grads.shape
    nx, ny = lax.axis_size("batch"), lax.axis_size("yy")
    cut = grads.astype(BF).reshape(heads, nx, ny, total // (nx * ny), width)
    first = halve(halve(cut[: heads // 2], "batch", 1), "yy", 1)
    second = halve(halve(cut[heads // 2 :], "yy", 2), "batch", 1)
    cut = jnp.concatenate([first, second], 0)
    cut = lax.all_to_all(cut, "head", 0, 0, tiled=True)
    summed = jnp.sum(cut.astype(F32), 0).astype(BF)
    summed = lax.all_gather(summed, "yy", axis=0, tiled=True)
    return lax.all_gather(summed, "batch", axis=0, tiled=True)


def chances_of(query, keys, allowed):
    scores = jnp.einsum("qhe,khe->hqk", query, keys, preferred_element_type=F32)
    scores = jnp.where(allowed[None], scores * HEAD_DIM**-0.5, MASKED)
    weights = jnp.exp(scores - jnp.max(scores, -1, keepdims=True))
    return weights / jnp.sum(weights, -1, keepdims=True)


def heads_of(matrix):
    return matrix.reshape(matrix.shape[0], -1, HEAD_DIM)


def attend(query, keys, values, allowed):
    chances = chances_of(heads_of(query), heads_of(keys), allowed)
    mixed = jnp.einsum("hqk,khe->qhe", chances.astype(BF), heads_of(values), preferred_element_type=F32)
    return mixed.astype(BF).reshape(query.shape)


def attend_back(query, keys, values, allowed, grad):
    query, keys, values, grad = (heads_of(m) for m in (query, keys, values, grad))
    chances = chances_of(query, keys, allowed)
    grad_chances = jnp.einsum("qhe,khe->hqk", grad, values, preferred_element_type=F32)
    inner = jnp.sum(chances * grad_chances, -1, keepdims=True)
    grad_scores = (chances * (grad_chances - inner)).astype(BF)
    scale = HEAD_DIM**-0.5
    gq = jnp.einsum("hqk,khe->qhe", grad_scores, keys, preferred_element_type=F32) * scale
    gk = jnp.einsum("hqk,qhe->khe", grad_scores, query, preferred_element_type=F32) * scale
    gv = jnp.einsum("hqk,qhe->khe", chances.astype(BF), grad, preferred_element_type=F32)
    return tuple(m.astype(BF).reshape(m.shape[0], -1) for m in (gq, gk, gv))


def body(
    inputs,
    memory,
    cotangent,
    tgt_lengths,
    src_ids,
    gain_one,
    w_query,
    w_key,
    w_value,
    w_out,
    gain_two,
    w_cross_query,
    w_mem_key,
    w_mem_value,
    w_cross_out,
    gain_three,
    w_up,
    w_down,
):
    nx, ny, nz = (lax.axis_size(a) for a in ("batch", "yy", "head"))
    ix, iy, core, iz = (lax.axis_index(a) for a in ("batch", "yy", "core", "head"))
    rows = inputs.shape[0]
    nxy, place = nx * ny, ix * ny + iy

    def column_part(*matrices):
        parts = []
        for matrix in matrices:
            deep, wide = matrix.shape[0] // nxy, matrix.shape[1] // 2
            parts.append(lax.dynamic_slice(matrix, (place * deep, core * wide), (deep, wide)))
        return jnp.concatenate(parts, 1) if len(parts) > 1 else parts[0]

    def row_part(matrix):
        deep = matrix.shape[0] // 2 // nxy
        return lax.dynamic_slice_in_dim(matrix, (core * nxy + place) * deep, deep, 0)

    def spread(tokens, gathered):
        return jnp.einsum("td,zdf->tzf", tokens, gathered, preferred_element_type=F32)

    def spread_back(grads, gathered):
        return jnp.einsum("tzf,zdf->td", grads, gathered, preferred_element_type=F32)

    def flat(matrix):
        return matrix.reshape(matrix.shape[0], -1)

    def tall(gathered):
        return gathered.reshape(-1, gathered.shape[2])

    row = iy * nz + iz
    lengths = lax.dynamic_index_in_dim(tgt_lengths, row, 0, keepdims=False)
    source_ids = lax.dynamic_index_in_dim(src_ids, row, 0, keepdims=False)
    positions = jnp.arange(LEN, dtype=jnp.int32)
    ends = jnp.cumsum(lengths)[:-1]
    target_ids = jnp.sum((positions[:, None] >= ends[None, :]).astype(jnp.int32), -1)

    def ordered(values):
        cut = values.reshape(ny, 2, -1)
        own = lax.dynamic_index_in_dim(cut, core, 1, keepdims=False)
        other = lax.dynamic_index_in_dim(cut, 1 - core, 1, keepdims=False)
        return jnp.concatenate([own.reshape(-1), other.reshape(-1)])

    target_ids, source_ids, positions = ordered(target_ids), ordered(source_ids), ordered(positions)
    self_allowed = (target_ids[:, None] == target_ids[None, :]) & (
        positions[None, :] <= positions[:, None]
    )
    cross_allowed = target_ids[:, None] == source_ids[None, :]

    residual = to_row(inputs).astype(F32)
    source = both(to_row(memory))
    cot_own = to_row(cotangent)
    cot = both(cot_own)

    w_self = gather_weight(column_part(w_query, w_key, w_value))
    w_o = tall(gather_weight(row_part(w_out)))
    w_mem = gather_weight(column_part(w_mem_key, w_mem_value))
    w_cq = gather_weight(column_part(w_cross_query))
    w_co = tall(gather_weight(row_part(w_cross_out)))
    w_u = gather_weight(column_part(w_up))
    w_d = tall(gather_weight(row_part(w_down)))

    normed_one = both(normalize(residual, gain_one))
    qkv = spread(normed_one, w_self).astype(BF)
    part = w_query.shape[1] // 2
    q, k, v = (flat(qkv[:, :, i * part : (i + 1) * part]) for i in range(3))
    mkv = spread(source, w_mem).astype(BF)
    mk, mv = (flat(mkv[:, :, i * part : (i + 1) * part]) for i in range(2))

    self_mixed = attend(q, k, v, self_allowed)
    after_self = residual + own_sum(dot(self_mixed, w_o, 1, 0))
    normed_two = both(normalize(after_self, gain_two))
    cq = flat(spread(normed_two, w_cq).astype(BF))
    cross_mixed = attend(cq, mk, mv, cross_allowed)
    after_cross = after_self + own_sum(dot(cross_mixed, w_co, 1, 0))
    normed_three = both(normalize(after_cross, gain_three))
    hidden_pre = spread(normed_three, w_u)
    hidden_act, gate_pull = jax.vjp(lambda p: jax.nn.gelu(p, approximate=True), hidden_pre)
    hidden_act = flat(hidden_act.astype(BF))
    output = (after_cross + own_sum(dot(hidden_act, w_d, 1, 0))).astype(BF)
    output = from_row(output, rows)

    def stacked(grads):
        return grads.reshape(nz, -1, grads.shape[1])

    g_down = sum_weight(stacked(dot(hidden_act, cot, 0, 0)))
    grad_pre = gate_pull(dot(cot, w_d, 1, 1).reshape(hidden_pre.shape))[0].astype(BF)
    g_up = sum_weight(jnp.einsum("td,tzf->zdf", normed_three, grad_pre, preferred_element_type=F32))
    third_back = own_sum(spread_back(grad_pre, w_u))
    step, grad_gain_three = normalize_back(after_cross, gain_three, third_back)
    grad_after_cross = cot_own.astype(F32) + step

    cross_grad = both(grad_after_cross.astype(BF))
    g_co = sum_weight(stacked(dot(cross_mixed, cross_grad, 0, 0)))
    grad_cross_mixed = dot(cross_grad, w_co, 1, 1).astype(BF)
    gcq, gmk, gmv = attend_back(cq, mk, mv, cross_allowed, grad_cross_mixed)

    def three(matrix):
        return matrix.reshape(matrix.shape[0], nz, -1)

    gcq = three(gcq)
    gmkv = jnp.concatenate([three(gmk), three(gmv)], 2)
    g_cq = sum_weight(jnp.einsum("td,tzf->zdf", normed_two, gcq, preferred_element_type=F32))
    g_mem = sum_weight(jnp.einsum("td,tzf->zdf", source, gmkv, preferred_element_type=F32))
    second_back = own_sum(spread_back(gcq, w_cq))
    grad_memory = own_sum(spread_back(gmkv, w_mem))
    grad_memory = from_row(grad_memory.astype(BF), rows).astype(F32)
    step, grad_gain_two = normalize_back(after_self, gain_two, second_back)
    grad_after_self = grad_after_cross + step

    self_grad = both(grad_after_self.astype(BF))
    g_o = sum_weight(stacked(dot(self_mixed, self_grad, 0, 0)))
    grad_self_mixed = dot(self_grad, w_o, 1, 1).astype(BF)
    gq, gk, gv = attend_back(q, k, v, self_allowed, grad_self_mixed)
    gqkv = jnp.concatenate([three(gq), three(gk), three(gv)], 2)
    g_self = sum_weight(jnp.einsum("td,tzf->zdf", normed_one, gqkv, preferred_element_type=F32))
    first_back = own_sum(spread_back(gqkv, w_self))
    step, grad_gain_one = normalize_back(residual, gain_one, first_back)
    grad_inputs = from_row((grad_after_self + step).astype(BF), rows).astype(F32)

    gains = lax.psum(
        jnp.stack([grad_gain_one, grad_gain_two, grad_gain_three]), ("batch", "yy", "core", "head")
    )

    def cored(grads, dim):
        other = core_swap(grads)
        low = jnp.where(core == 0, grads, other)
        high = jnp.where(core == 0, other, grads)
        return low.astype(F32), high.astype(F32)

    def columns(grads, count):
        low, high = cored(grads, 1)
        wide = grads.shape[1] // count
        return [
            jnp.concatenate([low[:, i * wide : (i + 1) * wide], high[:, i * wide : (i + 1) * wide]], 1)
            for i in range(count)
        ]

    def tall_rows(grads):
        return jnp.concatenate(cored(grads, 0), 0)

    grad_q, grad_k, grad_v = columns(g_self, 3)
    grad_mk, grad_mv = columns(g_mem, 2)
    return (
        output,
        grad_inputs,
        grad_memory,
        gains[0],
        grad_q,
        grad_k,
        grad_v,
        tall_rows(g_o),
        gains[1],
        columns(g_cq, 1)[0],
        grad_mk,
        grad_mv,
        tall_rows(g_co),
        gains[2],
        columns(g_up, 1)[0],
        tall_rows(g_down),
    )


def solution(mesh):
    nb, ns, nh = (mesh.shape[a] for a in ("batch", "seq", "head"))
    fine = Mesh(mesh.devices.reshape(nb, ns // 2, 2, nh), ("batch", "yy", "core", "head"))
    tokens = P("batch", ("yy", "core", "head"), None)
    ids = P("batch", None)
    wide, tall = P(None, "head"), P("head", None)
    return jax.shard_map(
        body,
        mesh=fine,
        in_specs=(
            tokens, tokens, tokens, ids, ids,
            P(), wide, wide, wide, tall,
            P(), wide, wide, wide, tall,
            P(), wide, tall,
        ),
        out_specs=(
            tokens, tokens, tokens,
            P(), wide, wide, wide, tall,
            P(), wide, wide, wide, tall,
            P(), wide, tall,
        ),
        check_vma=False,
    )
```

```python
import functools

import jax
import jax.numpy as jnp
from jax import lax
from jax.experimental import pallas as pl
from jax.experimental.pallas import tpu as pltpu
from jax.sharding import Mesh
from jax.sharding import PartitionSpec as P

HEAD_DIM = 64
LEN = 1024
BLOCK = 256
BLOCKS = LEN // BLOCK
EPSILON = 1e-05
MASKED = -1000000000.0
SCALE = HEAD_DIM**-0.5
BF = jnp.bfloat16
F32 = jnp.float32


def dot(left, right, left_dim, right_dim):
    return lax.dot_general(
        left, right, (((left_dim,), (right_dim,)), ((), ())), preferred_element_type=F32
    )


def normalize(activity, gain):
    centre = jnp.mean(activity, -1, keepdims=True)
    shifted = activity - centre
    variance = jnp.mean(shifted * shifted, -1, keepdims=True)
    return (shifted * lax.rsqrt(variance + EPSILON) * gain).astype(BF)


def normalize_back(activity, gain, grad):
    centre = jnp.mean(activity, -1, keepdims=True)
    shifted = activity - centre
    variance = jnp.mean(shifted * shifted, -1, keepdims=True)
    rate = lax.rsqrt(variance + EPSILON)
    unit = shifted * rate
    scaled = grad * gain
    inner = scaled - jnp.mean(scaled, -1, keepdims=True)
    grad_activity = rate * (inner - unit * jnp.mean(scaled * unit, -1, keepdims=True))
    return grad_activity, jnp.sum(grad * unit, 0)


def shift(piece, axis, step):
    count = lax.axis_size(axis)
    return lax.ppermute(piece, axis, [(i, (i + step) % count) for i in range(count)])


def core_swap(piece):
    return shift(piece, "core", 1)


def both(own):
    return jnp.concatenate([own, core_swap(own)], 0)


def own_sum(transposed, matrix):
    half = transposed.shape[1] // 2
    other = core_swap(dot(transposed[:, half:], matrix, 0, 0).astype(BF))
    return dot(transposed[:, :half], matrix, 0, 0) + other.astype(F32)


def to_row(tokens):
    rows, span, width = tokens.shape
    moved = lax.all_to_all(tokens, ("yy", "head"), 0, 0, tiled=True)
    return moved.reshape(rows * span, width)


def from_row(own, rows):
    parts = own.reshape(rows, own.shape[0] // rows, own.shape[1])
    return lax.all_to_all(parts, ("yy", "head"), 0, 0, tiled=True)


def ring(piece, axis):
    count = lax.axis_size(axis)
    return jnp.stack([piece] + [shift(piece, axis, k) for k in range(1, count)], 0)


def gather_weight(piece):
    along = ring(piece, "head")
    half = along.shape[0] // 2
    first = ring(ring(along[:half], "batch"), "yy")
    second = ring(ring(along[half:], "yy"), "batch")
    return first, second


def fold(grads, axis):
    count = lax.axis_size(axis)
    total = grads[0].astype(F32)
    for k in range(1, count):
        total = total + shift(grads[k], axis, -k).astype(F32)
    return total.astype(BF)


def sum_weight(grads, rows):
    nx, ny, nz = (lax.axis_size(a) for a in ("batch", "yy", "head"))
    half = grads.shape[0] // 2
    width = grads.shape[1]
    first = grads[:half].reshape(ny, nx, nz // 2, rows, width)
    second = grads[half:].reshape(nx, ny, nz // 2, rows, width)
    first = fold(fold(first, "yy"), "batch")
    second = fold(fold(second, "batch"), "yy")
    total = first[0].astype(F32)
    for k in range(1, nz):
        slot = first[k] if k < nz // 2 else second[k - nz // 2]
        total = total + shift(slot, "head", -k).astype(F32)
    return total.astype(BF)


def in_place(piece, axis):
    if lax.axis_size(axis) != 2:
        return lax.all_gather(piece, axis, axis=0, tiled=False)
    other = shift(piece, axis, 1)
    low = lax.axis_index(axis) == 0
    return jnp.stack([jnp.where(low, piece, other), jnp.where(low, other, piece)], 0)


def replicate(piece):
    return in_place(in_place(in_place(piece, "yy"), "batch"), "core")


def total_of(value):
    for axis in ("core", "yy", "batch", "head"):
        count = lax.axis_size(axis)
        step = 1
        while step < count:
            value = value + lax.ppermute(value, axis, [(i, i ^ step) for i in range(count)])
            step *= 2
    return value


def head_rows(ref, half, index, kind):
    x, z = index
    if ref.shape[5] == HEAD_DIM:
        return (0, 0, x, z, kind)
    return (0, slice(None), x, z, kind) if half == 0 else (0, x, slice(None), z, kind)


def read_head(ref, half, index, kind):
    return ref[head_rows(ref, half, index, kind)].reshape(HEAD_DIM, LEN)


def write_head(ref, half, index, kind, value):
    at = head_rows(ref, half, index, kind)
    if ref.shape[5] == HEAD_DIM:
        ref[at] = value
    else:
        ref[at] = value.reshape(-1, ref.shape[5], LEN)


def allowed_block(span_ref, base, columns, chunk):
    ahead = lax.broadcasted_iota(jnp.int32, (BLOCK, BLOCK), 0)
    if chunk < BLOCK:
        ahead = ahead + ahead // chunk * chunk
    away = ahead + (base - span_ref[0:1, columns])
    return (away >= 0) & (away <= span_ref[1:2, columns])


def span_of(index):
    return slice(index * BLOCK, (index + 1) * BLOCK)


def attend_kernel(heads, kinds, chunk, need_ref, base_ref, span_ref, *refs):
    sources = refs[: len(kinds)]
    mixed_ref, lse_ref, q_s, k_s, v_s, top_s, sum_s, acc_s = refs[len(kinds) :]
    where = [(source, kind) for source, count in zip(sources, kinds) for kind in range(count)]

    def load(half):
        for h, index in enumerate(heads):
            q, k, v = (read_head(source, half, index, kind) for source, kind in where)
            q_s[h] = (q.astype(F32) * SCALE).astype(BF)
            k_s[h] = k.T
            v_s[h] = v

    half_now = pl.program_id(0)
    for half in range(2):
        pl.when(half_now == half)(functools.partial(load, half))

    for i in range(BLOCKS):
        columns = span_of(i)
        top_s[...] = jnp.full(top_s.shape, -3e38, F32)
        sum_s[...] = jnp.zeros(sum_s.shape, F32)
        acc_s[...] = jnp.zeros(acc_s.shape, F32)
        for j in range(BLOCKS):

            @pl.when(need_ref[i * BLOCKS + j] > 0)
            def _(j=j):
                allowed = allowed_block(span_ref, base_ref[j], columns, chunk)
                for h in range(len(heads)):
                    scores = dot(k_s[h, span_of(j), :], q_s[h, :, columns], 1, 0)
                    scores = jnp.where(allowed, scores, MASKED)
                    top = jnp.maximum(top_s[h], jnp.max(scores, 0, keepdims=True))
                    fade = jnp.exp(top_s[h] - top)
                    weights = jnp.exp(scores - top)
                    top_s[h] = top
                    sum_s[h] = sum_s[h] * fade + jnp.sum(weights, 0, keepdims=True)
                    acc_s[h] = acc_s[h] * fade + dot(v_s[h, :, span_of(j)], weights.astype(BF), 1, 0)

        for h in range(len(heads)):
            lse_ref[0, h, :, columns] = top_s[h] + jnp.log(sum_s[h])
            q_s[h, :, columns] = (acc_s[h] / sum_s[h]).astype(BF)

    def store(half):
        for h, index in enumerate(heads):
            write_head(mixed_ref, half, index, 0, q_s[h])

    for half in range(2):
        pl.when(half_now == half)(functools.partial(store, half))


def attend_back_kernel(heads, kinds, chunk, need_ref, base_ref, span_ref, *refs):
    sources = refs[: len(kinds)]
    mixed_ref, grad_ref, lse_ref = refs[len(kinds) : len(kinds) + 3]
    outs = refs[len(kinds) + 3 : 2 * len(kinds) + 3]
    q_s, k_s, kt_s, v_s, g_s, inner_s, dq_s, dk_s, dv_s = refs[2 * len(kinds) + 3 :]
    where = [(source, kind) for source, count in zip(sources, kinds) for kind in range(count)]
    into = [(out, kind) for out, count in zip(outs, kinds) for kind in range(count)]

    def load(half):
        for h, index in enumerate(heads):
            q, k, v = (read_head(source, half, index, kind) for source, kind in where)
            q_s[h] = (q.astype(F32) * SCALE).astype(BF)
            kt_s[h] = k
            k_s[h] = k.T
            v_s[h] = v.T
            grad = read_head(grad_ref, half, index, 0)
            g_s[h] = grad
            mixed = read_head(mixed_ref, half, index, 0)
            inner_s[h] = jnp.sum(grad.astype(F32) * mixed.astype(F32), 0, keepdims=True)

    half_now = pl.program_id(0)
    for half in range(2):
        pl.when(half_now == half)(functools.partial(load, half))

    for acc in (dq_s, dk_s, dv_s):
        acc[...] = jnp.zeros(acc.shape, F32)

    for i in range(BLOCKS):
        columns = span_of(i)
        for j in range(BLOCKS):

            @pl.when(need_ref[i * BLOCKS + j] > 0)
            def _(j=j):
                allowed = allowed_block(span_ref, base_ref[j], columns, chunk)
                keys = span_of(j)
                for h in range(len(heads)):
                    query, grad = q_s[h, :, columns], g_s[h, :, columns]
                    scores = dot(k_s[h, keys, :], query, 1, 0)
                    scores = jnp.where(allowed, scores, MASKED)
                    chances = jnp.exp(scores - lse_ref[0, h, :, columns])
                    steep = dot(v_s[h, keys, :], grad, 1, 0)
                    back = (chances * (steep - inner_s[h, :, columns])).astype(BF)
                    dv_s[h, :, keys] += dot(grad, chances.astype(BF), 1, 1)
                    dk_s[h, :, keys] += dot(query, back, 1, 1)
                    dq_s[h, :, columns] += dot(kt_s[h, :, keys], back, 1, 0)

    def store(half):
        for h, index in enumerate(heads):
            made = (dq_s[h] * SCALE, dk_s[h], dv_s[h])
            for (out, kind), value in zip(into, made):
                write_head(out, half, index, kind, value.astype(BF))

    for half in range(2):
        pl.when(half_now == half)(functools.partial(store, half))


def by_half(shape):
    rest = (0,) * (len(shape) - 1)
    return pl.BlockSpec((1,) + tuple(shape[1:]), lambda i, *_: (i,) + rest)


class Heads:
    def __init__(self, nx, ny, nz, chunk):
        self.nx, self.ny, self.nz, self.chunk = nx, ny, nz, chunk
        self.index = [(x, z) for x in range(nx) for z in range(nz // 2)]

    def split(self, matrix, kinds):
        nx, ny, nz = self.nx, self.ny, self.nz
        rows = HEAD_DIM // ny
        if nx == ny and rows % 16 == 0:
            return matrix.reshape(2, ny, nx, nz // 2, kinds, rows, LEN)
        half = matrix.shape[0] // 2
        first = matrix[:half].reshape(ny, nx, nz // 2, kinds, rows, LEN).transpose(1, 2, 3, 0, 4, 5)
        second = matrix[half:].reshape(nx, ny, nz // 2, kinds, rows, LEN).transpose(0, 2, 3, 1, 4, 5)
        both_halves = jnp.stack([first, second], 0)
        return both_halves.reshape(2, 1, nx, nz // 2, kinds, HEAD_DIM, LEN)

    def join(self, split):
        nx, ny, nz = self.nx, self.ny, self.nz
        rows = HEAD_DIM // ny
        if split.shape[5] == rows:
            return split.reshape(-1, LEN)
        kinds = split.shape[4]
        cut = split.reshape(2, nx, nz // 2, kinds, ny, rows, LEN)
        first = cut[0].transpose(3, 0, 1, 2, 4, 5).reshape(-1, LEN)
        second = cut[1].transpose(0, 3, 1, 2, 4, 5).reshape(-1, LEN)
        return jnp.concatenate([first, second], 0)

    def call(self, kernel, kinds, tables, arrays, outs, scratch, flops):
        need, bases, spans = tables
        return pl.pallas_call(
            functools.partial(kernel, self.index, kinds, self.chunk),
            out_shape=outs,
            grid_spec=pltpu.PrefetchScalarGridSpec(
                num_scalar_prefetch=2,
                grid=(2,),
                in_specs=[pl.BlockSpec((2, LEN), lambda i, *_: (0, 0))] + [by_half(a.shape) for a in arrays],
                out_specs=[by_half(o.shape) for o in outs],
                scratch_shapes=scratch,
            ),
            compiler_params=pltpu.CompilerParams(vmem_limit_bytes=48 * 2**20),
            cost_estimate=pl.CostEstimate(flops=flops, bytes_accessed=8 * 2**20, transcendentals=4 * 2**20),
        )(need, bases, spans, *arrays)

    def attend(self, tables, sources, kinds):
        count = len(self.index)
        split = [self.split(s, k) for s, k in zip(sources, kinds)]
        like = split[0].shape
        wide = (count, HEAD_DIM, LEN)
        mixed, lse = self.call(
            attend_kernel,
            kinds,
            tables,
            split,
            [
                jax.ShapeDtypeStruct(like[:4] + (1,) + like[5:], BF),
                jax.ShapeDtypeStruct((2, count, 1, LEN), F32),
            ],
            [
                pltpu.VMEM(wide, BF),
                pltpu.VMEM((count, LEN, HEAD_DIM), BF),
                pltpu.VMEM(wide, BF),
                pltpu.VMEM((count, 1, BLOCK), F32),
                pltpu.VMEM((count, 1, BLOCK), F32),
                pltpu.VMEM((count, HEAD_DIM, BLOCK), F32),
            ],
            8 * 10**9,
        )
        return self.join(mixed), lse

    def attend_back(self, tables, sources, kinds, mixed, grad, lse):
        count = len(self.index)
        split = [self.split(s, k) for s, k in zip(sources, kinds)]
        wide, tall = (count, HEAD_DIM, LEN), (count, LEN, HEAD_DIM)
        grads = self.call(
            attend_back_kernel,
            kinds,
            tables,
            split + [self.split(mixed, 1), self.split(grad, 1), lse],
            [jax.ShapeDtypeStruct(s.shape, BF) for s in split],
            [
                pltpu.VMEM(wide, BF),
                pltpu.VMEM(tall, BF),
                pltpu.VMEM(wide, BF),
                pltpu.VMEM(tall, BF),
                pltpu.VMEM(wide, BF),
                pltpu.VMEM((count, 1, LEN), F32),
                pltpu.VMEM(wide, F32),
                pltpu.VMEM(wide, F32),
                pltpu.VMEM(wide, F32),
            ],
            20 * 10**9,
        )
        return [self.join(g) for g in grads]


def body(
    inputs,
    memory,
    cotangent,
    tgt_lengths,
    src_ids,
    gain_one,
    w_query,
    w_key,
    w_value,
    w_out,
    gain_two,
    w_cross_query,
    w_mem_key,
    w_mem_value,
    w_cross_out,
    gain_three,
    w_up,
    w_down,
):
    nx, ny, nz = (lax.axis_size(a) for a in ("batch", "yy", "head"))
    ix, iy, core, iz = (lax.axis_index(a) for a in ("batch", "yy", "core", "head"))
    rows = inputs.shape[0]
    nxy, place = nx * ny, ix * ny + iy
    chunk = LEN // (2 * ny)

    def part(matrix):
        deep = matrix.shape[0] // 2 // nxy
        return lax.dynamic_slice_in_dim(matrix, (core * nxy + place) * deep, deep, 0)

    def column_part(matrix):
        wide = matrix.shape[1] // 2
        return lax.dynamic_slice_in_dim(
            lax.dynamic_slice_in_dim(matrix, core * wide, wide, 1).T, place * (wide // nxy), wide // nxy, 0
        )

    def gathered(*parts):
        piece = jnp.concatenate(parts, 0) if len(parts) > 1 else parts[0]
        first, second = gather_weight(piece)
        width = piece.shape[1]
        return jnp.concatenate([first.reshape(-1, width), second.reshape(-1, width)], 0)

    row = iy * nz + iz
    lengths = lax.dynamic_index_in_dim(tgt_lengths, row, 0, keepdims=False)
    source_ids = lax.dynamic_index_in_dim(src_ids, row, 0, keepdims=False)
    index = jnp.arange(LEN, dtype=jnp.int32)
    within = index % (LEN // 2)
    turn = jnp.where(index < LEN // 2, core, 1 - core)
    positions = (2 * (within // chunk) + turn) * chunk + within % chunk
    ends = jnp.cumsum(lengths)
    starts = ends - lengths
    reached = positions[:, None] >= starts[None, :]
    target_ids = jnp.sum(reached.astype(jnp.int32), -1) - 1
    self_start = jnp.max(jnp.where(reached, starts[None, :], 0), -1)
    kinds = jnp.arange(lengths.shape[0], dtype=jnp.int32)
    source_start = jnp.sum((source_ids[None, :] < kinds[:, None]).astype(jnp.int32), -1)
    source_end = jnp.sum((source_ids[None, :] <= kinds[:, None]).astype(jnp.int32), -1) - 1
    mine = target_ids[:, None] == kinds[None, :]
    cross_start = jnp.sum(jnp.where(mine, source_start[None, :], 0), -1)
    cross_end = jnp.sum(jnp.where(mine, source_end[None, :], 0), -1)
    block_positions = positions.reshape(BLOCKS, BLOCK)
    lowest, highest = jnp.min(block_positions, 1), jnp.max(block_positions, 1)

    def tables_of(start, end):
        least = jnp.min(start.reshape(BLOCKS, BLOCK), 1)
        most = jnp.max(end.reshape(BLOCKS, BLOCK), 1)
        need = (least[:, None] <= highest[None, :]) & (most[:, None] >= lowest[None, :])
        return need.astype(jnp.int32).reshape(-1), lowest, jnp.stack([start, end - start], 0)

    self_tables = tables_of(self_start, positions)
    cross_tables = tables_of(cross_start, cross_end)
    heads = Heads(nx, ny, nz, chunk)

    w_self = gathered(column_part(w_query), column_part(w_key), column_part(w_value))
    residual = to_row(inputs).astype(F32)
    w_o = gathered(part(w_out))
    w_mem = gathered(column_part(w_mem_key), column_part(w_mem_value))
    w_cq = gathered(column_part(w_cross_query))
    w_co = gathered(part(w_cross_out))
    w_u = gathered(column_part(w_up))
    w_d = gathered(part(w_down))
    source = both(to_row(memory))
    cot_own = to_row(cotangent)
    cot = both(cot_own)

    normed_one = both(normalize(residual, gain_one))
    qkv = dot(w_self, normed_one, 1, 1).astype(BF)
    mkv = dot(w_mem, source, 1, 1).astype(BF)
    self_mixed, self_lse = heads.attend(self_tables, (qkv,), (3,))
    after_self = residual + own_sum(self_mixed, w_o)
    normed_two = both(normalize(after_self, gain_two))
    cq = dot(w_cq, normed_two, 1, 1).astype(BF)
    cross_mixed, cross_lse = heads.attend(cross_tables, (cq, mkv), (1, 2))
    after_cross = after_self + own_sum(cross_mixed, w_co)
    normed_three = both(normalize(after_cross, gain_three))
    hidden_pre = dot(w_u, normed_three, 1, 1)
    hidden_act, gate_pull = jax.vjp(lambda p: jax.nn.gelu(p, approximate=True), hidden_pre)
    hidden_act = hidden_act.astype(BF)
    output = (after_cross + own_sum(hidden_act, w_d)).astype(BF)
    output = from_row(output, rows)

    def weight_sum(transposed, tokens):
        grads = dot(transposed, tokens, 1, 0).astype(BF)
        return sum_weight(grads, grads.shape[0] // (nxy * nz))

    g_down = weight_sum(hidden_act, cot)
    grad_pre = gate_pull(dot(w_d, cot, 1, 1))[0].astype(BF)
    g_up = weight_sum(grad_pre, normed_three)
    step, grad_gain_three = normalize_back(after_cross, gain_three, own_sum(grad_pre, w_u))
    grad_after_cross = cot_own.astype(F32) + step

    cross_grad = both(grad_after_cross.astype(BF))
    g_co = weight_sum(cross_mixed, cross_grad)
    grad_cross_mixed = dot(w_co, cross_grad, 1, 1).astype(BF)
    gcq, gmkv = heads.attend_back(
        cross_tables, (cq, mkv), (1, 2), cross_mixed, grad_cross_mixed, cross_lse
    )
    g_cq = weight_sum(gcq, normed_two)
    g_mem = weight_sum(gmkv, source)
    grad_memory = from_row(own_sum(gmkv, w_mem).astype(BF), rows).astype(F32)
    step, grad_gain_two = normalize_back(after_self, gain_two, own_sum(gcq, w_cq))
    grad_after_self = grad_after_cross + step

    self_grad = both(grad_after_self.astype(BF))
    g_o = weight_sum(self_mixed, self_grad)
    grad_self_mixed = dot(w_o, self_grad, 1, 1).astype(BF)
    (gqkv,) = heads.attend_back(self_tables, (qkv,), (3,), self_mixed, grad_self_mixed, self_lse)
    g_self = weight_sum(gqkv, normed_one)
    step, grad_gain_one = normalize_back(residual, gain_one, own_sum(gqkv, w_self))
    grad_inputs = from_row((grad_after_self + step).astype(BF), rows).astype(F32)
    gains = total_of(jnp.stack([grad_gain_one, grad_gain_two, grad_gain_three]))

    def tall(grads):
        return replicate(grads).reshape(-1, grads.shape[1]).astype(F32)

    def columns(grads, count):
        whole = replicate(grads)
        whole = whole.reshape(whole.shape[:3] + (count, -1, grads.shape[1]))
        return [whole[:, :, :, i].reshape(-1, grads.shape[1]).T.astype(F32) for i in range(count)]

    grad_q, grad_k, grad_v = columns(g_self, 3)
    grad_mk, grad_mv = columns(g_mem, 2)
    return (
        output,
        grad_inputs,
        grad_memory,
        gains[0],
        grad_q,
        grad_k,
        grad_v,
        tall(g_o),
        gains[1],
        columns(g_cq, 1)[0],
        grad_mk,
        grad_mv,
        tall(g_co),
        gains[2],
        columns(g_up, 1)[0],
        tall(g_down),
    )


def solution(mesh):
    nb, ns, nh = (mesh.shape[a] for a in ("batch", "seq", "head"))
    fine = Mesh(mesh.devices.reshape(nb, ns // 2, 2, nh), ("batch", "yy", "core", "head"))
    tokens = P("batch", ("yy", "core", "head"), None)
    ids = P("batch", None)
    wide, tall = P(None, "head"), P("head", None)
    return jax.shard_map(
        body,
        mesh=fine,
        in_specs=(
            tokens, tokens, tokens, ids, ids,
            P(), wide, wide, wide, tall,
            P(), wide, wide, wide, tall,
            P(), wide, tall,
        ),
        out_specs=(
            tokens, tokens, tokens,
            P(), wide, wide, wide, tall,
            P(), wide, wide, wide, tall,
            P(), wide, tall,
        ),
        check_vma=False,
    )
```

```python
import functools

import jax
import jax.numpy as jnp
from jax import lax
from jax.experimental import pallas as pl
from jax.experimental.pallas import tpu as pltpu
from jax.sharding import Mesh
from jax.sharding import PartitionSpec as P

HEAD_DIM = 64
LEN = 1024
BLOCK = 256
BLOCKS = LEN // BLOCK
EPSILON = 1e-05
MASKED = -1000000000.0
SCALE = HEAD_DIM**-0.5
GELU_A = 0.7978845608028654
GELU_B = 0.044715
BF = jnp.bfloat16
F32 = jnp.float32


def dot(left, right, left_dim, right_dim):
    return lax.dot_general(
        left, right, (((left_dim,), (right_dim,)), ((), ())), preferred_element_type=F32
    )


def normalize(activity, gain):
    centre = jnp.mean(activity, -1, keepdims=True)
    shifted = activity - centre
    variance = jnp.mean(shifted * shifted, -1, keepdims=True)
    return (shifted * lax.rsqrt(variance + EPSILON) * gain).astype(BF)


def normalize_back(activity, gain, grad):
    centre = jnp.mean(activity, -1, keepdims=True)
    shifted = activity - centre
    variance = jnp.mean(shifted * shifted, -1, keepdims=True)
    rate = lax.rsqrt(variance + EPSILON)
    unit = shifted * rate
    scaled = grad * gain
    inner = scaled - jnp.mean(scaled, -1, keepdims=True)
    grad_activity = rate * (inner - unit * jnp.mean(scaled * unit, -1, keepdims=True))
    return grad_activity, jnp.sum(grad * unit, 0)


def shift(piece, axis, step):
    count = lax.axis_size(axis)
    return lax.ppermute(piece, axis, [(i, (i + step) % count) for i in range(count)])


def core_swap(piece):
    return shift(piece, "core", 1)


def both(own):
    return jnp.concatenate([own, core_swap(own)], 0)


def own_sum(transposed, matrix):
    half = transposed.shape[1] // 2
    other = core_swap(dot(transposed[:, half:], matrix, 0, 0).astype(BF))
    return dot(transposed[:, :half], matrix, 0, 0) + other.astype(F32)


def to_row(tokens):
    rows, span, width = tokens.shape
    moved = lax.all_to_all(tokens, ("yy", "head"), 0, 0, tiled=True)
    return moved.reshape(rows * span, width)


def from_row(own, rows):
    parts = own.reshape(rows, own.shape[0] // rows, own.shape[1])
    return lax.all_to_all(parts, ("yy", "head"), 0, 0, tiled=True)


def tied(values, *others):
    return lax.optimization_barrier((values, others))[0]


def meet(values, *moves):
    values, got = lax.optimization_barrier((values, [m.got for m in moves]))
    for move, pieces in zip(moves, got):
        move.got = pieces
    return values


def others_of(axis):
    return range(1, lax.axis_size(axis))


class Gather:
    def __init__(self, parts, *others):
        self.deep = [p.shape[0] for p in parts]
        self.mine = tied(jnp.concatenate(parts, 0), *others)
        self.got = [shift(self.mine, "head", k) for k in others_of("head")]

    def send(self, first, second, one, two):
        self.mine = first, second
        self.got = [shift(first, one, k) for k in others_of(one)] + [shift(second, two, k) for k in others_of(two)]
        self.cut = len(others_of(one))

    def two(self):
        along = jnp.stack([self.mine] + self.got, 0)
        half = along.shape[0] // 2
        self.send(along[:half], along[half:], "batch", "yy")

    def slots(self):
        first, second = self.mine
        return [first] + self.got[: self.cut], [second] + self.got[self.cut :]

    def three(self):
        first, second = self.slots()
        self.send(jnp.stack(first, 0), jnp.stack(second, 0), "yy", "batch")

    def result(self):
        first, second = self.slots()
        made, at = [], 0
        for deep in self.deep:
            cut = [slot[..., at : at + deep, :].reshape(-1, slot.shape[-1]) for slot in first + second]
            made.append(jnp.concatenate(cut, 0))
            at += deep
        return made


class Sum:
    def __init__(self, grads):
        nx, ny, self.nz = (lax.axis_size(a) for a in ("batch", "yy", "head"))
        width = grads[0].shape[1]
        half = [g.shape[0] // 2 for g in grads]
        first = [g[:n].reshape(ny, nx, self.nz // 2, -1, width) for g, n in zip(grads, half)]
        second = [g[n:].reshape(nx, ny, self.nz // 2, -1, width) for g, n in zip(grads, half)]
        self.send(first, second, "yy", "batch")

    def send(self, first, second, one, two):
        def slot(grads, k):
            return jnp.concatenate([g[k] for g in grads], -2)

        self.mine = slot(first, 0), slot(second, 0)
        self.got = [shift(slot(first, k), one, -k) for k in others_of(one)]
        self.cut = len(self.got)
        self.got = self.got + [shift(slot(second, k), two, -k) for k in others_of(two)]

    def add(self, mine, got):
        total = mine.astype(F32)
        for piece in got:
            total = total + piece.astype(F32)
        return total.astype(BF)

    def sums(self):
        first, second = self.mine
        return self.add(first, self.got[: self.cut]), self.add(second, self.got[self.cut :])

    def two(self):
        first, second = self.sums()
        self.send([first], [second], "batch", "yy")

    def three(self):
        first, second = self.sums()
        slots = [first[k] if k < self.nz // 2 else second[k - self.nz // 2] for k in range(self.nz)]
        self.mine, self.got = slots[0], [shift(slots[k], "head", -k) for k in range(1, self.nz)]

    def result(self):
        return self.add(self.mine, self.got)


def in_place(piece, axis):
    if lax.axis_size(axis) != 2:
        return lax.all_gather(piece, axis, axis=0, tiled=False)
    other = shift(piece, axis, 1)
    low = lax.axis_index(axis) == 0
    return jnp.stack([jnp.where(low, piece, other), jnp.where(low, other, piece)], 0)


def gathered(piece):
    sizes = tuple(lax.axis_size(a) for a in ("core", "batch", "yy"))
    return lax.all_gather(piece, ("core", "batch", "yy"), axis=0, tiled=True).reshape(sizes + piece.shape)


def replicate(piece):
    return in_place(in_place(in_place(piece, "yy"), "batch"), "core")


def unfold_kernel(kinds, source_ref, *outs):
    at = 0
    for (size, turned), out in zip(kinds, outs):
        piece = source_ref[..., at : at + size, :].reshape(-1, source_ref.shape[-1]).astype(F32)
        out[...] = piece.T if turned else piece
        at += size


def unfold(whole, kinds):
    width = whole.shape[-1]
    count = whole.shape[0] * whole.shape[1] * whole.shape[2]
    if any(size % 16 for size, _ in kinds):
        made, at = [], 0
        for size, turned in kinds:
            piece = whole[..., at : at + size, :].reshape(-1, width)
            made.append((piece.T if turned else piece).astype(F32))
            at += size
        return made
    step = 256
    return pl.pallas_call(
        functools.partial(unfold_kernel, kinds),
        out_shape=[
            jax.ShapeDtypeStruct((width, count * size) if turned else (count * size, width), F32) for size, turned in kinds
        ],
        grid=(width // step,),
        in_specs=[pl.BlockSpec(whole.shape[:4] + (step,), lambda i: (0, 0, 0, 0, i))],
        out_specs=[
            pl.BlockSpec((step, count * size), lambda i: (i, 0))
            if turned
            else pl.BlockSpec((count * size, step), lambda i: (0, i))
            for size, turned in kinds
        ],
        compiler_params=pltpu.CompilerParams(vmem_limit_bytes=32 * 2**20),
    )(whole)


def total_of(value):
    for axis in ("core", "yy", "batch", "head"):
        count = lax.axis_size(axis)
        step = 1
        while step < count:
            value = value + lax.ppermute(value, axis, [(i, i ^ step) for i in range(count)])
            step *= 2
    return value


def head_rows(ref, half, index, kind):
    x, z = index
    if ref.shape[5] == HEAD_DIM:
        return (0, 0, x, z, kind)
    return (0, slice(None), x, z, kind) if half == 0 else (0, x, slice(None), z, kind)


def read_head(ref, half, index, kind):
    return ref[head_rows(ref, half, index, kind)].reshape(HEAD_DIM, LEN)


def write_head(ref, half, index, kind, value):
    at = head_rows(ref, half, index, kind)
    if ref.shape[5] == HEAD_DIM:
        ref[at] = value
    else:
        ref[at] = value.reshape(-1, ref.shape[5], LEN)


def allowed_block(span_ref, base, columns, chunk):
    ahead = lax.broadcasted_iota(jnp.int32, (BLOCK, BLOCK), 0)
    if chunk < BLOCK:
        ahead = ahead + ahead // chunk * chunk
    away = ahead + (base - span_ref[0:1, columns])
    return (away >= 0) & (away <= span_ref[1:2, columns])


def span_of(index):
    return slice(index * BLOCK, (index + 1) * BLOCK)


def per_block(need_ref, base_ref, span_ref, columns, chunk, i, j, work):
    need = need_ref[i * BLOCKS + j]

    @pl.when(need == 1)
    def _():
        allowed = allowed_block(span_ref, base_ref[j], columns, chunk)
        work(lambda scores: jnp.where(allowed, scores, MASKED))

    @pl.when(need == 2)
    def _():
        work(lambda scores: scores)


def attend_kernel(heads, kinds, chunk, need_ref, base_ref, span_ref, *refs):
    sources = refs[: len(kinds)]
    mixed_ref, lse_ref, q_s, k_s, v_s, top_s, sum_s, acc_s = refs[len(kinds) :]
    where = [(source, kind) for source, count in zip(sources, kinds) for kind in range(count)]
    every = range(len(heads))

    def load(half):
        for h, index in enumerate(heads):
            q, k, v = (read_head(source, half, index, kind) for source, kind in where)
            q_s[h] = (q.astype(F32) * SCALE).astype(BF)
            k_s[h] = k.T
            v_s[h] = v

    half_now = pl.program_id(0)
    for half in range(2):
        pl.when(half_now == half)(functools.partial(load, half))

    for i in range(BLOCKS):
        columns = span_of(i)
        top_s[...] = jnp.full(top_s.shape, -3e38, F32)
        sum_s[...] = jnp.zeros(sum_s.shape, F32)
        acc_s[...] = jnp.zeros(acc_s.shape, F32)
        for j in range(BLOCKS):
            keys = span_of(j)

            def work(mask, keys=keys, columns=columns):
                scores = [mask(dot(k_s[h, keys, :], q_s[h, :, columns], 1, 0)) for h in every]
                tops = [jnp.maximum(top_s[h], jnp.max(scores[h], 0, keepdims=True)) for h in every]
                weights = [jnp.exp(scores[h] - tops[h]) for h in every]
                fades = [jnp.exp(top_s[h] - tops[h]) for h in every]
                mixed = [dot(v_s[h, :, keys], weights[h].astype(BF), 1, 0) for h in every]
                for h in every:
                    top_s[h] = tops[h]
                    sum_s[h] = sum_s[h] * fades[h] + jnp.sum(weights[h], 0, keepdims=True)
                    acc_s[h] = acc_s[h] * fades[h] + mixed[h]

            per_block(need_ref, base_ref, span_ref, columns, chunk, i, j, work)

        for h in every:
            lse_ref[0, h, :, columns] = top_s[h] + jnp.log(sum_s[h])
            q_s[h, :, columns] = (acc_s[h] / sum_s[h]).astype(BF)

    def store(half):
        for h, index in enumerate(heads):
            write_head(mixed_ref, half, index, 0, q_s[h])

    for half in range(2):
        pl.when(half_now == half)(functools.partial(store, half))


def attend_back_kernel(heads, kinds, chunk, need_ref, base_ref, span_ref, *refs):
    sources = refs[: len(kinds)]
    mixed_ref, grad_ref, lse_ref = refs[len(kinds) : len(kinds) + 3]
    outs = refs[len(kinds) + 3 : 2 * len(kinds) + 3]
    q_s, k_s, kt_s, v_s, g_s, inner_s, dq_s, dk_s, dv_s = refs[2 * len(kinds) + 3 :]
    where = [(source, kind) for source, count in zip(sources, kinds) for kind in range(count)]
    into = [(out, kind) for out, count in zip(outs, kinds) for kind in range(count)]
    every = range(len(heads))

    def load(half):
        for h, index in enumerate(heads):
            q, k, v = (read_head(source, half, index, kind) for source, kind in where)
            q_s[h] = (q.astype(F32) * SCALE).astype(BF)
            kt_s[h] = k
            k_s[h] = k.T
            v_s[h] = v.T
            grad = read_head(grad_ref, half, index, 0)
            g_s[h] = grad
            mixed = read_head(mixed_ref, half, index, 0)
            inner_s[h] = jnp.sum(grad.astype(F32) * mixed.astype(F32), 0, keepdims=True)

    half_now = pl.program_id(0)
    for half in range(2):
        pl.when(half_now == half)(functools.partial(load, half))

    for acc in (dq_s, dk_s, dv_s):
        acc[...] = jnp.zeros(acc.shape, F32)

    for i in range(BLOCKS):
        columns = span_of(i)
        for j in range(BLOCKS):
            keys = span_of(j)

            def work(mask, keys=keys, columns=columns):
                scores = [mask(dot(k_s[h, keys, :], q_s[h, :, columns], 1, 0)) for h in every]
                steep = [dot(v_s[h, keys, :], g_s[h, :, columns], 1, 0) for h in every]
                chances = [jnp.exp(scores[h] - lse_ref[0, h, :, columns]) for h in every]
                back = [(chances[h] * (steep[h] - inner_s[h, :, columns])).astype(BF) for h in every]
                for h in every:
                    dv_s[h, :, keys] += dot(g_s[h, :, columns], chances[h].astype(BF), 1, 1)
                for h in every:
                    dk_s[h, :, keys] += dot(q_s[h, :, columns], back[h], 1, 1)
                for h in every:
                    dq_s[h, :, columns] += dot(kt_s[h, :, keys], back[h], 1, 0)

            per_block(need_ref, base_ref, span_ref, columns, chunk, i, j, work)

    def store(half):
        for h, index in enumerate(heads):
            made = (dq_s[h] * SCALE, dk_s[h], dv_s[h])
            for (out, kind), value in zip(into, made):
                write_head(out, half, index, kind, value.astype(BF))

    for half in range(2):
        pl.when(half_now == half)(functools.partial(store, half))


def by_half(shape):
    rest = (0,) * (len(shape) - 1)
    return pl.BlockSpec((1,) + tuple(shape[1:]), lambda i, *_: (i,) + rest)


class Heads:
    def __init__(self, nx, ny, nz, chunk):
        self.nx, self.ny, self.nz, self.chunk = nx, ny, nz, chunk
        self.index = [(x, z) for x in range(nx) for z in range(nz // 2)]

    def split(self, matrix, kinds):
        nx, ny, nz = self.nx, self.ny, self.nz
        rows = HEAD_DIM // ny
        if nx == ny and rows % 16 == 0:
            return matrix.reshape(2, ny, nx, nz // 2, kinds, rows, LEN)
        half = matrix.shape[0] // 2
        first = matrix[:half].reshape(ny, nx, nz // 2, kinds, rows, LEN).transpose(1, 2, 3, 0, 4, 5)
        second = matrix[half:].reshape(nx, ny, nz // 2, kinds, rows, LEN).transpose(0, 2, 3, 1, 4, 5)
        both_halves = jnp.stack([first, second], 0)
        return both_halves.reshape(2, 1, nx, nz // 2, kinds, HEAD_DIM, LEN)

    def join(self, split):
        nx, ny, nz = self.nx, self.ny, self.nz
        rows = HEAD_DIM // ny
        if split.shape[5] == rows:
            return split.reshape(-1, LEN)
        kinds = split.shape[4]
        cut = split.reshape(2, nx, nz // 2, kinds, ny, rows, LEN)
        first = cut[0].transpose(3, 0, 1, 2, 4, 5).reshape(-1, LEN)
        second = cut[1].transpose(0, 3, 1, 2, 4, 5).reshape(-1, LEN)
        return jnp.concatenate([first, second], 0)

    def call(self, kernel, kinds, tables, arrays, outs, scratch, flops):
        need, bases, spans = tables
        return pl.pallas_call(
            functools.partial(kernel, self.index, kinds, self.chunk),
            out_shape=outs,
            grid_spec=pltpu.PrefetchScalarGridSpec(
                num_scalar_prefetch=2,
                grid=(2,),
                in_specs=[pl.BlockSpec((2, LEN), lambda i, *_: (0, 0))] + [by_half(a.shape) for a in arrays],
                out_specs=[by_half(o.shape) for o in outs],
                scratch_shapes=scratch,
            ),
            compiler_params=pltpu.CompilerParams(vmem_limit_bytes=48 * 2**20),
            cost_estimate=pl.CostEstimate(flops=flops, bytes_accessed=8 * 2**20, transcendentals=4 * 2**20),
        )(need, bases, spans, *arrays)

    def attend(self, tables, sources, kinds):
        count = len(self.index)
        split = [self.split(s, k) for s, k in zip(sources, kinds)]
        like = split[0].shape
        wide = (count, HEAD_DIM, LEN)
        mixed, lse = self.call(
            attend_kernel,
            kinds,
            tables,
            split,
            [
                jax.ShapeDtypeStruct(like[:4] + (1,) + like[5:], BF),
                jax.ShapeDtypeStruct((2, count, 1, LEN), F32),
            ],
            [
                pltpu.VMEM(wide, BF),
                pltpu.VMEM((count, LEN, HEAD_DIM), BF),
                pltpu.VMEM(wide, BF),
                pltpu.VMEM((count, 1, BLOCK), F32),
                pltpu.VMEM((count, 1, BLOCK), F32),
                pltpu.VMEM((count, HEAD_DIM, BLOCK), F32),
            ],
            40 * 10**9,
        )
        return self.join(mixed), lse

    def attend_back(self, tables, sources, kinds, mixed, grad, lse):
        count = len(self.index)
        split = [self.split(s, k) for s, k in zip(sources, kinds)]
        wide, tall = (count, HEAD_DIM, LEN), (count, LEN, HEAD_DIM)
        grads = self.call(
            attend_back_kernel,
            kinds,
            tables,
            split + [self.split(mixed, 1), self.split(grad, 1), lse],
            [jax.ShapeDtypeStruct(s.shape, BF) for s in split],
            [
                pltpu.VMEM(wide, BF),
                pltpu.VMEM(tall, BF),
                pltpu.VMEM(wide, BF),
                pltpu.VMEM(tall, BF),
                pltpu.VMEM(wide, BF),
                pltpu.VMEM((count, 1, LEN), F32),
                pltpu.VMEM(wide, F32),
                pltpu.VMEM(wide, F32),
                pltpu.VMEM(wide, F32),
            ],
            46 * 10**9,
        )
        return [self.join(g) for g in grads]


def body(
    inputs,
    memory,
    cotangent,
    tgt_lengths,
    src_ids,
    gain_one,
    w_query,
    w_key,
    w_value,
    w_out,
    gain_two,
    w_cross_query,
    w_mem_key,
    w_mem_value,
    w_cross_out,
    gain_three,
    w_up,
    w_down,
):
    nx, ny, nz = (lax.axis_size(a) for a in ("batch", "yy", "head"))
    ix, iy, core, iz = (lax.axis_index(a) for a in ("batch", "yy", "core", "head"))
    rows = inputs.shape[0]
    nxy, place = nx * ny, ix * ny + iy
    chunk = LEN // (2 * ny)

    def part(matrix):
        deep = matrix.shape[0] // 2 // nxy
        return lax.dynamic_slice_in_dim(matrix, (core * nxy + place) * deep, deep, 0)

    def column_parts(*matrices):
        parts = []
        for matrix in matrices:
            wide = matrix.shape[1] // 2
            turned = lax.dynamic_slice_in_dim(matrix, core * wide, wide, 1).T
            parts.append(lax.dynamic_slice_in_dim(turned, place * (wide // nxy), wide // nxy, 0))
        return jnp.concatenate(parts, 0)

    row = iy * nz + iz
    lengths = lax.dynamic_index_in_dim(tgt_lengths, row, 0, keepdims=False)
    source_ids = lax.dynamic_index_in_dim(src_ids, row, 0, keepdims=False)
    index = jnp.arange(LEN, dtype=jnp.int32)
    within = index % (LEN // 2)
    turn = jnp.where(index < LEN // 2, core, 1 - core)
    positions = (2 * (within // chunk) + turn) * chunk + within % chunk
    ends = jnp.cumsum(lengths)
    starts = ends - lengths
    reached = positions[:, None] >= starts[None, :]
    target_ids = jnp.sum(reached.astype(jnp.int32), -1) - 1
    self_start = jnp.max(jnp.where(reached, starts[None, :], 0), -1)
    kinds = jnp.arange(lengths.shape[0], dtype=jnp.int32)
    source_start = jnp.sum((source_ids[None, :] < kinds[:, None]).astype(jnp.int32), -1)
    source_end = jnp.sum((source_ids[None, :] <= kinds[:, None]).astype(jnp.int32), -1) - 1
    mine = target_ids[:, None] == kinds[None, :]
    cross_start = jnp.sum(jnp.where(mine, source_start[None, :], 0), -1)
    cross_end = jnp.sum(jnp.where(mine, source_end[None, :], 0), -1)
    block_positions = positions.reshape(BLOCKS, BLOCK)
    lowest, highest = jnp.min(block_positions, 1), jnp.max(block_positions, 1)

    def tables_of(start, end):
        least = jnp.min(start.reshape(BLOCKS, BLOCK), 1)
        most = jnp.max(end.reshape(BLOCKS, BLOCK), 1)
        some = (least[:, None] <= highest[None, :]) & (most[:, None] >= lowest[None, :])
        last, first = jnp.max(start.reshape(BLOCKS, BLOCK), 1), jnp.min(end.reshape(BLOCKS, BLOCK), 1)
        whole = (last[:, None] <= lowest[None, :]) & (first[:, None] >= highest[None, :])
        need = jnp.where(whole, 2, some.astype(jnp.int32))
        return need.reshape(-1), lowest, jnp.stack([start, end - start], 0)

    self_tables = tables_of(self_start, positions)
    cross_tables = tables_of(cross_start, cross_end)
    heads = Heads(nx, ny, nz, chunk)

    residual = to_row(inputs).astype(F32)
    self_weights = Gather([column_parts(w_query, w_key, w_value)])
    residual = to_row(tied(inputs, self_weights.mine)).astype(F32)
    self_weights.two()
    residual = meet(residual, self_weights)
    self_weights.three()
    cross_weights = Gather(
        [part(w_out), column_parts(w_mem_key, w_mem_value), column_parts(w_cross_query), part(w_cross_out)],
        residual,
    )
    normed_one = both(normalize(tied(residual, self_weights.mine, cross_weights.mine), gain_one))
    normed_one = meet(normed_one, self_weights)
    (w_self,) = self_weights.result()
    qkv = dot(w_self, normed_one, 1, 1).astype(BF)
    qkv = meet(qkv, cross_weights)
    cross_weights.two()
    up_weights = Gather([column_parts(w_up)], cross_weights.mine)
    qkv = tied(qkv, cross_weights.mine, up_weights.mine)
    self_mixed, self_lse = heads.attend(self_tables, (qkv,), (3,))
    self_mixed = meet(self_mixed, cross_weights, up_weights)
    cross_weights.three()
    down_weights = Gather([part(w_down)], up_weights.got, cross_weights.mine)
    self_mixed = meet(self_mixed, cross_weights)
    up_weights.two()
    source_own = to_row(tied(memory, self_mixed))
    self_mixed = tied(self_mixed, up_weights.mine)
    w_o, w_mem, w_cq, w_co = cross_weights.result()
    after_self = residual + own_sum(self_mixed, w_o)
    normed_two = meet(normalize(after_self, gain_two), up_weights, down_weights)
    up_weights.three()
    down_weights.two()
    normed_two, source_own = tied((normed_two, source_own), up_weights.mine, down_weights.mine)
    source = both(source_own)
    mkv = dot(w_mem, source, 1, 1).astype(BF)
    normed_two = both(normed_two)
    cq = dot(w_cq, normed_two, 1, 1).astype(BF)
    cross_mixed, cross_lse = heads.attend(cross_tables, (cq, mkv), (1, 2))
    cross_mixed = meet(cross_mixed, up_weights, down_weights)
    down_weights.three()
    cross_mixed = tied(cross_mixed, down_weights.mine)
    cot_own = to_row(tied(cotangent, down_weights.mine))
    after_cross = after_self + own_sum(cross_mixed, w_co)
    normed_three = both(normalize(after_cross, gain_three))
    (w_u,) = up_weights.result()

    hidden_pre = dot(w_u, normed_three, 1, 1)
    squared = hidden_pre * hidden_pre
    bent = jnp.tanh(GELU_A * hidden_pre * (1.0 + GELU_B * squared))
    gate = 0.5 + 0.5 * bent
    slope = gate + (0.5 * GELU_A) * hidden_pre * (1.0 - bent * bent) * (1.0 + 3.0 * GELU_B * squared)
    hidden_act, slope = lax.optimization_barrier(((hidden_pre * gate).astype(BF), slope.astype(BF)))
    hidden_act = meet(hidden_act, down_weights)
    (w_d,) = down_weights.result()
    cot = both(tied(cot_own, hidden_act))
    output = (after_cross + own_sum(hidden_act, w_d)).astype(BF)
    output = from_row(output, rows)

    def weight_grad(transposed, tokens):
        return dot(transposed, tokens, 1, 0).astype(BF)

    g_down = weight_grad(hidden_act, cot)
    grad_pre = (slope.astype(F32) * dot(w_d, cot, 1, 1)).astype(BF)
    g_up = weight_grad(grad_pre, normed_three)
    ffn_sum = Sum([g_down, g_up])
    step, grad_gain_three = normalize_back(after_cross, gain_three, own_sum(grad_pre, w_u))
    grad_after_cross = cot_own.astype(F32) + step

    cross_grad = both(grad_after_cross.astype(BF))
    grad_cross_mixed = dot(w_co, cross_grad, 1, 1).astype(BF)
    gcq, gmkv = heads.attend_back(
        cross_tables, (cq, mkv), (1, 2), cross_mixed, grad_cross_mixed, cross_lse
    )
    gcq, gmkv, output = meet((gcq, gmkv, output), ffn_sum)
    ffn_sum.two()
    gcq, gmkv = tied((gcq, gmkv), ffn_sum.mine)
    step, grad_gain_two = normalize_back(after_self, gain_two, own_sum(gcq, w_cq))
    grad_after_self = grad_after_cross + step
    grad_after_self = meet(grad_after_self, ffn_sum)
    ffn_sum.three()
    self_grad = both(grad_after_self.astype(BF))
    g_co = weight_grad(cross_mixed, cross_grad)
    g_cq = weight_grad(gcq, normed_two)
    g_mem = weight_grad(gmkv, source)
    cross_sum = Sum([g_co, g_cq, g_mem])
    memory_back = own_sum(gmkv, w_mem).astype(BF)
    grad_self_mixed = dot(w_o, self_grad, 1, 1).astype(BF)
    grad_self_mixed, memory_back = tied((grad_self_mixed, memory_back), ffn_sum.mine, cross_sum.mine)
    grad_memory = from_row(memory_back, rows).astype(F32)
    (gqkv,) = heads.attend_back(self_tables, (qkv,), (3,), self_mixed, grad_self_mixed, self_lse)
    gqkv = meet(gqkv, cross_sum)
    cross_sum.two()
    g_self = weight_grad(gqkv, normed_one)
    g_o = weight_grad(self_mixed, self_grad)
    self_sum = Sum([g_o, g_self])
    first_back = own_sum(gqkv, w_self)
    first_back = meet(tied(first_back, self_sum.mine), cross_sum, ffn_sum)
    cross_sum.three()
    step, grad_gain_one = normalize_back(residual, gain_one, first_back)
    grad_inputs = from_row((grad_after_self + step).astype(BF), rows).astype(F32)
    gains = total_of(jnp.stack([grad_gain_one, grad_gain_two, grad_gain_three]))
    self_sum.two()
    self_sum.three()

    deep = w_query.shape[1] // 2 // nxy
    far = w_up.shape[1] // 2 // nxy
    grad_down, grad_up = unfold(gathered(ffn_sum.result()), [(far, False), (far, True)])
    grad_co, grad_cq, grad_mk, grad_mv = unfold(
        gathered(cross_sum.result()), [(deep, False), (deep, True), (deep, True), (deep, True)]
    )
    self_sum.got = tied(self_sum.got, grad_down, grad_up, grad_inputs, gains, grad_memory)
    grad_o, grad_q, grad_k, grad_v = unfold(
        replicate(self_sum.result()), [(deep, False), (deep, True), (deep, True), (deep, True)]
    )
    return (
        output,
        grad_inputs,
        grad_memory,
        gains[0],
        grad_q,
        grad_k,
        grad_v,
        grad_o,
        gains[1],
        grad_cq,
        grad_mk,
        grad_mv,
        grad_co,
        gains[2],
        grad_up,
        grad_down,
    )


def solution(mesh):
    nb, ns, nh = (mesh.shape[a] for a in ("batch", "seq", "head"))
    fine = Mesh(mesh.devices.reshape(nb, ns // 2, 2, nh), ("batch", "yy", "core", "head"))
    tokens = P("batch", ("yy", "core", "head"), None)
    ids = P("batch", None)
    wide, tall = P(None, "head"), P("head", None)
    return jax.shard_map(
        body,
        mesh=fine,
        in_specs=(
            tokens, tokens, tokens, ids, ids,
            P(), wide, wide, wide, tall,
            P(), wide, wide, wide, tall,
            P(), wide, tall,
        ),
        out_specs=(
            tokens, tokens, tokens,
            P(), wide, wide, wide, tall,
            P(), wide, wide, wide, tall,
            P(), wide, tall,
        ),
        check_vma=False,
    )
```

```python
import functools

import jax
import jax.numpy as jnp
from jax import lax
from jax.experimental import pallas as pl
from jax.experimental.pallas import tpu as pltpu
from jax.sharding import Mesh
from jax.sharding import PartitionSpec as P

HEAD_DIM = 64
LEN = 1024
BLOCK = 256
BLOCKS = LEN // BLOCK
EPSILON = 1e-05
MASKED = -1000000000.0
SCALE = HEAD_DIM**-0.5
GELU_A = 0.7978845608028654
GELU_B = 0.044715
BF = jnp.bfloat16
F32 = jnp.float32


def dot(left, right, left_dim, right_dim):
    return lax.dot_general(
        left, right, (((left_dim,), (right_dim,)), ((), ())), preferred_element_type=F32
    )


STEP = 128


def centred(activity):
    shifted = activity - jnp.mean(activity, -1, keepdims=True)
    return shifted, lax.rsqrt(jnp.mean(shifted * shifted, -1, keepdims=True) + EPSILON)


def norm_kernel(terms, gain_ref, *refs):
    activity = refs[0][...].astype(F32)
    for ref in refs[1:terms]:
        activity = activity + ref[...].astype(F32)
    shifted, rate = centred(activity)
    refs[terms][...] = (shifted * rate * gain_ref[...]).astype(BF)
    if terms > 1:
        refs[terms + 1][...] = activity


def norm_back_kernel(gain_ref, activity_ref, own_ref, other_ref, onward_ref, grad_ref, rounded_ref, gain_grad_ref):
    shifted, rate = centred(activity_ref[...].astype(F32))
    unit = shifted * rate
    arrived = own_ref[...] + other_ref[...].astype(F32)
    scaled = arrived * gain_ref[...]
    inner = scaled - jnp.mean(scaled, -1, keepdims=True)
    step = rate * (inner - unit * jnp.mean(scaled * unit, -1, keepdims=True))
    total = onward_ref[...].astype(F32) + step
    grad_ref[...] = total
    rounded_ref[...] = total.astype(BF)

    @pl.when(pl.program_id(0) == 0)
    def _():
        gain_grad_ref[...] = jnp.zeros(gain_grad_ref.shape, F32)

    gain_grad_ref[...] += jnp.sum(arrived * unit, 0, keepdims=True)


def by_rows(kernel, gain, arrays, outs, sums=0):
    tokens, width = arrays[0].shape
    tile, line = pl.BlockSpec((STEP, width), lambda i: (i, 0)), pl.BlockSpec((1, width), lambda i: (0, 0))
    return pl.pallas_call(
        kernel,
        out_shape=[jax.ShapeDtypeStruct((tokens, width), t) for t in outs]
        + [jax.ShapeDtypeStruct((1, width), F32)] * sums,
        grid=(tokens // STEP,),
        in_specs=[line] + [tile] * len(arrays),
        out_specs=[tile] * len(outs) + [line] * sums,
        compiler_params=pltpu.CompilerParams(vmem_limit_bytes=32 * 2**20),
        cost_estimate=pl.CostEstimate(flops=20 * tokens * width, bytes_accessed=8 * tokens * width, transcendentals=tokens),
    )(gain.reshape(1, width), *arrays)


def normalize(terms, gain):
    return by_rows(functools.partial(norm_kernel, len(terms)), gain, terms, [BF] + [F32] * (len(terms) > 1))


def normalize_back(activity, gain, arrived, onward):
    grad, rounded, gain_grad = by_rows(norm_back_kernel, gain, [activity, *arrived, onward], [F32, BF], 1)
    return grad, rounded, gain_grad[0]


def shift(piece, axis, step):
    count = lax.axis_size(axis)
    return lax.ppermute(piece, axis, [(i, (i + step) % count) for i in range(count)])


def core_swap(piece):
    return shift(piece, "core", 1)


def both(own):
    return jnp.concatenate([own, core_swap(own)], 0)


def own_parts(transposed, matrix):
    half = transposed.shape[1] // 2
    other = core_swap(dot(transposed[:, half:], matrix, 0, 0).astype(BF))
    return [dot(transposed[:, :half], matrix, 0, 0), other]


def own_sum(transposed, matrix):
    own, other = own_parts(transposed, matrix)
    return own + other.astype(F32)


def to_row(tokens):
    rows, span, width = tokens.shape
    moved = lax.all_to_all(tokens, ("yy", "head"), 0, 0, tiled=True)
    return moved.reshape(rows * span, width)


def from_row(own, rows):
    parts = own.reshape(rows, own.shape[0] // rows, own.shape[1])
    return lax.all_to_all(parts, ("yy", "head"), 0, 0, tiled=True)


def tied(values, *others):
    return lax.optimization_barrier((values, others))[0]


def meet(values, *moves):
    values, got = lax.optimization_barrier((values, [m.got for m in moves]))
    for move, pieces in zip(moves, got):
        move.got = pieces
    return values


def others_of(axis):
    return range(1, lax.axis_size(axis))


class Gather:
    def __init__(self, parts, *others):
        self.deep = [p.shape[0] for p in parts]
        self.mine = tied(jnp.concatenate(parts, 0), *others)
        self.got = [shift(self.mine, "head", k) for k in others_of("head")]

    def send(self, first, second, one, two):
        self.mine = first, second
        self.got = [shift(first, one, k) for k in others_of(one)] + [shift(second, two, k) for k in others_of(two)]
        self.cut = len(others_of(one))

    def two(self):
        along = jnp.stack([self.mine] + self.got, 0)
        half = along.shape[0] // 2
        self.send(along[:half], along[half:], "batch", "yy")

    def slots(self):
        first, second = self.mine
        return [first] + self.got[: self.cut], [second] + self.got[self.cut :]

    def three(self):
        first, second = self.slots()
        self.send(jnp.stack(first, 0), jnp.stack(second, 0), "yy", "batch")

    def result(self):
        first, second = self.slots()
        made, at = [], 0
        for deep in self.deep:
            cut = [slot[..., at : at + deep, :].reshape(-1, slot.shape[-1]) for slot in first + second]
            made.append(jnp.concatenate(cut, 0))
            at += deep
        return made


class Sum:
    def __init__(self, grads):
        nx, ny, self.nz = (lax.axis_size(a) for a in ("batch", "yy", "head"))
        width = grads[0].shape[1]
        half = [g.shape[0] // 2 for g in grads]
        first = [g[:n].reshape(ny, nx, self.nz // 2, -1, width) for g, n in zip(grads, half)]
        second = [g[n:].reshape(nx, ny, self.nz // 2, -1, width) for g, n in zip(grads, half)]
        self.send(first, second, "yy", "batch")

    def send(self, first, second, one, two):
        def slot(grads, k):
            return jnp.concatenate([g[k] for g in grads], -2)

        self.mine = slot(first, 0), slot(second, 0)
        self.got = [shift(slot(first, k), one, -k) for k in others_of(one)]
        self.cut = len(self.got)
        self.got = self.got + [shift(slot(second, k), two, -k) for k in others_of(two)]

    def add(self, mine, got):
        total = mine.astype(F32)
        for piece in got:
            total = total + piece.astype(F32)
        return total.astype(BF)

    def sums(self):
        first, second = self.mine
        return self.add(first, self.got[: self.cut]), self.add(second, self.got[self.cut :])

    def two(self):
        first, second = self.sums()
        self.send([first], [second], "batch", "yy")

    def three(self):
        first, second = self.sums()
        slots = [first[k] if k < self.nz // 2 else second[k - self.nz // 2] for k in range(self.nz)]
        self.mine, self.got = slots[0], [shift(slots[k], "head", -k) for k in range(1, self.nz)]

    def result(self):
        return self.add(self.mine, self.got)


def in_place(piece, axis):
    if lax.axis_size(axis) != 2:
        return lax.all_gather(piece, axis, axis=0, tiled=False)
    other = shift(piece, axis, 1)
    low = lax.axis_index(axis) == 0
    return jnp.stack([jnp.where(low, piece, other), jnp.where(low, other, piece)], 0)


def gathered(piece):
    sizes = tuple(lax.axis_size(a) for a in ("core", "batch", "yy"))
    return lax.all_gather(piece, ("core", "batch", "yy"), axis=0, tiled=True).reshape(sizes + piece.shape)


def replicate(piece):
    return in_place(in_place(in_place(piece, "yy"), "batch"), "core")


def unfold_kernel(kinds, source_ref, *outs):
    at = 0
    for (size, turned), out in zip(kinds, outs):
        piece = source_ref[..., at : at + size, :].reshape(-1, source_ref.shape[-1]).astype(F32)
        out[...] = piece.T if turned else piece
        at += size


def unfold(whole, kinds):
    width = whole.shape[-1]
    count = whole.shape[0] * whole.shape[1] * whole.shape[2]
    if any(size % 16 for size, _ in kinds):
        made, at = [], 0
        for size, turned in kinds:
            piece = whole[..., at : at + size, :].reshape(-1, width)
            made.append((piece.T if turned else piece).astype(F32))
            at += size
        return made
    step = 256
    return pl.pallas_call(
        functools.partial(unfold_kernel, kinds),
        out_shape=[
            jax.ShapeDtypeStruct((width, count * size) if turned else (count * size, width), F32) for size, turned in kinds
        ],
        grid=(width // step,),
        in_specs=[pl.BlockSpec(whole.shape[:4] + (step,), lambda i: (0, 0, 0, 0, i))],
        out_specs=[
            pl.BlockSpec((step, count * size), lambda i: (i, 0))
            if turned
            else pl.BlockSpec((count * size, step), lambda i: (0, i))
            for size, turned in kinds
        ],
        compiler_params=pltpu.CompilerParams(vmem_limit_bytes=32 * 2**20),
    )(whole)


def total_of(value):
    for axis in ("core", "yy", "batch", "head"):
        count = lax.axis_size(axis)
        step = 1
        while step < count:
            value = value + lax.ppermute(value, axis, [(i, i ^ step) for i in range(count)])
            step *= 2
    return value


class Rows:
    def __init__(self, nx, ny, nz, kinds):
        self.nx, self.ny, self.depth, self.kinds = nx, ny, nz // 2, kinds
        self.size = HEAD_DIM // ny

    def starts(self, half, index, kind):
        x, z = index
        slots = [y * self.nx + x if half == 0 else x * self.ny + y for y in range(self.ny)]
        return [((slot * self.depth + z) * self.kinds + kind) * self.size for slot in slots]

    def read(self, ref, half, index, kind):
        return jnp.concatenate([ref[at : at + self.size, :] for at in self.starts(half, index, kind)], 0)

    def write(self, ref, half, index, kind, value):
        for k, at in enumerate(self.starts(half, index, kind)):
            ref[at : at + self.size, :] = value[k * self.size : (k + 1) * self.size]


def allowed_block(span_ref, base, columns, chunk):
    ahead = lax.broadcasted_iota(jnp.int32, (BLOCK, BLOCK), 0)
    if chunk < BLOCK:
        ahead = ahead + ahead // chunk * chunk
    away = ahead + (base - span_ref[0:1, columns])
    return (away >= 0) & (away <= span_ref[1:2, columns])


def span_of(index):
    return slice(index * BLOCK, (index + 1) * BLOCK)


def per_block(need_ref, base_ref, span_ref, columns, chunk, i, j, work):
    need = need_ref[i * BLOCKS + j]

    @pl.when(need == 1)
    def _():
        allowed = allowed_block(span_ref, base_ref[j], columns, chunk)
        work(lambda scores: jnp.where(allowed, scores, MASKED))

    @pl.when(need == 2)
    def _():
        work(lambda scores: scores)


def attend_kernel(heads, layouts, chunk, need_ref, base_ref, span_ref, *refs):
    *layouts, single = layouts
    count = len(layouts)
    mixed_ref, lse_ref, q_s, k_s, v_s, top_s, sum_s, acc_s = refs[count:]
    where = [(source, lay, kind) for source, lay in zip(refs[:count], layouts) for kind in range(lay.kinds)]
    every = range(len(heads))

    def load(half):
        for h, index in enumerate(heads):
            q, k, v = (lay.read(source, half, index, kind) for source, lay, kind in where)
            q_s[h] = (q.astype(F32) * SCALE).astype(BF)
            k_s[h] = k.T
            v_s[h] = v

    half_now = pl.program_id(0)
    for half in range(2):
        pl.when(half_now == half)(functools.partial(load, half))

    for i in range(BLOCKS):
        columns = span_of(i)
        top_s[...] = jnp.full(top_s.shape, -3e38, F32)
        sum_s[...] = jnp.zeros(sum_s.shape, F32)
        acc_s[...] = jnp.zeros(acc_s.shape, F32)
        for j in range(BLOCKS):
            keys = span_of(j)

            def work(mask, keys=keys, columns=columns):
                scores = [mask(dot(k_s[h, keys, :], q_s[h, :, columns], 1, 0)) for h in every]
                tops = [jnp.maximum(top_s[h], jnp.max(scores[h], 0, keepdims=True)) for h in every]
                weights = [jnp.exp(scores[h] - tops[h]) for h in every]
                fades = [jnp.exp(top_s[h] - tops[h]) for h in every]
                mixed = [dot(v_s[h, :, keys], weights[h].astype(BF), 1, 0) for h in every]
                for h in every:
                    top_s[h] = tops[h]
                    sum_s[h] = sum_s[h] * fades[h] + jnp.sum(weights[h], 0, keepdims=True)
                    acc_s[h] = acc_s[h] * fades[h] + mixed[h]

            per_block(need_ref, base_ref, span_ref, columns, chunk, i, j, work)

        for h in every:
            lse_ref[0, h, :, columns] = top_s[h] + jnp.log(sum_s[h])
            q_s[h, :, columns] = (acc_s[h] / sum_s[h]).astype(BF)

    def store(half):
        for h, index in enumerate(heads):
            single.write(mixed_ref, half, index, 0, q_s[h])

    for half in range(2):
        pl.when(half_now == half)(functools.partial(store, half))


def attend_back_kernel(heads, layouts, chunk, need_ref, base_ref, span_ref, *refs):
    *layouts, single = layouts
    count = len(layouts)
    mixed_ref, grad_ref, lse_ref = refs[count : count + 3]
    q_s, k_s, kt_s, v_s, g_s, inner_s, dq_s, dk_s, dv_s = refs[2 * count + 3 :]
    where = [(source, lay, kind) for source, lay in zip(refs[:count], layouts) for kind in range(lay.kinds)]
    outs = refs[count + 3 : 2 * count + 3]
    into = [(out, lay, kind) for out, lay in zip(outs, layouts) for kind in range(lay.kinds)]
    every = range(len(heads))

    def load(half):
        for h, index in enumerate(heads):
            q, k, v = (lay.read(source, half, index, kind) for source, lay, kind in where)
            q_s[h] = (q.astype(F32) * SCALE).astype(BF)
            kt_s[h] = k
            k_s[h] = k.T
            v_s[h] = v.T
            grad = single.read(grad_ref, half, index, 0)
            g_s[h] = grad
            mixed = single.read(mixed_ref, half, index, 0)
            inner_s[h] = jnp.sum(grad.astype(F32) * mixed.astype(F32), 0, keepdims=True)

    half_now = pl.program_id(0)
    for half in range(2):
        pl.when(half_now == half)(functools.partial(load, half))

    for acc in (dq_s, dk_s, dv_s):
        acc[...] = jnp.zeros(acc.shape, F32)

    for i in range(BLOCKS):
        columns = span_of(i)
        for j in range(BLOCKS):
            keys = span_of(j)

            def work(mask, keys=keys, columns=columns):
                scores = [mask(dot(k_s[h, keys, :], q_s[h, :, columns], 1, 0)) for h in every]
                steep = [dot(v_s[h, keys, :], g_s[h, :, columns], 1, 0) for h in every]
                chances = [jnp.exp(scores[h] - lse_ref[0, h, :, columns]) for h in every]
                back = [(chances[h] * (steep[h] - inner_s[h, :, columns])).astype(BF) for h in every]
                for h in every:
                    dv_s[h, :, keys] += dot(g_s[h, :, columns], chances[h].astype(BF), 1, 1)
                for h in every:
                    dk_s[h, :, keys] += dot(q_s[h, :, columns], back[h], 1, 1)
                for h in every:
                    dq_s[h, :, columns] += dot(kt_s[h, :, keys], back[h], 1, 0)

            per_block(need_ref, base_ref, span_ref, columns, chunk, i, j, work)

    def store(half):
        for h, index in enumerate(heads):
            made = (dq_s[h] * SCALE, dk_s[h], dv_s[h])
            for (out, lay, kind), value in zip(into, made):
                lay.write(out, half, index, kind, value.astype(BF))

    for half in range(2):
        pl.when(half_now == half)(functools.partial(store, half))


class Heads:
    def __init__(self, nx, ny, nz, chunk):
        self.nx, self.ny, self.nz, self.chunk = nx, ny, nz, chunk
        self.index = [(x, z) for x in range(nx) for z in range(nz // 2)]
        self.plain = (HEAD_DIM // ny) % 16 == 0

    def split(self, matrix, kinds):
        if self.plain:
            return matrix
        nx, ny, deep = self.nx, self.ny, self.nz // 2
        half, rows = matrix.shape[0] // 2, HEAD_DIM // ny
        first = matrix[:half].reshape(ny, nx, deep, kinds, rows, LEN).transpose(1, 2, 3, 0, 4, 5)
        second = matrix[half:].reshape(nx, ny, deep, kinds, rows, LEN).transpose(0, 2, 3, 1, 4, 5)
        return jnp.stack([first, second], 0).reshape(-1, LEN)

    def join(self, split, kinds):
        if self.plain:
            return split
        nx, ny, deep = self.nx, self.ny, self.nz // 2
        cut = split.reshape(2, nx, deep, kinds, ny, HEAD_DIM // ny, LEN)
        first = cut[0].transpose(3, 0, 1, 2, 4, 5).reshape(-1, LEN)
        second = cut[1].transpose(0, 3, 1, 2, 4, 5).reshape(-1, LEN)
        return jnp.concatenate([first, second], 0)

    def call(self, kernel, kinds, tables, arrays, outs, scratch, flops):
        need, bases, spans = tables
        layouts = [Rows(self.nx, self.ny if self.plain else 1, self.nz, k) for k in kinds + (1,)]

        def by_half(shape):
            rest = (0,) * (len(shape) - 1)
            return pl.BlockSpec((shape[0] // 2,) + tuple(shape[1:]), lambda i, *_: (i,) + rest)

        return pl.pallas_call(
            functools.partial(kernel, self.index, layouts, self.chunk),
            out_shape=outs,
            grid_spec=pltpu.PrefetchScalarGridSpec(
                num_scalar_prefetch=2,
                grid=(2,),
                in_specs=[pl.BlockSpec((2, LEN), lambda i, *_: (0, 0))] + [by_half(a.shape) for a in arrays],
                out_specs=[by_half(o.shape) for o in outs],
                scratch_shapes=scratch,
            ),
            compiler_params=pltpu.CompilerParams(vmem_limit_bytes=48 * 2**20),
            cost_estimate=pl.CostEstimate(flops=flops, bytes_accessed=8 * 2**20, transcendentals=4 * 2**20),
        )(need, bases, spans, *arrays)

    def attend(self, tables, sources, kinds):
        count = len(self.index)
        split = [self.split(s, k) for s, k in zip(sources, kinds)]
        wide = (count, HEAD_DIM, LEN)
        mixed, lse = self.call(
            attend_kernel,
            kinds,
            tables,
            split,
            [
                jax.ShapeDtypeStruct((2 * count * HEAD_DIM, LEN), BF),
                jax.ShapeDtypeStruct((2, count, 1, LEN), F32),
            ],
            [
                pltpu.VMEM(wide, BF),
                pltpu.VMEM((count, LEN, HEAD_DIM), BF),
                pltpu.VMEM(wide, BF),
                pltpu.VMEM((count, 1, BLOCK), F32),
                pltpu.VMEM((count, 1, BLOCK), F32),
                pltpu.VMEM((count, HEAD_DIM, BLOCK), F32),
            ],
            40 * 10**9,
        )
        return self.join(mixed, 1), lse

    def attend_back(self, tables, sources, kinds, mixed, grad, lse):
        count = len(self.index)
        split = [self.split(s, k) for s, k in zip(sources, kinds)]
        wide, tall = (count, HEAD_DIM, LEN), (count, LEN, HEAD_DIM)
        grads = self.call(
            attend_back_kernel,
            kinds,
            tables,
            split + [self.split(mixed, 1), self.split(grad, 1), lse],
            [jax.ShapeDtypeStruct(s.shape, BF) for s in split],
            [
                pltpu.VMEM(wide, BF),
                pltpu.VMEM(tall, BF),
                pltpu.VMEM(wide, BF),
                pltpu.VMEM(tall, BF),
                pltpu.VMEM(wide, BF),
                pltpu.VMEM((count, 1, LEN), F32),
                pltpu.VMEM(wide, F32),
                pltpu.VMEM(wide, F32),
                pltpu.VMEM(wide, F32),
            ],
            46 * 10**9,
        )
        return [self.join(g, k) for g, k in zip(grads, kinds)]


def body(
    inputs,
    memory,
    cotangent,
    tgt_lengths,
    src_ids,
    gain_one,
    w_query,
    w_key,
    w_value,
    w_out,
    gain_two,
    w_cross_query,
    w_mem_key,
    w_mem_value,
    w_cross_out,
    gain_three,
    w_up,
    w_down,
):
    nx, ny, nz = (lax.axis_size(a) for a in ("batch", "yy", "head"))
    ix, iy, core, iz = (lax.axis_index(a) for a in ("batch", "yy", "core", "head"))
    rows = inputs.shape[0]
    nxy, place = nx * ny, ix * ny + iy
    chunk = LEN // (2 * ny)

    def part(matrix):
        deep = matrix.shape[0] // 2 // nxy
        return lax.dynamic_slice_in_dim(matrix, (core * nxy + place) * deep, deep, 0)

    def column_parts(*matrices):
        parts = []
        for matrix in matrices:
            wide = matrix.shape[1] // 2
            turned = lax.dynamic_slice_in_dim(matrix, core * wide, wide, 1).T
            parts.append(lax.dynamic_slice_in_dim(turned, place * (wide // nxy), wide // nxy, 0))
        return jnp.concatenate(parts, 0)

    row = iy * nz + iz
    lengths = lax.dynamic_index_in_dim(tgt_lengths, row, 0, keepdims=False)
    source_ids = lax.dynamic_index_in_dim(src_ids, row, 0, keepdims=False)
    index = jnp.arange(LEN, dtype=jnp.int32)
    within = index % (LEN // 2)
    turn = jnp.where(index < LEN // 2, core, 1 - core)
    positions = (2 * (within // chunk) + turn) * chunk + within % chunk
    ends = jnp.cumsum(lengths)
    starts = ends - lengths
    reached = positions[:, None] >= starts[None, :]
    target_ids = jnp.sum(reached.astype(jnp.int32), -1) - 1
    self_start = jnp.max(jnp.where(reached, starts[None, :], 0), -1)
    kinds = jnp.arange(lengths.shape[0], dtype=jnp.int32)
    source_start = jnp.sum((source_ids[None, :] < kinds[:, None]).astype(jnp.int32), -1)
    source_end = jnp.sum((source_ids[None, :] <= kinds[:, None]).astype(jnp.int32), -1) - 1
    mine = target_ids[:, None] == kinds[None, :]
    cross_start = jnp.sum(jnp.where(mine, source_start[None, :], 0), -1)
    cross_end = jnp.sum(jnp.where(mine, source_end[None, :], 0), -1)
    block_positions = positions.reshape(BLOCKS, BLOCK)
    lowest, highest = jnp.min(block_positions, 1), jnp.max(block_positions, 1)

    def tables_of(start, end):
        least = jnp.min(start.reshape(BLOCKS, BLOCK), 1)
        most = jnp.max(end.reshape(BLOCKS, BLOCK), 1)
        some = (least[:, None] <= highest[None, :]) & (most[:, None] >= lowest[None, :])
        last, first = jnp.max(start.reshape(BLOCKS, BLOCK), 1), jnp.min(end.reshape(BLOCKS, BLOCK), 1)
        whole = (last[:, None] <= lowest[None, :]) & (first[:, None] >= highest[None, :])
        need = jnp.where(whole, 2, some.astype(jnp.int32))
        return need.reshape(-1), lowest, jnp.stack([start, end - start], 0)

    self_tables = tables_of(self_start, positions)
    cross_tables = tables_of(cross_start, cross_end)
    heads = Heads(nx, ny, nz, chunk)

    residual = to_row(inputs).astype(F32)
    self_weights = Gather([column_parts(w_query, w_key, w_value)])
    residual = to_row(tied(inputs, self_weights.got))
    self_weights.two()
    residual = meet(residual, self_weights)
    self_weights.three()
    cross_weights = Gather(
        [part(w_out), column_parts(w_mem_key, w_mem_value), column_parts(w_cross_query), part(w_cross_out)],
        residual,
    )
    (normed_one,) = normalize([tied(residual, self_weights.mine, cross_weights.mine)], gain_one)
    normed_one = both(normed_one)
    normed_one = meet(normed_one, self_weights)
    (w_self,) = self_weights.result()
    qkv = dot(w_self, normed_one, 1, 1).astype(BF)
    qkv = meet(qkv, cross_weights)
    cross_weights.two()
    up_weights = Gather([column_parts(w_up)], cross_weights.mine)
    source_own = to_row(tied(memory, up_weights.mine))
    qkv = meet(qkv, cross_weights)
    cross_weights.three()
    qkv = tied(qkv, cross_weights.mine)
    self_mixed, self_lse = heads.attend(self_tables, (qkv,), (3,))
    self_mixed, source_own = meet((self_mixed, source_own), cross_weights, up_weights)
    down_weights = Gather([part(w_down)], up_weights.got)
    up_weights.two()
    self_mixed = tied(self_mixed, up_weights.mine, down_weights.mine)
    w_o, w_mem, w_cq, w_co = cross_weights.result()
    normed_two, after_self = normalize([residual, *own_parts(self_mixed, w_o)], gain_two)
    normed_two = meet(normed_two, up_weights, down_weights)
    up_weights.three()
    down_weights.two()
    normed_two, source_own = tied((normed_two, source_own), up_weights.mine, down_weights.mine)
    cot_own = to_row(tied(cotangent, up_weights.mine, source_own))
    source = both(source_own)
    mkv = dot(w_mem, source, 1, 1).astype(BF)
    normed_two = both(normed_two)
    cq = dot(w_cq, normed_two, 1, 1).astype(BF)
    cross_mixed, cross_lse = heads.attend(cross_tables, (cq, mkv), (1, 2))
    cross_mixed, cot_own = meet((cross_mixed, cot_own), up_weights, down_weights)
    down_weights.three()
    cross_mixed = tied(cross_mixed, down_weights.mine)
    cot = both(cot_own)
    normed_three, after_cross = normalize([after_self, *own_parts(cross_mixed, w_co)], gain_three)
    normed_three = both(normed_three)
    (w_u,) = up_weights.result()

    def weight_grad(transposed, tokens):
        return dot(transposed, tokens, 1, 0).astype(BF)

    hidden_pre = dot(w_u, normed_three, 1, 1)
    squared = hidden_pre * hidden_pre
    bent = jnp.tanh(GELU_A * hidden_pre * (1.0 + GELU_B * squared))
    gate = 0.5 + 0.5 * bent
    slope = gate + (0.5 * GELU_A) * hidden_pre * (1.0 - bent * bent) * (1.0 + 3.0 * GELU_B * squared)
    hidden_act, slope = lax.optimization_barrier(((hidden_pre * gate).astype(BF), slope.astype(BF)))
    down_sum = Sum([weight_grad(hidden_act, cot)])
    hidden_act = meet(tied(hidden_act, down_sum.mine), down_weights)
    (w_d,) = down_weights.result()
    output = (after_cross + own_sum(hidden_act, w_d)).astype(BF)
    output = from_row(output, rows)

    grad_pre = (slope.astype(F32) * dot(w_d, cot, 1, 1)).astype(BF)
    grad_pre = meet(grad_pre, down_sum)
    down_sum.two()
    third_back = own_parts(tied(grad_pre, down_sum.mine), w_u)
    grad_after_cross, cross_grad, grad_gain_three = normalize_back(after_cross, gain_three, third_back, cot_own)

    cross_grad = both(cross_grad)
    up_sum = Sum([weight_grad(tied(grad_pre, down_sum.mine), normed_three)])
    grad_cross_mixed = dot(w_co, cross_grad, 1, 1).astype(BF)
    grad_cross_mixed = meet(grad_cross_mixed, down_sum)
    down_sum.three()
    grad_cross_mixed = tied(grad_cross_mixed, up_sum.mine, down_sum.mine)
    gcq, gmkv = heads.attend_back(
        cross_tables, (cq, mkv), (1, 2), cross_mixed, grad_cross_mixed, cross_lse
    )
    gcq, gmkv, output = meet((gcq, gmkv, output), up_sum, down_sum)
    up_sum.two()
    down_all = gathered(down_sum.result())
    gcq, gmkv = tied((gcq, gmkv), up_sum.mine)
    grad_after_self, self_grad, grad_gain_two = normalize_back(
        after_self, gain_two, own_parts(gcq, w_cq), grad_after_cross
    )
    self_grad = meet(self_grad, up_sum)
    up_sum.three()
    self_grad = both(self_grad)
    g_co = weight_grad(cross_mixed, cross_grad)
    g_cq = weight_grad(gcq, normed_two)
    g_mem = weight_grad(gmkv, source)
    g_o = weight_grad(self_mixed, self_grad)
    cross_sum = Sum([g_co, g_cq, g_mem])
    memory_back = own_sum(gmkv, w_mem).astype(BF)
    grad_self_mixed = dot(w_o, self_grad, 1, 1).astype(BF)
    grad_self_mixed, memory_back = tied((grad_self_mixed, memory_back), up_sum.mine, cross_sum.mine, g_o)
    grad_memory = from_row(memory_back, rows)
    (gqkv,) = heads.attend_back(self_tables, (qkv,), (3,), self_mixed, grad_self_mixed, self_lse)
    gqkv, down_all = meet((gqkv, down_all), cross_sum, up_sum)
    cross_sum.two()
    up_all = gathered(up_sum.result())
    g_self = weight_grad(gqkv, normed_one)
    self_sum = Sum([g_o, g_self])
    first_back = own_parts(tied(gqkv, self_sum.mine), w_self)
    first_back, grad_memory = lax.optimization_barrier((first_back, grad_memory))
    _, grad_inputs, grad_gain_one = normalize_back(residual, gain_one, first_back, grad_after_self)
    grad_inputs = from_row(grad_inputs, rows).astype(F32)
    gains = total_of(jnp.stack([grad_gain_one, grad_gain_two, grad_gain_three]))
    self_sum.two()
    cross_sum.got = tied(cross_sum.got, self_sum.mine)
    cross_sum.three()
    self_sum.three()

    deep = w_query.shape[1] // 2 // nxy
    far = w_up.shape[1] // 2 // nxy
    (grad_down,) = unfold(down_all, [(far, False)])
    (grad_up,) = unfold(up_all, [(far, True)])
    grad_co, grad_cq, grad_mk, grad_mv = unfold(
        gathered(cross_sum.result()), [(deep, False), (deep, True), (deep, True), (deep, True)]
    )
    self_sum.got = tied(self_sum.got, grad_down, grad_up, grad_inputs, gains, grad_memory)
    grad_o, grad_q, grad_k, grad_v = unfold(
        replicate(self_sum.result()), [(deep, False), (deep, True), (deep, True), (deep, True)]
    )
    return (
        output,
        grad_inputs,
        grad_memory.astype(F32),
        gains[0],
        grad_q,
        grad_k,
        grad_v,
        grad_o,
        gains[1],
        grad_cq,
        grad_mk,
        grad_mv,
        grad_co,
        gains[2],
        grad_up,
        grad_down,
    )


def solution(mesh):
    nb, ns, nh = (mesh.shape[a] for a in ("batch", "seq", "head"))
    fine = Mesh(mesh.devices.reshape(nb, ns // 2, 2, nh), ("batch", "yy", "core", "head"))
    tokens = P("batch", ("yy", "core", "head"), None)
    ids = P("batch", None)
    wide, tall = P(None, "head"), P("head", None)
    return jax.shard_map(
        body,
        mesh=fine,
        in_specs=(
            tokens, tokens, tokens, ids, ids,
            P(), wide, wide, wide, tall,
            P(), wide, wide, wide, tall,
            P(), wide, tall,
        ),
        out_specs=(
            tokens, tokens, tokens,
            P(), wide, wide, wide, tall,
            P(), wide, wide, wide, tall,
            P(), wide, tall,
        ),
        check_vma=False,
    )
```

```python
import functools

import jax
import jax.numpy as jnp
from jax import lax
from jax.experimental import pallas as pl
from jax.experimental.pallas import tpu as pltpu
from jax.sharding import Mesh
from jax.sharding import PartitionSpec as P

HEAD_DIM = 64
LEN = 1024
BLOCK = 256
BLOCKS = LEN // BLOCK
EPSILON = 1e-05
MASKED = -1000000000.0
SCALE = HEAD_DIM**-0.5
GELU_A = 0.7978845608028654
GELU_B = 0.044715
BF = jnp.bfloat16
F32 = jnp.float32


def dot(left, right, left_dim, right_dim):
    return lax.dot_general(
        left, right, (((left_dim,), (right_dim,)), ((), ())), preferred_element_type=F32
    )


STEP = 128


def centred(activity):
    shifted = activity - jnp.mean(activity, -1, keepdims=True)
    return shifted, lax.rsqrt(jnp.mean(shifted * shifted, -1, keepdims=True) + EPSILON)


def norm_kernel(terms, gain_ref, *refs):
    activity = refs[0][...].astype(F32)
    for ref in refs[1:terms]:
        activity = activity + ref[...].astype(F32)
    shifted, rate = centred(activity)
    refs[terms][...] = (shifted * rate * gain_ref[...]).astype(BF)
    if terms > 1:
        refs[terms + 1][...] = activity


def norm_back_kernel(gain_ref, activity_ref, own_ref, other_ref, onward_ref, grad_ref, rounded_ref, gain_grad_ref):
    shifted, rate = centred(activity_ref[...].astype(F32))
    unit = shifted * rate
    arrived = own_ref[...] + other_ref[...].astype(F32)
    scaled = arrived * gain_ref[...]
    inner = scaled - jnp.mean(scaled, -1, keepdims=True)
    step = rate * (inner - unit * jnp.mean(scaled * unit, -1, keepdims=True))
    total = onward_ref[...].astype(F32) + step
    grad_ref[...] = total
    rounded_ref[...] = total.astype(BF)

    @pl.when(pl.program_id(0) == 0)
    def _():
        gain_grad_ref[...] = jnp.zeros(gain_grad_ref.shape, F32)

    gain_grad_ref[...] += jnp.sum(arrived * unit, 0, keepdims=True)


def by_rows(kernel, gain, arrays, outs, sums=0):
    tokens, width = arrays[0].shape
    tile, line = pl.BlockSpec((STEP, width), lambda i: (i, 0)), pl.BlockSpec((1, width), lambda i: (0, 0))
    return pl.pallas_call(
        kernel,
        out_shape=[jax.ShapeDtypeStruct((tokens, width), t) for t in outs]
        + [jax.ShapeDtypeStruct((1, width), F32)] * sums,
        grid=(tokens // STEP,),
        in_specs=[line] + [tile] * len(arrays),
        out_specs=[tile] * len(outs) + [line] * sums,
        compiler_params=pltpu.CompilerParams(vmem_limit_bytes=32 * 2**20),
        cost_estimate=pl.CostEstimate(flops=20 * tokens * width, bytes_accessed=8 * tokens * width, transcendentals=tokens),
    )(gain.reshape(1, width), *arrays)


def normalize(terms, gain):
    return by_rows(functools.partial(norm_kernel, len(terms)), gain, terms, [BF] + [F32] * (len(terms) > 1))


def normalize_back(activity, gain, arrived, onward):
    grad, rounded, gain_grad = by_rows(norm_back_kernel, gain, [activity, *arrived, onward], [F32, BF], 1)
    return grad, rounded, gain_grad[0]


def shift(piece, axis, step):
    count = lax.axis_size(axis)
    return lax.ppermute(piece, axis, [(i, (i + step) % count) for i in range(count)])


def core_swap(piece):
    return shift(piece, "core", 1)


def both(own):
    return jnp.concatenate([own, core_swap(own)], 0)


def own_parts(transposed, matrix):
    half = transposed.shape[1] // 2
    other = core_swap(dot(transposed[:, half:], matrix, 0, 0).astype(BF))
    return [dot(transposed[:, :half], matrix, 0, 0), other]


def own_sum(transposed, matrix):
    own, other = own_parts(transposed, matrix)
    return own + other.astype(F32)


def to_row(tokens):
    rows, span, width = tokens.shape
    moved = lax.all_to_all(tokens, ("yy", "head"), 0, 0, tiled=True)
    return moved.reshape(rows * span, width)


def from_row(own, rows):
    parts = own.reshape(rows, own.shape[0] // rows, own.shape[1])
    return lax.all_to_all(parts, ("yy", "head"), 0, 0, tiled=True)


def tied(values, *others):
    return lax.optimization_barrier((values, others))[0]


def meet(values, *moves):
    values, got = lax.optimization_barrier((values, [m.got for m in moves]))
    for move, pieces in zip(moves, got):
        move.got = pieces
    return values


def others_of(axis):
    return range(1, lax.axis_size(axis))


class Gather:
    def __init__(self, parts, *others):
        self.deep = [p.shape[0] for p in parts]
        self.mine = tied(jnp.concatenate(parts, 0), *others)
        self.got = [shift(self.mine, "head", k) for k in others_of("head")]

    def send(self, first, second, one, two):
        self.mine = first, second
        self.got = [shift(first, one, k) for k in others_of(one)] + [shift(second, two, k) for k in others_of(two)]
        self.cut = len(others_of(one))

    def two(self):
        along = jnp.stack([self.mine] + self.got, 0)
        half = along.shape[0] // 2
        self.send(along[:half], along[half:], "batch", "yy")

    def slots(self):
        first, second = self.mine
        return [first] + self.got[: self.cut], [second] + self.got[self.cut :]

    def three(self):
        first, second = self.slots()
        self.send(jnp.stack(first, 0), jnp.stack(second, 0), "yy", "batch")

    def result(self):
        first, second = self.slots()
        made, at = [], 0
        for deep in self.deep:
            cut = [slot[..., at : at + deep, :].reshape(-1, slot.shape[-1]) for slot in first + second]
            made.append(jnp.concatenate(cut, 0))
            at += deep
        return made


class Sum:
    def __init__(self, grads):
        nx, ny, self.nz = (lax.axis_size(a) for a in ("batch", "yy", "head"))
        width = grads[0].shape[1]
        half = [g.shape[0] // 2 for g in grads]
        first = [g[:n].reshape(ny, nx, self.nz // 2, -1, width) for g, n in zip(grads, half)]
        second = [g[n:].reshape(nx, ny, self.nz // 2, -1, width) for g, n in zip(grads, half)]
        self.send(first, second, "yy", "batch")

    def send(self, first, second, one, two):
        def slot(grads, k):
            return jnp.concatenate([g[k] for g in grads], -2)

        self.mine = slot(first, 0), slot(second, 0)
        self.got = [shift(slot(first, k), one, -k) for k in others_of(one)]
        self.cut = len(self.got)
        self.got = self.got + [shift(slot(second, k), two, -k) for k in others_of(two)]

    def add(self, mine, got):
        total = mine.astype(F32)
        for piece in got:
            total = total + piece.astype(F32)
        return total.astype(BF)

    def sums(self):
        first, second = self.mine
        return self.add(first, self.got[: self.cut]), self.add(second, self.got[self.cut :])

    def two(self):
        first, second = self.sums()
        self.send([first], [second], "batch", "yy")

    def three(self):
        first, second = self.sums()
        slots = [first[k] if k < self.nz // 2 else second[k - self.nz // 2] for k in range(self.nz)]
        self.mine, self.got = slots[0], [shift(slots[k], "head", -k) for k in range(1, self.nz)]

    def result(self):
        return self.add(self.mine, self.got)


def in_place(piece, axis, beside):
    if lax.axis_size(axis) != 2:
        return lax.all_gather(piece, axis, axis=0, tiled=False), beside
    other, beside = lax.optimization_barrier((shift(piece, axis, 1), beside))
    low = lax.axis_index(axis) == 0
    return jnp.stack([jnp.where(low, piece, other), jnp.where(low, other, piece)], 0), beside


def gathered(piece):
    sizes = tuple(lax.axis_size(a) for a in ("core", "batch", "yy"))
    return lax.all_gather(piece, ("core", "batch", "yy"), axis=0, tiled=True).reshape(sizes + piece.shape)


def replicate(piece, *beside):
    done = []
    for axis, values in zip(("yy", "batch", "core"), beside):
        piece, values = in_place(piece, axis, values)
        done.append(values)
    return piece, *done


def unfold_kernel(kinds, source_ref, *outs):
    at = 0
    for (size, turned), out in zip(kinds, outs):
        piece = source_ref[..., at : at + size, :].reshape(-1, source_ref.shape[-1]).astype(F32)
        out[...] = piece.T if turned else piece
        at += size


def unfold(whole, kinds):
    width = whole.shape[-1]
    count = whole.shape[0] * whole.shape[1] * whole.shape[2]
    if any(size % 16 for size, _ in kinds):
        made, at = [], 0
        for size, turned in kinds:
            piece = whole[..., at : at + size, :].reshape(-1, width)
            made.append((piece.T if turned else piece).astype(F32))
            at += size
        return made
    step = 256
    return pl.pallas_call(
        functools.partial(unfold_kernel, kinds),
        out_shape=[
            jax.ShapeDtypeStruct((width, count * size) if turned else (count * size, width), F32) for size, turned in kinds
        ],
        grid=(width // step,),
        in_specs=[pl.BlockSpec(whole.shape[:4] + (step,), lambda i: (0, 0, 0, 0, i))],
        out_specs=[
            pl.BlockSpec((step, count * size), lambda i: (i, 0))
            if turned
            else pl.BlockSpec((count * size, step), lambda i: (0, i))
            for size, turned in kinds
        ],
        compiler_params=pltpu.CompilerParams(vmem_limit_bytes=32 * 2**20),
    )(whole)


def total_of(value, axis):
    count = lax.axis_size(axis)
    step = 1
    while step < count:
        value = value + lax.ppermute(value, axis, [(i, i ^ step) for i in range(count)])
        step *= 2
    return value


class Rows:
    def __init__(self, nx, ny, nz, kinds):
        self.nx, self.ny, self.depth, self.kinds = nx, ny, nz // 2, kinds
        self.size = HEAD_DIM // ny

    def starts(self, half, index, kind):
        x, z = index
        slots = [y * self.nx + x if half == 0 else x * self.ny + y for y in range(self.ny)]
        return [((slot * self.depth + z) * self.kinds + kind) * self.size for slot in slots]

    def read(self, ref, half, index, kind):
        return jnp.concatenate([ref[at : at + self.size, :] for at in self.starts(half, index, kind)], 0)

    def write(self, ref, half, index, kind, value):
        for k, at in enumerate(self.starts(half, index, kind)):
            ref[at : at + self.size, :] = value[k * self.size : (k + 1) * self.size]


def allowed_block(span_ref, base, columns, chunk):
    ahead = lax.broadcasted_iota(jnp.int32, (BLOCK, BLOCK), 0)
    if chunk < BLOCK:
        ahead = ahead + ahead // chunk * chunk
    away = ahead + (base - span_ref[0:1, columns])
    return (away >= 0) & (away <= span_ref[1:2, columns])


def span_of(index):
    return slice(index * BLOCK, (index + 1) * BLOCK)


def per_block(need_ref, base_ref, span_ref, columns, chunk, i, j, work):
    need = need_ref[i * BLOCKS + j]

    @pl.when(need == 1)
    def _():
        allowed = allowed_block(span_ref, base_ref[j], columns, chunk)
        work(lambda scores: jnp.where(allowed, scores, MASKED))

    @pl.when(need == 2)
    def _():
        work(lambda scores: scores)


def attend_kernel(heads, layouts, chunk, need_ref, base_ref, span_ref, *refs):
    *layouts, single = layouts
    count = len(layouts)
    mixed_ref, lse_ref, q_s, k_s, v_s, top_s, sum_s, acc_s = refs[count:]
    where = [(source, lay, kind) for source, lay in zip(refs[:count], layouts) for kind in range(lay.kinds)]
    every = range(len(heads))

    def load(half):
        for h, index in enumerate(heads):
            q, k, v = (lay.read(source, half, index, kind) for source, lay, kind in where)
            q_s[h] = (q.astype(F32) * SCALE).astype(BF)
            k_s[h] = k.T
            v_s[h] = v

    half_now = pl.program_id(0)
    for half in range(2):
        pl.when(half_now == half)(functools.partial(load, half))

    for i in range(BLOCKS):
        columns = span_of(i)
        top_s[...] = jnp.full(top_s.shape, -3e38, F32)
        sum_s[...] = jnp.zeros(sum_s.shape, F32)
        acc_s[...] = jnp.zeros(acc_s.shape, F32)
        for j in range(BLOCKS):
            keys = span_of(j)

            def work(mask, keys=keys, columns=columns):
                scores = [mask(dot(k_s[h, keys, :], q_s[h, :, columns], 1, 0)) for h in every]
                tops = [jnp.maximum(top_s[h], jnp.max(scores[h], 0, keepdims=True)) for h in every]
                weights = [jnp.exp(scores[h] - tops[h]) for h in every]
                fades = [jnp.exp(top_s[h] - tops[h]) for h in every]
                mixed = [dot(v_s[h, :, keys], weights[h].astype(BF), 1, 0) for h in every]
                for h in every:
                    top_s[h] = tops[h]
                    sum_s[h] = sum_s[h] * fades[h] + jnp.sum(weights[h], 0, keepdims=True)
                    acc_s[h] = acc_s[h] * fades[h] + mixed[h]

            per_block(need_ref, base_ref, span_ref, columns, chunk, i, j, work)

        for h in every:
            lse_ref[0, h, :, columns] = top_s[h] + jnp.log(sum_s[h])
            q_s[h, :, columns] = (acc_s[h] / sum_s[h]).astype(BF)

    def store(half):
        for h, index in enumerate(heads):
            single.write(mixed_ref, half, index, 0, q_s[h])

    for half in range(2):
        pl.when(half_now == half)(functools.partial(store, half))


def attend_back_kernel(heads, layouts, chunk, need_ref, base_ref, span_ref, *refs):
    *layouts, single = layouts
    count = len(layouts)
    mixed_ref, grad_ref, lse_ref = refs[count : count + 3]
    q_s, k_s, kt_s, v_s, g_s, inner_s, dq_s, dk_s, dv_s = refs[2 * count + 3 :]
    where = [(source, lay, kind) for source, lay in zip(refs[:count], layouts) for kind in range(lay.kinds)]
    outs = refs[count + 3 : 2 * count + 3]
    into = [(out, lay, kind) for out, lay in zip(outs, layouts) for kind in range(lay.kinds)]
    every = range(len(heads))

    def load(half):
        for h, index in enumerate(heads):
            q, k, v = (lay.read(source, half, index, kind) for source, lay, kind in where)
            q_s[h] = (q.astype(F32) * SCALE).astype(BF)
            kt_s[h] = k
            k_s[h] = k.T
            v_s[h] = v.T
            grad = single.read(grad_ref, half, index, 0)
            g_s[h] = grad
            mixed = single.read(mixed_ref, half, index, 0)
            inner_s[h] = jnp.sum(grad.astype(F32) * mixed.astype(F32), 0, keepdims=True)

    half_now = pl.program_id(0)
    for half in range(2):
        pl.when(half_now == half)(functools.partial(load, half))

    for acc in (dq_s, dk_s, dv_s):
        acc[...] = jnp.zeros(acc.shape, F32)

    for i in range(BLOCKS):
        columns = span_of(i)
        for j in range(BLOCKS):
            keys = span_of(j)

            def work(mask, keys=keys, columns=columns):
                scores = [mask(dot(k_s[h, keys, :], q_s[h, :, columns], 1, 0)) for h in every]
                steep = [dot(v_s[h, keys, :], g_s[h, :, columns], 1, 0) for h in every]
                chances = [jnp.exp(scores[h] - lse_ref[0, h, :, columns]) for h in every]
                back = [(chances[h] * (steep[h] - inner_s[h, :, columns])).astype(BF) for h in every]
                for h in every:
                    dv_s[h, :, keys] += dot(g_s[h, :, columns], chances[h].astype(BF), 1, 1)
                for h in every:
                    dk_s[h, :, keys] += dot(q_s[h, :, columns], back[h], 1, 1)
                for h in every:
                    dq_s[h, :, columns] += dot(kt_s[h, :, keys], back[h], 1, 0)

            per_block(need_ref, base_ref, span_ref, columns, chunk, i, j, work)

    def store(half):
        for h, index in enumerate(heads):
            made = (dq_s[h] * SCALE, dk_s[h], dv_s[h])
            for (out, lay, kind), value in zip(into, made):
                lay.write(out, half, index, kind, value.astype(BF))

    for half in range(2):
        pl.when(half_now == half)(functools.partial(store, half))


class Heads:
    def __init__(self, nx, ny, nz, chunk):
        self.nx, self.ny, self.nz, self.chunk = nx, ny, nz, chunk
        self.index = [(x, z) for x in range(nx) for z in range(nz // 2)]
        self.plain = (HEAD_DIM // ny) % 16 == 0

    def split(self, matrix, kinds):
        if self.plain:
            return matrix
        nx, ny, deep = self.nx, self.ny, self.nz // 2
        half, rows = matrix.shape[0] // 2, HEAD_DIM // ny
        first = matrix[:half].reshape(ny, nx, deep, kinds, rows, LEN).transpose(1, 2, 3, 0, 4, 5)
        second = matrix[half:].reshape(nx, ny, deep, kinds, rows, LEN).transpose(0, 2, 3, 1, 4, 5)
        return jnp.stack([first, second], 0).reshape(-1, LEN)

    def join(self, split, kinds):
        if self.plain:
            return split
        nx, ny, deep = self.nx, self.ny, self.nz // 2
        cut = split.reshape(2, nx, deep, kinds, ny, HEAD_DIM // ny, LEN)
        first = cut[0].transpose(3, 0, 1, 2, 4, 5).reshape(-1, LEN)
        second = cut[1].transpose(0, 3, 1, 2, 4, 5).reshape(-1, LEN)
        return jnp.concatenate([first, second], 0)

    def call(self, kernel, kinds, tables, arrays, outs, scratch, flops):
        need, bases, spans = tables
        layouts = [Rows(self.nx, self.ny if self.plain else 1, self.nz, k) for k in kinds + (1,)]

        def by_half(shape):
            rest = (0,) * (len(shape) - 1)
            return pl.BlockSpec((shape[0] // 2,) + tuple(shape[1:]), lambda i, *_: (i,) + rest)

        return pl.pallas_call(
            functools.partial(kernel, self.index, layouts, self.chunk),
            out_shape=outs,
            grid_spec=pltpu.PrefetchScalarGridSpec(
                num_scalar_prefetch=2,
                grid=(2,),
                in_specs=[pl.BlockSpec((2, LEN), lambda i, *_: (0, 0))] + [by_half(a.shape) for a in arrays],
                out_specs=[by_half(o.shape) for o in outs],
                scratch_shapes=scratch,
            ),
            compiler_params=pltpu.CompilerParams(vmem_limit_bytes=30 * 2**20),
            cost_estimate=pl.CostEstimate(flops=flops, bytes_accessed=8 * 2**20, transcendentals=4 * 2**20),
        )(need, bases, spans, *arrays)

    def attend(self, tables, sources, kinds):
        count = len(self.index)
        split = [self.split(s, k) for s, k in zip(sources, kinds)]
        wide = (count, HEAD_DIM, LEN)
        mixed, lse = self.call(
            attend_kernel,
            kinds,
            tables,
            split,
            [
                jax.ShapeDtypeStruct((2 * count * HEAD_DIM, LEN), BF),
                jax.ShapeDtypeStruct((2, count, 1, LEN), F32),
            ],
            [
                pltpu.VMEM(wide, BF),
                pltpu.VMEM((count, LEN, HEAD_DIM), BF),
                pltpu.VMEM(wide, BF),
                pltpu.VMEM((count, 1, BLOCK), F32),
                pltpu.VMEM((count, 1, BLOCK), F32),
                pltpu.VMEM((count, HEAD_DIM, BLOCK), F32),
            ],
            40 * 10**9,
        )
        return self.join(mixed, 1), lse

    def attend_back(self, tables, sources, kinds, mixed, grad, lse):
        count = len(self.index)
        split = [self.split(s, k) for s, k in zip(sources, kinds)]
        wide, tall = (count, HEAD_DIM, LEN), (count, LEN, HEAD_DIM)
        grads = self.call(
            attend_back_kernel,
            kinds,
            tables,
            split + [self.split(mixed, 1), self.split(grad, 1), lse],
            [jax.ShapeDtypeStruct(s.shape, BF) for s in split],
            [
                pltpu.VMEM(wide, BF),
                pltpu.VMEM(tall, BF),
                pltpu.VMEM(wide, BF),
                pltpu.VMEM(tall, BF),
                pltpu.VMEM(wide, BF),
                pltpu.VMEM((count, 1, LEN), F32),
                pltpu.VMEM(wide, F32),
                pltpu.VMEM(wide, F32),
                pltpu.VMEM(wide, F32),
            ],
            46 * 10**9,
        )
        return [self.join(g, k) for g, k in zip(grads, kinds)]


def body(
    inputs,
    memory,
    cotangent,
    tgt_lengths,
    src_ids,
    gain_one,
    w_query,
    w_key,
    w_value,
    w_out,
    gain_two,
    w_cross_query,
    w_mem_key,
    w_mem_value,
    w_cross_out,
    gain_three,
    w_up,
    w_down,
):
    nx, ny, nz = (lax.axis_size(a) for a in ("batch", "yy", "head"))
    ix, iy, core, iz = (lax.axis_index(a) for a in ("batch", "yy", "core", "head"))
    rows = inputs.shape[0]
    nxy, place = nx * ny, ix * ny + iy
    chunk = LEN // (2 * ny)

    def part(matrix):
        deep = matrix.shape[0] // 2 // nxy
        return lax.dynamic_slice_in_dim(matrix, (core * nxy + place) * deep, deep, 0)

    def column_parts(*matrices):
        parts = []
        for matrix in matrices:
            wide = matrix.shape[1] // 2
            turned = lax.dynamic_slice_in_dim(matrix, core * wide, wide, 1).T
            parts.append(lax.dynamic_slice_in_dim(turned, place * (wide // nxy), wide // nxy, 0))
        return jnp.concatenate(parts, 0)

    row = iy * nz + iz
    lengths = lax.dynamic_index_in_dim(tgt_lengths, row, 0, keepdims=False)
    source_ids = lax.dynamic_index_in_dim(src_ids, row, 0, keepdims=False)
    index = jnp.arange(LEN, dtype=jnp.int32)
    within = index % (LEN // 2)
    turn = jnp.where(index < LEN // 2, core, 1 - core)
    positions = (2 * (within // chunk) + turn) * chunk + within % chunk
    ends = jnp.cumsum(lengths)
    starts = ends - lengths
    reached = positions[:, None] >= starts[None, :]
    target_ids = jnp.sum(reached.astype(jnp.int32), -1) - 1
    self_start = jnp.max(jnp.where(reached, starts[None, :], 0), -1)
    kinds = jnp.arange(lengths.shape[0], dtype=jnp.int32)
    source_start = jnp.sum((source_ids[None, :] < kinds[:, None]).astype(jnp.int32), -1)
    source_end = jnp.sum((source_ids[None, :] <= kinds[:, None]).astype(jnp.int32), -1) - 1
    mine = target_ids[:, None] == kinds[None, :]
    cross_start = jnp.sum(jnp.where(mine, source_start[None, :], 0), -1)
    cross_end = jnp.sum(jnp.where(mine, source_end[None, :], 0), -1)
    block_positions = positions.reshape(BLOCKS, BLOCK)
    lowest, highest = jnp.min(block_positions, 1), jnp.max(block_positions, 1)

    def tables_of(start, end):
        least = jnp.min(start.reshape(BLOCKS, BLOCK), 1)
        most = jnp.max(end.reshape(BLOCKS, BLOCK), 1)
        some = (least[:, None] <= highest[None, :]) & (most[:, None] >= lowest[None, :])
        last, first = jnp.max(start.reshape(BLOCKS, BLOCK), 1), jnp.min(end.reshape(BLOCKS, BLOCK), 1)
        whole = (last[:, None] <= lowest[None, :]) & (first[:, None] >= highest[None, :])
        need = jnp.where(whole, 2, some.astype(jnp.int32))
        return need.reshape(-1), lowest, jnp.stack([start, end - start], 0)

    self_tables = tables_of(self_start, positions)
    cross_tables = tables_of(cross_start, cross_end)
    heads = Heads(nx, ny, nz, chunk)

    residual = to_row(inputs).astype(F32)
    self_weights = Gather([column_parts(w_query, w_key, w_value)])
    residual = to_row(tied(inputs, self_weights.got))
    self_weights.two()
    residual = meet(residual, self_weights)
    self_weights.three()
    cross_weights = Gather(
        [part(w_out), column_parts(w_mem_key, w_mem_value), column_parts(w_cross_query), part(w_cross_out)],
        residual,
    )
    (normed_one,) = normalize([tied(residual, self_weights.mine, cross_weights.mine)], gain_one)
    normed_one = both(normed_one)
    normed_one = meet(normed_one, self_weights)
    (w_self,) = self_weights.result()
    qkv = dot(w_self, normed_one, 1, 1).astype(BF)
    qkv = meet(qkv, cross_weights)
    cross_weights.two()
    up_weights = Gather([column_parts(w_up)], cross_weights.mine)
    source_own = to_row(tied(memory, up_weights.mine))
    qkv = meet(qkv, cross_weights)
    cross_weights.three()
    qkv = tied(qkv, cross_weights.mine)
    self_mixed, self_lse = heads.attend(self_tables, (qkv,), (3,))
    self_mixed, source_own = meet((self_mixed, source_own), cross_weights, up_weights)
    down_weights = Gather([part(w_down)], up_weights.got)
    up_weights.two()
    self_mixed = tied(self_mixed, up_weights.mine, down_weights.mine)
    w_o, w_mem, w_cq, w_co = cross_weights.result()
    normed_two, after_self = normalize([residual, *own_parts(self_mixed, w_o)], gain_two)
    normed_two = meet(normed_two, up_weights)
    up_weights.three()
    normed_two, source_own = tied((normed_two, source_own), up_weights.mine)
    source = both(source_own)
    mkv = dot(w_mem, source, 1, 1).astype(BF)
    normed_two = both(normed_two)
    cq = dot(w_cq, normed_two, 1, 1).astype(BF)
    cq, mkv = meet((cq, mkv), down_weights)
    down_weights.two()
    cq = tied(cq, down_weights.mine)
    cot_own = to_row(tied(cotangent, down_weights.mine))
    cross_mixed, cross_lse = heads.attend(cross_tables, (cq, mkv), (1, 2))
    cross_mixed, cot_own = meet((cross_mixed, cot_own), up_weights, down_weights)
    down_weights.three()
    cross_mixed = tied(cross_mixed, down_weights.mine)
    cot = both(cot_own)
    normed_three, after_cross = normalize([after_self, *own_parts(cross_mixed, w_co)], gain_three)
    normed_three = both(normed_three)
    (w_u,) = up_weights.result()

    def weight_grad(transposed, tokens):
        return dot(transposed, tokens, 1, 0).astype(BF)

    hidden_pre = dot(w_u, normed_three, 1, 1)
    squared = hidden_pre * hidden_pre
    bent = jnp.tanh(GELU_A * hidden_pre * (1.0 + GELU_B * squared))
    gate = 0.5 + 0.5 * bent
    slope = gate + (0.5 * GELU_A) * hidden_pre * (1.0 - bent * bent) * (1.0 + 3.0 * GELU_B * squared)
    hidden_act, slope = lax.optimization_barrier(((hidden_pre * gate).astype(BF), slope.astype(BF)))
    down_sum = Sum([weight_grad(hidden_act, cot)])
    hidden_act = meet(tied(hidden_act, down_sum.mine), down_weights)
    (w_d,) = down_weights.result()
    output = (after_cross + own_sum(hidden_act, w_d)).astype(BF)
    output = from_row(output, rows)

    grad_pre = (slope.astype(F32) * dot(w_d, cot, 1, 1)).astype(BF)
    grad_pre = meet(grad_pre, down_sum)
    down_sum.two()
    third_back = own_parts(tied(grad_pre, down_sum.mine), w_u)
    grad_after_cross, cross_grad, grad_gain_three = normalize_back(after_cross, gain_three, third_back, cot_own)

    cross_grad = both(cross_grad)
    up_sum = Sum([weight_grad(tied(grad_pre, down_sum.mine), normed_three)])
    grad_cross_mixed = dot(w_co, cross_grad, 1, 1).astype(BF)
    grad_cross_mixed = meet(grad_cross_mixed, down_sum)
    down_sum.three()
    grad_cross_mixed = tied(grad_cross_mixed, up_sum.mine, down_sum.mine)
    gcq, gmkv = heads.attend_back(
        cross_tables, (cq, mkv), (1, 2), cross_mixed, grad_cross_mixed, cross_lse
    )
    gcq, gmkv, output = meet((gcq, gmkv, output), up_sum, down_sum)
    up_sum.two()
    down_total = down_sum.result()
    gcq, gmkv = tied((gcq, gmkv), up_sum.mine)
    grad_after_self, self_grad, grad_gain_two = normalize_back(
        after_self, gain_two, own_parts(gcq, w_cq), grad_after_cross
    )
    self_grad = meet(self_grad, up_sum)
    up_sum.three()
    self_grad = both(self_grad)
    g_co = weight_grad(cross_mixed, cross_grad)
    g_cq = weight_grad(gcq, normed_two)
    g_mem = weight_grad(gmkv, source)
    g_o = weight_grad(self_mixed, self_grad)
    cross_sum = Sum([g_co, g_cq, g_mem])
    memory_back = own_sum(gmkv, w_mem).astype(BF)
    grad_self_mixed = dot(w_o, self_grad, 1, 1).astype(BF)
    grad_self_mixed, memory_back, g_o, down_total = meet(
        (grad_self_mixed, memory_back, g_o, down_total), cross_sum
    )
    down_all = gathered(down_total)
    cross_sum.two()
    grad_self_mixed = tied(grad_self_mixed, up_sum.mine, cross_sum.mine)
    grad_memory = from_row(memory_back, rows)
    (gqkv,) = heads.attend_back(self_tables, (qkv,), (3,), self_mixed, grad_self_mixed, self_lse)
    gqkv = meet(gqkv, cross_sum, up_sum)
    g_self = weight_grad(gqkv, normed_one)
    gqkv, g_self, cross_sum.got = lax.optimization_barrier((gqkv, g_self, cross_sum.got))
    self_sum = Sum([g_o, g_self])
    cross_sum.three()
    first_back, grad_memory, up_total = meet((own_parts(gqkv, w_self), grad_memory, up_sum.result()), self_sum)
    self_sum.two()
    up_all = gathered(up_total)
    _, grad_inputs, grad_gain_one = normalize_back(residual, gain_one, first_back, grad_after_self)
    grad_inputs, cross_sum.got = lax.optimization_barrier((grad_inputs, cross_sum.got))
    grad_inputs = from_row(grad_inputs, rows).astype(F32)
    gains = jnp.stack([grad_gain_one, grad_gain_two, grad_gain_three])
    for axis in ("core", "yy", "batch"):
        gains = total_of(gains, axis)
    cross_total = meet(cross_sum.result(), self_sum)
    self_sum.three()

    deep = w_query.shape[1] // 2 // nxy
    far = w_up.shape[1] // 2 // nxy
    (grad_down,) = unfold(down_all, [(far, False)])
    (grad_up,) = unfold(up_all, [(far, True)])
    cross_grads = unfold(gathered(cross_total), [(deep, False), (deep, True), (deep, True), (deep, True)])
    grad_memory = grad_memory.astype(F32)
    self_sum.got, grad_down, grad_memory, gains = lax.optimization_barrier(
        (self_sum.got, grad_down, grad_memory, gains)
    )
    gains = total_of(gains, "head")
    self_all, grad_up, (grad_inputs, gains), cross_grads = replicate(
        self_sum.result(), grad_up, (grad_inputs, gains), cross_grads
    )
    grad_co, grad_cq, grad_mk, grad_mv = cross_grads
    grad_o, grad_q, grad_k, grad_v = unfold(
        self_all, [(deep, False), (deep, True), (deep, True), (deep, True)]
    )
    return (
        output,
        grad_inputs,
        grad_memory,
        gains[0],
        grad_q,
        grad_k,
        grad_v,
        grad_o,
        gains[1],
        grad_cq,
        grad_mk,
        grad_mv,
        grad_co,
        gains[2],
        grad_up,
        grad_down,
    )


def solution(mesh):
    nb, ns, nh = (mesh.shape[a] for a in ("batch", "seq", "head"))
    fine = Mesh(mesh.devices.reshape(nb, ns // 2, 2, nh), ("batch", "yy", "core", "head"))
    tokens = P("batch", ("yy", "core", "head"), None)
    ids = P("batch", None)
    wide, tall = P(None, "head"), P("head", None)
    return jax.shard_map(
        body,
        mesh=fine,
        in_specs=(
            tokens, tokens, tokens, ids, ids,
            P(), wide, wide, wide, tall,
            P(), wide, wide, wide, tall,
            P(), wide, tall,
        ),
        out_specs=(
            tokens, tokens, tokens,
            P(), wide, wide, wide, tall,
            P(), wide, wide, wide, tall,
            P(), wide, tall,
        ),
        check_vma=False,
    )
```

```python
import functools

import jax
import jax.numpy as jnp
from jax import lax
from jax.experimental import pallas as pl
from jax.experimental.pallas import tpu as pltpu
from jax.sharding import Mesh
from jax.sharding import PartitionSpec as P

HEAD_DIM = 64
LEN = 1024
BLOCK = 256
BLOCKS = LEN // BLOCK
EPSILON = 1e-05
MASKED = -1000000000.0
SCALE = HEAD_DIM**-0.5
GELU_A = 0.7978845608028654
GELU_B = 0.044715
BF = jnp.bfloat16
F32 = jnp.float32


def dot(left, right, left_dim, right_dim):
    return lax.dot_general(
        left, right, (((left_dim,), (right_dim,)), ((), ())), preferred_element_type=F32
    )


STEP = 128


def centred(activity):
    shifted = activity - jnp.mean(activity, -1, keepdims=True)
    return shifted, lax.rsqrt(jnp.mean(shifted * shifted, -1, keepdims=True) + EPSILON)


def norm_kernel(terms, gain_ref, *refs):
    activity = refs[0][...].astype(F32)
    for ref in refs[1:terms]:
        activity = activity + ref[...].astype(F32)
    shifted, rate = centred(activity)
    refs[terms][...] = (shifted * rate * gain_ref[...]).astype(BF)
    if terms > 1:
        refs[terms + 1][...] = activity


def norm_back_kernel(gain_ref, activity_ref, own_ref, other_ref, onward_ref, grad_ref, rounded_ref, gain_grad_ref):
    shifted, rate = centred(activity_ref[...].astype(F32))
    unit = shifted * rate
    arrived = own_ref[...] + other_ref[...].astype(F32)
    scaled = arrived * gain_ref[...]
    inner = scaled - jnp.mean(scaled, -1, keepdims=True)
    step = rate * (inner - unit * jnp.mean(scaled * unit, -1, keepdims=True))
    total = onward_ref[...].astype(F32) + step
    grad_ref[...] = total
    rounded_ref[...] = total.astype(BF)

    @pl.when(pl.program_id(0) == 0)
    def _():
        gain_grad_ref[...] = jnp.zeros(gain_grad_ref.shape, F32)

    gain_grad_ref[...] += jnp.sum(arrived * unit, 0, keepdims=True)


def by_rows(kernel, gain, arrays, outs, sums=0):
    tokens, width = arrays[0].shape
    tile, line = pl.BlockSpec((STEP, width), lambda i: (i, 0)), pl.BlockSpec((1, width), lambda i: (0, 0))
    return pl.pallas_call(
        kernel,
        out_shape=[jax.ShapeDtypeStruct((tokens, width), t) for t in outs]
        + [jax.ShapeDtypeStruct((1, width), F32)] * sums,
        grid=(tokens // STEP,),
        in_specs=[line] + [tile] * len(arrays),
        out_specs=[tile] * len(outs) + [line] * sums,
        compiler_params=pltpu.CompilerParams(vmem_limit_bytes=32 * 2**20),
        cost_estimate=pl.CostEstimate(flops=20 * tokens * width, bytes_accessed=8 * tokens * width, transcendentals=tokens),
    )(gain.reshape(1, width), *arrays)


def normalize(terms, gain):
    return by_rows(functools.partial(norm_kernel, len(terms)), gain, terms, [BF] + [F32] * (len(terms) > 1))


def normalize_back(activity, gain, arrived, onward):
    grad, rounded, gain_grad = by_rows(norm_back_kernel, gain, [activity, *arrived, onward], [F32, BF], 1)
    return grad, rounded, gain_grad[0]


def shift(piece, axis, step):
    count = lax.axis_size(axis)
    return lax.ppermute(piece, axis, [(i, (i + step) % count) for i in range(count)])


def core_swap(piece):
    return shift(piece, "core", 1)


def both(own):
    return jnp.concatenate([own, core_swap(own)], 0)


def own_parts(transposed, matrix):
    half = transposed.shape[1] // 2
    other = core_swap(dot(transposed[:, half:], matrix, 0, 0).astype(BF))
    return [dot(transposed[:, :half], matrix, 0, 0), other]


def own_sum(transposed, matrix):
    own, other = own_parts(transposed, matrix)
    return own + other.astype(F32)


def to_row(tokens):
    rows, span, width = tokens.shape
    moved = lax.all_to_all(tokens, ("yy", "head"), 0, 0, tiled=True)
    return moved.reshape(rows * span, width)


def from_row(own, rows):
    parts = own.reshape(rows, own.shape[0] // rows, own.shape[1])
    return lax.all_to_all(parts, ("yy", "head"), 0, 0, tiled=True)


def tied(values, *others):
    return lax.optimization_barrier((values, others))[0]


def meet(values, *moves):
    values, got = lax.optimization_barrier((values, [m.got for m in moves]))
    for move, pieces in zip(moves, got):
        move.got = pieces
    return values


def others_of(axis):
    return range(1, lax.axis_size(axis))


class Gather:
    def __init__(self, parts, *others):
        self.deep = [p.shape[0] for p in parts]
        self.mine = tied(jnp.concatenate(parts, 0), *others)
        self.got = [shift(self.mine, "head", k) for k in others_of("head")]

    def send(self, first, second, one, two):
        self.mine = first, second
        self.got = [shift(first, one, k) for k in others_of(one)] + [shift(second, two, k) for k in others_of(two)]
        self.cut = len(others_of(one))

    def two(self):
        along = jnp.stack([self.mine] + self.got, 0)
        half = along.shape[0] // 2
        self.send(along[:half], along[half:], "batch", "yy")

    def slots(self):
        first, second = self.mine
        return [first] + self.got[: self.cut], [second] + self.got[self.cut :]

    def three(self):
        first, second = self.slots()
        self.send(jnp.stack(first, 0), jnp.stack(second, 0), "yy", "batch")

    def result(self):
        first, second = self.slots()
        made, at = [], 0
        for deep in self.deep:
            cut = [slot[..., at : at + deep, :].reshape(-1, slot.shape[-1]) for slot in first + second]
            made.append(jnp.concatenate(cut, 0))
            at += deep
        return made


class Sum:
    def __init__(self, grads):
        nx, ny, self.nz = (lax.axis_size(a) for a in ("batch", "yy", "head"))
        width = grads[0].shape[1]
        half = [g.shape[0] // 2 for g in grads]
        first = [g[:n].reshape(ny, nx, self.nz // 2, -1, width) for g, n in zip(grads, half)]
        second = [g[n:].reshape(nx, ny, self.nz // 2, -1, width) for g, n in zip(grads, half)]
        self.send(first, second, "yy", "batch")

    def send(self, first, second, one, two):
        def slot(grads, k):
            return jnp.concatenate([g[k] for g in grads], -2)

        self.mine = slot(first, 0), slot(second, 0)
        self.got = [shift(slot(first, k), one, -k) for k in others_of(one)]
        self.cut = len(self.got)
        self.got = self.got + [shift(slot(second, k), two, -k) for k in others_of(two)]

    def add(self, mine, got):
        total = mine.astype(F32)
        for piece in got:
            total = total + piece.astype(F32)
        return total.astype(BF)

    def sums(self):
        first, second = self.mine
        return self.add(first, self.got[: self.cut]), self.add(second, self.got[self.cut :])

    def two(self):
        first, second = self.sums()
        self.send([first], [second], "batch", "yy")

    def three(self):
        first, second = self.sums()
        slots = [first[k] if k < self.nz // 2 else second[k - self.nz // 2] for k in range(self.nz)]
        self.mine, self.got = slots[0], [shift(slots[k], "head", -k) for k in range(1, self.nz)]

    def result(self):
        return self.add(self.mine, self.got)


def in_place(piece, axis, beside):
    if lax.axis_size(axis) != 2:
        return lax.all_gather(piece, axis, axis=0, tiled=False), beside
    other, beside = lax.optimization_barrier((shift(piece, axis, 1), beside))
    low = lax.axis_index(axis) == 0
    return jnp.stack([jnp.where(low, piece, other), jnp.where(low, other, piece)], 0), beside


def gathered(piece):
    sizes = tuple(lax.axis_size(a) for a in ("core", "batch", "yy"))
    return lax.all_gather(piece, ("core", "batch", "yy"), axis=0, tiled=True).reshape(sizes + piece.shape)


def replicate(piece, *beside):
    done = []
    for axis, values in zip(("yy", "batch", "core"), beside):
        piece, values = in_place(piece, axis, values)
        done.append(values)
    return piece, *done


def unfold_kernel(kinds, source_ref, *outs):
    at = 0
    for (size, turned), out in zip(kinds, outs):
        piece = source_ref[..., at : at + size, :].reshape(-1, source_ref.shape[-1]).astype(F32)
        out[...] = piece.T if turned else piece
        at += size


def unfold(whole, kinds):
    width = whole.shape[-1]
    count = whole.shape[0] * whole.shape[1] * whole.shape[2]
    if any(size % 16 for size, _ in kinds):
        made, at = [], 0
        for size, turned in kinds:
            piece = whole[..., at : at + size, :].reshape(-1, width)
            made.append((piece.T if turned else piece).astype(F32))
            at += size
        return made
    step = 256
    return pl.pallas_call(
        functools.partial(unfold_kernel, kinds),
        out_shape=[
            jax.ShapeDtypeStruct((width, count * size) if turned else (count * size, width), F32) for size, turned in kinds
        ],
        grid=(width // step,),
        in_specs=[pl.BlockSpec(whole.shape[:4] + (step,), lambda i: (0, 0, 0, 0, i))],
        out_specs=[
            pl.BlockSpec((step, count * size), lambda i: (i, 0))
            if turned
            else pl.BlockSpec((count * size, step), lambda i: (0, i))
            for size, turned in kinds
        ],
        compiler_params=pltpu.CompilerParams(vmem_limit_bytes=32 * 2**20),
    )(whole)


def total_of(value, axis):
    count = lax.axis_size(axis)
    step = 1
    while step < count:
        value = value + lax.ppermute(value, axis, [(i, i ^ step) for i in range(count)])
        step *= 2
    return value


class Rows:
    def __init__(self, nx, ny, nz, kinds):
        self.nx, self.ny, self.depth, self.kinds = nx, ny, nz // 2, kinds
        self.size = HEAD_DIM // ny

    def starts(self, half, index, kind):
        x, z = index
        slots = [y * self.nx + x if half == 0 else x * self.ny + y for y in range(self.ny)]
        return [((slot * self.depth + z) * self.kinds + kind) * self.size for slot in slots]

    def read(self, ref, half, index, kind):
        return jnp.concatenate([ref[at : at + self.size, :] for at in self.starts(half, index, kind)], 0)

    def write(self, ref, half, index, kind, value):
        for k, at in enumerate(self.starts(half, index, kind)):
            ref[at : at + self.size, :] = value[k * self.size : (k + 1) * self.size]


def allowed_block(span_ref, base, columns, chunk):
    ahead = lax.broadcasted_iota(jnp.int32, (BLOCK, BLOCK), 0)
    if chunk < BLOCK:
        ahead = ahead + ahead // chunk * chunk
    away = ahead + (base - span_ref[0:1, columns])
    return (away >= 0) & (away <= span_ref[1:2, columns])


def span_of(index):
    return slice(index * BLOCK, (index + 1) * BLOCK)


def per_block(need_ref, base_ref, span_ref, columns, chunk, i, j, work):
    need = need_ref[i * BLOCKS + j]

    @pl.when(need == 1)
    def _():
        allowed = allowed_block(span_ref, base_ref[j], columns, chunk)
        work(lambda scores: jnp.where(allowed, scores, MASKED))

    @pl.when(need == 2)
    def _():
        work(lambda scores: scores)


def attend_kernel(heads, layouts, chunk, need_ref, base_ref, span_ref, *refs):
    *layouts, single = layouts
    count = len(layouts)
    mixed_ref, lse_ref, q_s, k_s, v_s, top_s, sum_s, acc_s = refs[count:]
    where = [(source, lay, kind) for source, lay in zip(refs[:count], layouts) for kind in range(lay.kinds)]
    every = range(len(heads))

    def load(half):
        for h, index in enumerate(heads):
            q, k, v = (lay.read(source, half, index, kind) for source, lay, kind in where)
            q_s[h] = (q.astype(F32) * SCALE).astype(BF)
            k_s[h] = k.T
            v_s[h] = v

    half_now = pl.program_id(0)
    for half in range(2):
        pl.when(half_now == half)(functools.partial(load, half))

    for i in range(BLOCKS):
        columns = span_of(i)
        top_s[...] = jnp.full(top_s.shape, -3e38, F32)
        sum_s[...] = jnp.zeros(sum_s.shape, F32)
        acc_s[...] = jnp.zeros(acc_s.shape, F32)
        for j in range(BLOCKS):
            keys = span_of(j)

            def work(mask, keys=keys, columns=columns):
                scores = [mask(dot(k_s[h, keys, :], q_s[h, :, columns], 1, 0)) for h in every]
                tops = [jnp.maximum(top_s[h], jnp.max(scores[h], 0, keepdims=True)) for h in every]
                weights = [jnp.exp(scores[h] - tops[h]) for h in every]
                fades = [jnp.exp(top_s[h] - tops[h]) for h in every]
                mixed = [dot(v_s[h, :, keys], weights[h].astype(BF), 1, 0) for h in every]
                for h in every:
                    top_s[h] = tops[h]
                    sum_s[h] = sum_s[h] * fades[h] + jnp.sum(weights[h], 0, keepdims=True)
                    acc_s[h] = acc_s[h] * fades[h] + mixed[h]

            per_block(need_ref, base_ref, span_ref, columns, chunk, i, j, work)

        for h in every:
            lse_ref[0, h, :, columns] = top_s[h] + jnp.log(sum_s[h])
            q_s[h, :, columns] = (acc_s[h] / sum_s[h]).astype(BF)

    def store(half):
        for h, index in enumerate(heads):
            single.write(mixed_ref, half, index, 0, q_s[h])

    for half in range(2):
        pl.when(half_now == half)(functools.partial(store, half))


def attend_back_kernel(heads, layouts, chunk, need_ref, base_ref, span_ref, *refs):
    *layouts, single = layouts
    count = len(layouts)
    mixed_ref, grad_ref, lse_ref = refs[count : count + 3]
    q_s, k_s, kt_s, v_s, g_s, inner_s, dq_s, dk_s, dv_s = refs[2 * count + 3 :]
    where = [(source, lay, kind) for source, lay in zip(refs[:count], layouts) for kind in range(lay.kinds)]
    outs = refs[count + 3 : 2 * count + 3]
    into = [(out, lay, kind) for out, lay in zip(outs, layouts) for kind in range(lay.kinds)]
    every = range(len(heads))

    def load(half):
        for h, index in enumerate(heads):
            q, k, v = (lay.read(source, half, index, kind) for source, lay, kind in where)
            q_s[h] = (q.astype(F32) * SCALE).astype(BF)
            kt_s[h] = k
            k_s[h] = k.T
            v_s[h] = v.T
            grad = single.read(grad_ref, half, index, 0)
            g_s[h] = grad
            mixed = single.read(mixed_ref, half, index, 0)
            inner_s[h] = jnp.sum(grad.astype(F32) * mixed.astype(F32), 0, keepdims=True)

    half_now = pl.program_id(0)
    for half in range(2):
        pl.when(half_now == half)(functools.partial(load, half))

    for acc in (dq_s, dk_s, dv_s):
        acc[...] = jnp.zeros(acc.shape, F32)

    for i in range(BLOCKS):
        columns = span_of(i)
        for j in range(BLOCKS):
            keys = span_of(j)

            def work(mask, keys=keys, columns=columns):
                scores = [mask(dot(k_s[h, keys, :], q_s[h, :, columns], 1, 0)) for h in every]
                steep = [dot(v_s[h, keys, :], g_s[h, :, columns], 1, 0) for h in every]
                chances = [jnp.exp(scores[h] - lse_ref[0, h, :, columns]) for h in every]
                back = [(chances[h] * (steep[h] - inner_s[h, :, columns])).astype(BF) for h in every]
                for h in every:
                    dv_s[h, :, keys] += dot(g_s[h, :, columns], chances[h].astype(BF), 1, 1)
                for h in every:
                    dk_s[h, :, keys] += dot(q_s[h, :, columns], back[h], 1, 1)
                for h in every:
                    dq_s[h, :, columns] += dot(kt_s[h, :, keys], back[h], 1, 0)

            per_block(need_ref, base_ref, span_ref, columns, chunk, i, j, work)

    def store(half):
        for h, index in enumerate(heads):
            made = (dq_s[h] * SCALE, dk_s[h], dv_s[h])
            for (out, lay, kind), value in zip(into, made):
                lay.write(out, half, index, kind, value.astype(BF))

    for half in range(2):
        pl.when(half_now == half)(functools.partial(store, half))


class Heads:
    def __init__(self, nx, ny, nz, chunk):
        self.nx, self.ny, self.nz, self.chunk = nx, ny, nz, chunk
        self.index = [(x, z) for x in range(nx) for z in range(nz // 2)]
        self.plain = (HEAD_DIM // ny) % 16 == 0

    def split(self, matrix, kinds):
        if self.plain:
            return matrix
        nx, ny, deep = self.nx, self.ny, self.nz // 2
        half, rows = matrix.shape[0] // 2, HEAD_DIM // ny
        first = matrix[:half].reshape(ny, nx, deep, kinds, rows, LEN).transpose(1, 2, 3, 0, 4, 5)
        second = matrix[half:].reshape(nx, ny, deep, kinds, rows, LEN).transpose(0, 2, 3, 1, 4, 5)
        return jnp.stack([first, second], 0).reshape(-1, LEN)

    def join(self, split, kinds):
        if self.plain:
            return split
        nx, ny, deep = self.nx, self.ny, self.nz // 2
        cut = split.reshape(2, nx, deep, kinds, ny, HEAD_DIM // ny, LEN)
        first = cut[0].transpose(3, 0, 1, 2, 4, 5).reshape(-1, LEN)
        second = cut[1].transpose(0, 3, 1, 2, 4, 5).reshape(-1, LEN)
        return jnp.concatenate([first, second], 0)

    def call(self, kernel, kinds, tables, arrays, outs, scratch, flops):
        need, bases, spans = tables
        layouts = [Rows(self.nx, self.ny if self.plain else 1, self.nz, k) for k in kinds + (1,)]

        def by_half(shape):
            rest = (0,) * (len(shape) - 1)
            return pl.BlockSpec((shape[0] // 2,) + tuple(shape[1:]), lambda i, *_: (i,) + rest)

        return pl.pallas_call(
            functools.partial(kernel, self.index, layouts, self.chunk),
            out_shape=outs,
            grid_spec=pltpu.PrefetchScalarGridSpec(
                num_scalar_prefetch=2,
                grid=(2,),
                in_specs=[pl.BlockSpec((2, LEN), lambda i, *_: (0, 0))] + [by_half(a.shape) for a in arrays],
                out_specs=[by_half(o.shape) for o in outs],
                scratch_shapes=scratch,
            ),
            compiler_params=pltpu.CompilerParams(vmem_limit_bytes=30 * 2**20),
            cost_estimate=pl.CostEstimate(flops=flops, bytes_accessed=8 * 2**20, transcendentals=4 * 2**20),
        )(need, bases, spans, *arrays)

    def attend(self, tables, sources, kinds):
        count = len(self.index)
        split = [self.split(s, k) for s, k in zip(sources, kinds)]
        wide = (count, HEAD_DIM, LEN)
        mixed, lse = self.call(
            attend_kernel,
            kinds,
            tables,
            split,
            [
                jax.ShapeDtypeStruct((2 * count * HEAD_DIM, LEN), BF),
                jax.ShapeDtypeStruct((2, count, 1, LEN), F32),
            ],
            [
                pltpu.VMEM(wide, BF),
                pltpu.VMEM((count, LEN, HEAD_DIM), BF),
                pltpu.VMEM(wide, BF),
                pltpu.VMEM((count, 1, BLOCK), F32),
                pltpu.VMEM((count, 1, BLOCK), F32),
                pltpu.VMEM((count, HEAD_DIM, BLOCK), F32),
            ],
            40 * 10**9,
        )
        return self.join(mixed, 1), lse

    def attend_back(self, tables, sources, kinds, mixed, grad, lse):
        count = len(self.index)
        split = [self.split(s, k) for s, k in zip(sources, kinds)]
        wide, tall = (count, HEAD_DIM, LEN), (count, LEN, HEAD_DIM)
        grads = self.call(
            attend_back_kernel,
            kinds,
            tables,
            split + [self.split(mixed, 1), self.split(grad, 1), lse],
            [jax.ShapeDtypeStruct(s.shape, BF) for s in split],
            [
                pltpu.VMEM(wide, BF),
                pltpu.VMEM(tall, BF),
                pltpu.VMEM(wide, BF),
                pltpu.VMEM(tall, BF),
                pltpu.VMEM(wide, BF),
                pltpu.VMEM((count, 1, LEN), F32),
                pltpu.VMEM(wide, F32),
                pltpu.VMEM(wide, F32),
                pltpu.VMEM(wide, F32),
            ],
            46 * 10**9,
        )
        return [self.join(g, k) for g, k in zip(grads, kinds)]


def body(
    inputs,
    memory,
    cotangent,
    tgt_lengths,
    src_ids,
    gain_one,
    w_query,
    w_key,
    w_value,
    w_out,
    gain_two,
    w_cross_query,
    w_mem_key,
    w_mem_value,
    w_cross_out,
    gain_three,
    w_up,
    w_down,
):
    nx, ny, nz = (lax.axis_size(a) for a in ("batch", "yy", "head"))
    ix, iy, core, iz = (lax.axis_index(a) for a in ("batch", "yy", "core", "head"))
    rows = inputs.shape[0]
    nxy, place = nx * ny, ix * ny + iy
    chunk = LEN // (2 * ny)

    def part(matrix):
        deep = matrix.shape[0] // 2 // nxy
        return lax.dynamic_slice_in_dim(matrix, (core * nxy + place) * deep, deep, 0)

    def column_parts(*matrices):
        parts = []
        for matrix in matrices:
            wide = matrix.shape[1] // 2
            turned = lax.dynamic_slice_in_dim(matrix, core * wide, wide, 1).T
            parts.append(lax.dynamic_slice_in_dim(turned, place * (wide // nxy), wide // nxy, 0))
        return jnp.concatenate(parts, 0)

    row = iy * nz + iz
    lengths = lax.dynamic_index_in_dim(tgt_lengths, row, 0, keepdims=False)
    source_ids = lax.dynamic_index_in_dim(src_ids, row, 0, keepdims=False)
    index = jnp.arange(LEN, dtype=jnp.int32)
    within = index % (LEN // 2)
    turn = jnp.where(index < LEN // 2, core, 1 - core)
    positions = (2 * (within // chunk) + turn) * chunk + within % chunk
    ends = jnp.cumsum(lengths)
    starts = ends - lengths
    reached = positions[:, None] >= starts[None, :]
    target_ids = jnp.sum(reached.astype(jnp.int32), -1) - 1
    self_start = jnp.max(jnp.where(reached, starts[None, :], 0), -1)
    kinds = jnp.arange(lengths.shape[0], dtype=jnp.int32)
    source_start = jnp.sum((source_ids[None, :] < kinds[:, None]).astype(jnp.int32), -1)
    source_end = jnp.sum((source_ids[None, :] <= kinds[:, None]).astype(jnp.int32), -1) - 1
    mine = target_ids[:, None] == kinds[None, :]
    cross_start = jnp.sum(jnp.where(mine, source_start[None, :], 0), -1)
    cross_end = jnp.sum(jnp.where(mine, source_end[None, :], 0), -1)
    block_positions = positions.reshape(BLOCKS, BLOCK)
    lowest, highest = jnp.min(block_positions, 1), jnp.max(block_positions, 1)

    def tables_of(start, end):
        least = jnp.min(start.reshape(BLOCKS, BLOCK), 1)
        most = jnp.max(end.reshape(BLOCKS, BLOCK), 1)
        some = (least[:, None] <= highest[None, :]) & (most[:, None] >= lowest[None, :])
        last, first = jnp.max(start.reshape(BLOCKS, BLOCK), 1), jnp.min(end.reshape(BLOCKS, BLOCK), 1)
        whole = (last[:, None] <= lowest[None, :]) & (first[:, None] >= highest[None, :])
        need = jnp.where(whole, 2, some.astype(jnp.int32))
        return need.reshape(-1), lowest, jnp.stack([start, end - start], 0)

    self_tables = tables_of(self_start, positions)
    cross_tables = tables_of(cross_start, cross_end)
    heads = Heads(nx, ny, nz, chunk)

    residual = to_row(inputs).astype(F32)
    self_weights = Gather([column_parts(w_query, w_key, w_value)])
    residual = to_row(tied(inputs, self_weights.got))
    self_weights.two()
    residual = meet(residual, self_weights)
    self_weights.three()
    cross_weights = Gather(
        [part(w_out), column_parts(w_mem_key, w_mem_value), column_parts(w_cross_query), part(w_cross_out)],
        residual,
    )
    (normed_one,) = normalize([tied(residual, self_weights.mine, cross_weights.mine)], gain_one)
    normed_one = both(normed_one)
    normed_one = meet(normed_one, self_weights)
    (w_self,) = self_weights.result()
    qkv = dot(w_self, normed_one, 1, 1).astype(BF)
    qkv = meet(qkv, cross_weights)
    cross_weights.two()
    up_weights = Gather([column_parts(w_up)], cross_weights.mine)
    source_own = to_row(tied(memory, up_weights.mine))
    qkv = meet(qkv, cross_weights)
    cross_weights.three()
    qkv = tied(qkv, cross_weights.mine)
    self_mixed, self_lse = heads.attend(self_tables, (qkv,), (3,))
    self_mixed, source_own = meet((self_mixed, source_own), cross_weights, up_weights)
    down_weights = Gather([part(w_down)], up_weights.got)
    up_weights.two()
    self_mixed = tied(self_mixed, up_weights.mine, down_weights.mine)
    w_o, w_mem, w_cq, w_co = cross_weights.result()
    normed_two, after_self = normalize([residual, *own_parts(self_mixed, w_o)], gain_two)
    normed_two, down_weights.got[0] = meet((normed_two, down_weights.got[0]), up_weights)
    up_weights.three()
    normed_two, source_own = tied((normed_two, source_own), up_weights.mine)
    source = both(source_own)
    mkv = dot(w_mem, source, 1, 1).astype(BF)
    normed_two = both(normed_two)
    cq = dot(w_cq, normed_two, 1, 1).astype(BF)
    cq, mkv = meet((cq, mkv), down_weights)
    down_weights.two()
    cq = tied(cq, down_weights.mine)
    cot_own = to_row(tied(cotangent, down_weights.mine))
    cross_mixed, cross_lse = heads.attend(cross_tables, (cq, mkv), (1, 2))
    cross_mixed, cot_own = meet((cross_mixed, cot_own), up_weights, down_weights)
    down_weights.three()
    cross_mixed = tied(cross_mixed, down_weights.mine)
    cot = both(cot_own)
    normed_three, after_cross = normalize([after_self, *own_parts(cross_mixed, w_co)], gain_three)
    normed_three = both(normed_three)
    (w_u,) = up_weights.result()

    def weight_grad(transposed, tokens):
        return dot(transposed, tokens, 1, 0).astype(BF)

    hidden_pre = dot(w_u, normed_three, 1, 1)
    squared = hidden_pre * hidden_pre
    bent = jnp.tanh(GELU_A * hidden_pre * (1.0 + GELU_B * squared))
    gate = 0.5 + 0.5 * bent
    slope = gate + (0.5 * GELU_A) * hidden_pre * (1.0 - bent * bent) * (1.0 + 3.0 * GELU_B * squared)
    hidden_act, slope = lax.optimization_barrier(((hidden_pre * gate).astype(BF), slope.astype(BF)))
    down_sum = Sum([weight_grad(hidden_act, cot)])
    hidden_act = meet(tied(hidden_act, down_sum.mine), down_weights)
    (w_d,) = down_weights.result()
    output = (after_cross + own_sum(hidden_act, w_d)).astype(BF)
    output = from_row(output, rows)

    grad_pre = (slope.astype(F32) * dot(w_d, cot, 1, 1)).astype(BF)
    grad_pre = meet(grad_pre, down_sum)
    down_sum.two()
    third_back = own_parts(tied(grad_pre, down_sum.mine), w_u)
    grad_after_cross, cross_grad, grad_gain_three = normalize_back(after_cross, gain_three, third_back, cot_own)

    cross_grad = both(cross_grad)
    up_sum = Sum([weight_grad(tied(grad_pre, down_sum.mine), normed_three)])
    grad_cross_mixed = dot(w_co, cross_grad, 1, 1).astype(BF)
    grad_cross_mixed = meet(grad_cross_mixed, down_sum)
    down_sum.three()
    grad_cross_mixed = tied(grad_cross_mixed, up_sum.mine, down_sum.mine)
    gcq, gmkv = heads.attend_back(
        cross_tables, (cq, mkv), (1, 2), cross_mixed, grad_cross_mixed, cross_lse
    )
    gcq, gmkv, output = meet((gcq, gmkv, output), up_sum, down_sum)
    up_sum.two()
    down_total = down_sum.result()
    gcq, gmkv = tied((gcq, gmkv), up_sum.mine)
    grad_after_self, self_grad, grad_gain_two = normalize_back(
        after_self, gain_two, own_parts(gcq, w_cq), grad_after_cross
    )
    self_grad = meet(self_grad, up_sum)
    up_sum.three()
    self_grad = both(self_grad)
    g_co = weight_grad(cross_mixed, cross_grad)
    g_cq = weight_grad(gcq, normed_two)
    g_mem = weight_grad(gmkv, source)
    g_o = weight_grad(self_mixed, self_grad)
    cross_sum = Sum([g_co, g_cq, g_mem])
    memory_back = own_sum(gmkv, w_mem).astype(BF)
    grad_self_mixed = dot(w_o, self_grad, 1, 1).astype(BF)
    grad_self_mixed, memory_back, g_o, down_total = meet(
        (grad_self_mixed, memory_back, g_o, down_total), cross_sum
    )
    down_all = gathered(down_total)
    cross_sum.two()
    grad_self_mixed = tied(grad_self_mixed, up_sum.mine, cross_sum.mine)
    grad_memory = from_row(memory_back, rows)
    (gqkv,) = heads.attend_back(self_tables, (qkv,), (3,), self_mixed, grad_self_mixed, self_lse)
    gqkv = meet(gqkv, cross_sum, up_sum)
    g_self = weight_grad(gqkv, normed_one)
    gqkv, g_self, cross_sum.got = lax.optimization_barrier((gqkv, g_self, cross_sum.got))
    self_sum = Sum([g_o, g_self])
    cross_sum.three()
    first_back, grad_memory, up_total = meet(
        (own_parts(gqkv, w_self), grad_memory, up_sum.result()), self_sum, cross_sum
    )
    self_sum.two()
    up_all = gathered(up_total)
    _, grad_inputs, grad_gain_one = normalize_back(residual, gain_one, first_back, grad_after_self)
    grad_inputs = from_row(grad_inputs, rows).astype(F32)
    gains = jnp.stack([grad_gain_one, grad_gain_two, grad_gain_three])
    for axis in ("core", "yy", "batch"):
        gains = total_of(gains, axis)
    cross_total = meet(cross_sum.result(), self_sum)
    self_sum.three()

    deep = w_query.shape[1] // 2 // nxy
    far = w_up.shape[1] // 2 // nxy
    (grad_down,) = unfold(down_all, [(far, False)])
    (grad_up,) = unfold(up_all, [(far, True)])
    cross_grads = unfold(gathered(cross_total), [(deep, False), (deep, True), (deep, True), (deep, True)])
    grad_memory = grad_memory.astype(F32)
    self_sum.got, grad_down, grad_memory, gains = lax.optimization_barrier(
        (self_sum.got, grad_down, grad_memory, gains)
    )
    gains = total_of(gains, "head")
    self_all, grad_up, (grad_inputs, gains), cross_grads = replicate(
        self_sum.result(), grad_up, (grad_inputs, gains), cross_grads
    )
    grad_co, grad_cq, grad_mk, grad_mv = cross_grads
    grad_o, grad_q, grad_k, grad_v = unfold(
        self_all, [(deep, False), (deep, True), (deep, True), (deep, True)]
    )
    return (
        output,
        grad_inputs,
        grad_memory,
        gains[0],
        grad_q,
        grad_k,
        grad_v,
        grad_o,
        gains[1],
        grad_cq,
        grad_mk,
        grad_mv,
        grad_co,
        gains[2],
        grad_up,
        grad_down,
    )


def solution(mesh):
    nb, ns, nh = (mesh.shape[a] for a in ("batch", "seq", "head"))
    fine = Mesh(mesh.devices.reshape(nb, ns // 2, 2, nh), ("batch", "yy", "core", "head"))
    tokens = P("batch", ("yy", "core", "head"), None)
    ids = P("batch", None)
    wide, tall = P(None, "head"), P("head", None)
    return jax.shard_map(
        body,
        mesh=fine,
        in_specs=(
            tokens, tokens, tokens, ids, ids,
            P(), wide, wide, wide, tall,
            P(), wide, wide, wide, tall,
            P(), wide, tall,
        ),
        out_specs=(
            tokens, tokens, tokens,
            P(), wide, wide, wide, tall,
            P(), wide, wide, wide, tall,
            P(), wide, tall,
        ),
        check_vma=False,
    )
```

```python
import functools

import jax
import jax.numpy as jnp
from jax import lax
from jax.experimental import pallas as pl
from jax.experimental.pallas import tpu as pltpu
from jax.sharding import Mesh
from jax.sharding import PartitionSpec as P

HEAD_DIM = 64
LEN = 1024
BLOCK = 256
BLOCKS = LEN // BLOCK
EPSILON = 1e-05
MASKED = -1000000000.0
SCALE = HEAD_DIM**-0.5
GELU_A = 0.7978845608028654
GELU_B = 0.044715
BF = jnp.bfloat16
F32 = jnp.float32


def dot(left, right, left_dim, right_dim):
    return lax.dot_general(
        left, right, (((left_dim,), (right_dim,)), ((), ())), preferred_element_type=F32
    )


STEP = 128


def centred(activity):
    shifted = activity - jnp.mean(activity, -1, keepdims=True)
    return shifted, lax.rsqrt(jnp.mean(shifted * shifted, -1, keepdims=True) + EPSILON)


def norm_kernel(terms, gain_ref, *refs):
    activity = refs[0][...].astype(F32)
    for ref in refs[1:terms]:
        activity = activity + ref[...].astype(F32)
    shifted, rate = centred(activity)
    refs[terms][...] = (shifted * rate * gain_ref[...]).astype(BF)
    if terms > 1:
        refs[terms + 1][...] = activity


def norm_back_kernel(gain_ref, activity_ref, own_ref, other_ref, onward_ref, grad_ref, rounded_ref, gain_grad_ref):
    shifted, rate = centred(activity_ref[...].astype(F32))
    unit = shifted * rate
    arrived = own_ref[...] + other_ref[...].astype(F32)
    scaled = arrived * gain_ref[...]
    inner = scaled - jnp.mean(scaled, -1, keepdims=True)
    step = rate * (inner - unit * jnp.mean(scaled * unit, -1, keepdims=True))
    total = onward_ref[...].astype(F32) + step
    grad_ref[...] = total
    rounded_ref[...] = total.astype(BF)

    @pl.when(pl.program_id(0) == 0)
    def _():
        gain_grad_ref[...] = jnp.zeros(gain_grad_ref.shape, F32)

    gain_grad_ref[...] += jnp.sum(arrived * unit, 0, keepdims=True)


def by_rows(kernel, gain, arrays, outs, sums=0):
    tokens, width = arrays[0].shape
    tile, line = pl.BlockSpec((STEP, width), lambda i: (i, 0)), pl.BlockSpec((1, width), lambda i: (0, 0))
    return pl.pallas_call(
        kernel,
        out_shape=[jax.ShapeDtypeStruct((tokens, width), t) for t in outs]
        + [jax.ShapeDtypeStruct((1, width), F32)] * sums,
        grid=(tokens // STEP,),
        in_specs=[line] + [tile] * len(arrays),
        out_specs=[tile] * len(outs) + [line] * sums,
        compiler_params=pltpu.CompilerParams(vmem_limit_bytes=32 * 2**20),
        cost_estimate=pl.CostEstimate(flops=20 * tokens * width, bytes_accessed=8 * tokens * width, transcendentals=tokens),
    )(gain.reshape(1, width), *arrays)


def normalize(terms, gain):
    return by_rows(functools.partial(norm_kernel, len(terms)), gain, terms, [BF] + [F32] * (len(terms) > 1))


def normalize_back(activity, gain, arrived, onward):
    grad, rounded, gain_grad = by_rows(norm_back_kernel, gain, [activity, *arrived, onward], [F32, BF], 1)
    return grad, rounded, gain_grad[0]


def shift(piece, axis, step):
    count = lax.axis_size(axis)
    return lax.ppermute(piece, axis, [(i, (i + step) % count) for i in range(count)])


def core_swap(piece):
    return shift(piece, "core", 1)


def both(own):
    return jnp.concatenate([own, core_swap(own)], 0)


def own_parts(transposed, matrix):
    half = transposed.shape[1] // 2
    other = core_swap(dot(transposed[:, half:], matrix, 0, 0).astype(BF))
    return [dot(transposed[:, :half], matrix, 0, 0), other]


def own_sum(transposed, matrix):
    own, other = own_parts(transposed, matrix)
    return own + other.astype(F32)


def to_row(tokens):
    rows, span, width = tokens.shape
    moved = lax.all_to_all(tokens, ("yy", "head"), 0, 0, tiled=True)
    return moved.reshape(rows * span, width)


def from_row(own, rows):
    parts = own.reshape(rows, own.shape[0] // rows, own.shape[1])
    return lax.all_to_all(parts, ("yy", "head"), 0, 0, tiled=True)


def tied(values, *others):
    return lax.optimization_barrier((values, others))[0]


def meet(values, *moves):
    values, got = lax.optimization_barrier((values, [m.got for m in moves]))
    for move, pieces in zip(moves, got):
        move.got = pieces
    return values


def others_of(axis):
    return range(1, lax.axis_size(axis))


class Gather:
    def __init__(self, parts, *others):
        self.deep = [p.shape[0] for p in parts]
        self.mine = tied(jnp.concatenate(parts, 0), *others)
        self.got = [shift(self.mine, "head", k) for k in others_of("head")]

    def send(self, first, second, one, two):
        self.mine = first, second
        self.got = [shift(first, one, k) for k in others_of(one)] + [shift(second, two, k) for k in others_of(two)]
        self.cut = len(others_of(one))

    def two(self):
        along = jnp.stack([self.mine] + self.got, 0)
        half = along.shape[0] // 2
        self.send(along[:half], along[half:], "batch", "yy")

    def slots(self):
        first, second = self.mine
        return [first] + self.got[: self.cut], [second] + self.got[self.cut :]

    def three(self):
        first, second = self.slots()
        self.send(jnp.stack(first, 0), jnp.stack(second, 0), "yy", "batch")

    def result(self):
        first, second = self.slots()
        made, at = [], 0
        for deep in self.deep:
            cut = [slot[..., at : at + deep, :].reshape(-1, slot.shape[-1]) for slot in first + second]
            made.append(jnp.concatenate(cut, 0))
            at += deep
        return made


class Sum:
    def __init__(self, grads):
        nx, ny, self.nz = (lax.axis_size(a) for a in ("batch", "yy", "head"))
        width = grads[0].shape[1]
        half = [g.shape[0] // 2 for g in grads]
        first = [g[:n].reshape(ny, nx, self.nz // 2, -1, width) for g, n in zip(grads, half)]
        second = [g[n:].reshape(nx, ny, self.nz // 2, -1, width) for g, n in zip(grads, half)]
        self.send(first, second, "yy", "batch")

    def send(self, first, second, one, two):
        def slot(grads, k):
            return jnp.concatenate([g[k] for g in grads], -2)

        self.mine = slot(first, 0), slot(second, 0)
        self.got = [shift(slot(first, k), one, -k) for k in others_of(one)]
        self.cut = len(self.got)
        self.got = self.got + [shift(slot(second, k), two, -k) for k in others_of(two)]

    def add(self, mine, got):
        total = mine.astype(F32)
        for piece in got:
            total = total + piece.astype(F32)
        return total.astype(BF)

    def sums(self):
        first, second = self.mine
        return self.add(first, self.got[: self.cut]), self.add(second, self.got[self.cut :])

    def two(self):
        first, second = self.sums()
        self.send([first], [second], "batch", "yy")

    def three(self):
        first, second = self.sums()
        slots = [first[k] if k < self.nz // 2 else second[k - self.nz // 2] for k in range(self.nz)]
        self.mine, self.got = slots[0], [shift(slots[k], "head", -k) for k in range(1, self.nz)]

    def result(self):
        return self.add(self.mine, self.got)


def in_place(piece, axis, beside):
    if lax.axis_size(axis) != 2:
        return lax.all_gather(piece, axis, axis=0, tiled=False), beside
    other, beside = lax.optimization_barrier((shift(piece, axis, 1), beside))
    low = lax.axis_index(axis) == 0
    return jnp.stack([jnp.where(low, piece, other), jnp.where(low, other, piece)], 0), beside


def gathered(piece):
    sizes = tuple(lax.axis_size(a) for a in ("core", "batch", "yy"))
    return lax.all_gather(piece, ("core", "batch", "yy"), axis=0, tiled=True).reshape(sizes + piece.shape)


def replicate(piece, *beside):
    done = []
    for axis, values in zip(("yy", "batch", "core"), beside):
        piece, values = in_place(piece, axis, values)
        done.append(values)
    return piece, *done


def unfold_kernel(kinds, source_ref, *outs):
    at = 0
    for (size, turned), out in zip(kinds, outs):
        piece = source_ref[..., at : at + size, :].reshape(-1, source_ref.shape[-1]).astype(F32)
        out[...] = piece.T if turned else piece
        at += size


def unfold(whole, kinds):
    width = whole.shape[-1]
    count = whole.shape[0] * whole.shape[1] * whole.shape[2]
    if any(size % 16 for size, _ in kinds):
        made, at = [], 0
        for size, turned in kinds:
            piece = whole[..., at : at + size, :].reshape(-1, width)
            made.append((piece.T if turned else piece).astype(F32))
            at += size
        return made
    step = 256
    return pl.pallas_call(
        functools.partial(unfold_kernel, kinds),
        out_shape=[
            jax.ShapeDtypeStruct((width, count * size) if turned else (count * size, width), F32) for size, turned in kinds
        ],
        grid=(width // step,),
        in_specs=[pl.BlockSpec(whole.shape[:4] + (step,), lambda i: (0, 0, 0, 0, i))],
        out_specs=[
            pl.BlockSpec((step, count * size), lambda i: (i, 0))
            if turned
            else pl.BlockSpec((count * size, step), lambda i: (0, i))
            for size, turned in kinds
        ],
        compiler_params=pltpu.CompilerParams(vmem_limit_bytes=32 * 2**20),
    )(whole)


def total_of(value, axis):
    count = lax.axis_size(axis)
    step = 1
    while step < count:
        value = value + lax.ppermute(value, axis, [(i, i ^ step) for i in range(count)])
        step *= 2
    return value


class Rows:
    def __init__(self, nx, ny, nz, kinds):
        self.nx, self.ny, self.depth, self.kinds = nx, ny, nz // 2, kinds
        self.size = HEAD_DIM // ny

    def starts(self, half, index, kind):
        x, z = index
        slots = [y * self.nx + x if half == 0 else x * self.ny + y for y in range(self.ny)]
        return [((slot * self.depth + z) * self.kinds + kind) * self.size for slot in slots]

    def read(self, ref, half, index, kind):
        return jnp.concatenate([ref[at : at + self.size, :] for at in self.starts(half, index, kind)], 0)

    def write(self, ref, half, index, kind, value):
        for k, at in enumerate(self.starts(half, index, kind)):
            ref[at : at + self.size, :] = value[k * self.size : (k + 1) * self.size]


def allowed_block(span_ref, base, columns, chunk):
    ahead = lax.broadcasted_iota(jnp.int32, (BLOCK, BLOCK), 0)
    if chunk < BLOCK:
        ahead = ahead + ahead // chunk * chunk
    away = ahead + (base - span_ref[0:1, columns])
    return (away >= 0) & (away <= span_ref[1:2, columns])


def span_of(index):
    return slice(index * BLOCK, (index + 1) * BLOCK)


def per_block(need_ref, base_ref, span_ref, columns, chunk, i, j, work):
    need = need_ref[i * BLOCKS + j]

    @pl.when(need == 1)
    def _():
        allowed = allowed_block(span_ref, base_ref[j], columns, chunk)
        work(lambda scores: jnp.where(allowed, scores, MASKED))

    @pl.when(need == 2)
    def _():
        work(lambda scores: scores)


def attend_kernel(heads, layouts, chunk, need_ref, base_ref, span_ref, *refs):
    *layouts, single = layouts
    count = len(layouts)
    mixed_ref, lse_ref, q_s, k_s, v_s, top_s, sum_s, acc_s = refs[count:]
    where = [(source, lay, kind) for source, lay in zip(refs[:count], layouts) for kind in range(lay.kinds)]
    every = range(len(heads))

    def load(half):
        for h, index in enumerate(heads):
            q, k, v = (lay.read(source, half, index, kind) for source, lay, kind in where)
            q_s[h] = (q.astype(F32) * SCALE).astype(BF)
            k_s[h] = k.T
            v_s[h] = v

    half_now = pl.program_id(0)
    for half in range(2):
        pl.when(half_now == half)(functools.partial(load, half))

    for i in range(BLOCKS):
        columns = span_of(i)
        top_s[...] = jnp.full(top_s.shape, -3e38, F32)
        sum_s[...] = jnp.zeros(sum_s.shape, F32)
        acc_s[...] = jnp.zeros(acc_s.shape, F32)
        for j in range(BLOCKS):
            keys = span_of(j)

            def work(mask, keys=keys, columns=columns):
                scores = [mask(dot(k_s[h, keys, :], q_s[h, :, columns], 1, 0)) for h in every]
                tops = [jnp.maximum(top_s[h], jnp.max(scores[h], 0, keepdims=True)) for h in every]
                weights = [jnp.exp(scores[h] - tops[h]) for h in every]
                fades = [jnp.exp(top_s[h] - tops[h]) for h in every]
                mixed = [dot(v_s[h, :, keys], weights[h].astype(BF), 1, 0) for h in every]
                for h in every:
                    top_s[h] = tops[h]
                    sum_s[h] = sum_s[h] * fades[h] + jnp.sum(weights[h], 0, keepdims=True)
                    acc_s[h] = acc_s[h] * fades[h] + mixed[h]

            per_block(need_ref, base_ref, span_ref, columns, chunk, i, j, work)

        for h in every:
            lse_ref[0, h, :, columns] = top_s[h] + jnp.log(sum_s[h])
            q_s[h, :, columns] = (acc_s[h] / sum_s[h]).astype(BF)

    def store(half):
        for h, index in enumerate(heads):
            single.write(mixed_ref, half, index, 0, q_s[h])

    for half in range(2):
        pl.when(half_now == half)(functools.partial(store, half))


def attend_back_kernel(heads, layouts, chunk, need_ref, base_ref, span_ref, *refs):
    *layouts, single = layouts
    count = len(layouts)
    mixed_ref, grad_ref, lse_ref = refs[count : count + 3]
    q_s, k_s, kt_s, v_s, g_s, inner_s, dq_s, dk_s, dv_s = refs[2 * count + 3 :]
    where = [(source, lay, kind) for source, lay in zip(refs[:count], layouts) for kind in range(lay.kinds)]
    outs = refs[count + 3 : 2 * count + 3]
    into = [(out, lay, kind) for out, lay in zip(outs, layouts) for kind in range(lay.kinds)]
    every = range(len(heads))

    def load(half):
        for h, index in enumerate(heads):
            q, k, v = (lay.read(source, half, index, kind) for source, lay, kind in where)
            q_s[h] = (q.astype(F32) * SCALE).astype(BF)
            kt_s[h] = k
            k_s[h] = k.T
            v_s[h] = v.T
            grad = single.read(grad_ref, half, index, 0)
            g_s[h] = grad
            mixed = single.read(mixed_ref, half, index, 0)
            inner_s[h] = jnp.sum(grad.astype(F32) * mixed.astype(F32), 0, keepdims=True)

    half_now = pl.program_id(0)
    for half in range(2):
        pl.when(half_now == half)(functools.partial(load, half))

    for acc in (dq_s, dk_s, dv_s):
        acc[...] = jnp.zeros(acc.shape, F32)

    for i in range(BLOCKS):
        columns = span_of(i)
        for j in range(BLOCKS):
            keys = span_of(j)

            def work(mask, keys=keys, columns=columns):
                scores = [mask(dot(k_s[h, keys, :], q_s[h, :, columns], 1, 0)) for h in every]
                steep = [dot(v_s[h, keys, :], g_s[h, :, columns], 1, 0) for h in every]
                chances = [jnp.exp(scores[h] - lse_ref[0, h, :, columns]) for h in every]
                back = [(chances[h] * (steep[h] - inner_s[h, :, columns])).astype(BF) for h in every]
                for h in every:
                    dv_s[h, :, keys] += dot(g_s[h, :, columns], chances[h].astype(BF), 1, 1)
                for h in every:
                    dk_s[h, :, keys] += dot(q_s[h, :, columns], back[h], 1, 1)
                for h in every:
                    dq_s[h, :, columns] += dot(kt_s[h, :, keys], back[h], 1, 0)

            per_block(need_ref, base_ref, span_ref, columns, chunk, i, j, work)

    def store(half):
        for h, index in enumerate(heads):
            made = (dq_s[h] * SCALE, dk_s[h], dv_s[h])
            for (out, lay, kind), value in zip(into, made):
                lay.write(out, half, index, kind, value.astype(BF))

    for half in range(2):
        pl.when(half_now == half)(functools.partial(store, half))


class Heads:
    def __init__(self, nx, ny, nz, chunk):
        self.nx, self.ny, self.nz, self.chunk = nx, ny, nz, chunk
        self.index = [(x, z) for x in range(nx) for z in range(nz // 2)]
        self.plain = (HEAD_DIM // ny) % 16 == 0

    def split(self, matrix, kinds):
        if self.plain:
            return matrix
        nx, ny, deep = self.nx, self.ny, self.nz // 2
        half, rows = matrix.shape[0] // 2, HEAD_DIM // ny
        first = matrix[:half].reshape(ny, nx, deep, kinds, rows, LEN).transpose(1, 2, 3, 0, 4, 5)
        second = matrix[half:].reshape(nx, ny, deep, kinds, rows, LEN).transpose(0, 2, 3, 1, 4, 5)
        return jnp.stack([first, second], 0).reshape(-1, LEN)

    def join(self, split, kinds):
        if self.plain:
            return split
        nx, ny, deep = self.nx, self.ny, self.nz // 2
        cut = split.reshape(2, nx, deep, kinds, ny, HEAD_DIM // ny, LEN)
        first = cut[0].transpose(3, 0, 1, 2, 4, 5).reshape(-1, LEN)
        second = cut[1].transpose(0, 3, 1, 2, 4, 5).reshape(-1, LEN)
        return jnp.concatenate([first, second], 0)

    def call(self, kernel, kinds, tables, arrays, outs, scratch, flops):
        need, bases, spans = tables
        layouts = [Rows(self.nx, self.ny if self.plain else 1, self.nz, k) for k in kinds + (1,)]

        def by_half(shape):
            rest = (0,) * (len(shape) - 1)
            return pl.BlockSpec((shape[0] // 2,) + tuple(shape[1:]), lambda i, *_: (i,) + rest)

        return pl.pallas_call(
            functools.partial(kernel, self.index, layouts, self.chunk),
            out_shape=outs,
            grid_spec=pltpu.PrefetchScalarGridSpec(
                num_scalar_prefetch=2,
                grid=(2,),
                in_specs=[pl.BlockSpec((2, LEN), lambda i, *_: (0, 0))] + [by_half(a.shape) for a in arrays],
                out_specs=[by_half(o.shape) for o in outs],
                scratch_shapes=scratch,
            ),
            compiler_params=pltpu.CompilerParams(vmem_limit_bytes=30 * 2**20),
            cost_estimate=pl.CostEstimate(flops=flops, bytes_accessed=8 * 2**20, transcendentals=4 * 2**20),
        )(need, bases, spans, *arrays)

    def attend(self, tables, sources, kinds):
        count = len(self.index)
        split = [self.split(s, k) for s, k in zip(sources, kinds)]
        wide = (count, HEAD_DIM, LEN)
        mixed, lse = self.call(
            attend_kernel,
            kinds,
            tables,
            split,
            [
                jax.ShapeDtypeStruct((2 * count * HEAD_DIM, LEN), BF),
                jax.ShapeDtypeStruct((2, count, 1, LEN), F32),
            ],
            [
                pltpu.VMEM(wide, BF),
                pltpu.VMEM((count, LEN, HEAD_DIM), BF),
                pltpu.VMEM(wide, BF),
                pltpu.VMEM((count, 1, BLOCK), F32),
                pltpu.VMEM((count, 1, BLOCK), F32),
                pltpu.VMEM((count, HEAD_DIM, BLOCK), F32),
            ],
            40 * 10**9,
        )
        return self.join(mixed, 1), lse

    def attend_back(self, tables, sources, kinds, mixed, grad, lse):
        count = len(self.index)
        split = [self.split(s, k) for s, k in zip(sources, kinds)]
        wide, tall = (count, HEAD_DIM, LEN), (count, LEN, HEAD_DIM)
        grads = self.call(
            attend_back_kernel,
            kinds,
            tables,
            split + [self.split(mixed, 1), self.split(grad, 1), lse],
            [jax.ShapeDtypeStruct(s.shape, BF) for s in split],
            [
                pltpu.VMEM(wide, BF),
                pltpu.VMEM(tall, BF),
                pltpu.VMEM(wide, BF),
                pltpu.VMEM(tall, BF),
                pltpu.VMEM(wide, BF),
                pltpu.VMEM((count, 1, LEN), F32),
                pltpu.VMEM(wide, F32),
                pltpu.VMEM(wide, F32),
                pltpu.VMEM(wide, F32),
            ],
            46 * 10**9,
        )
        return [self.join(g, k) for g, k in zip(grads, kinds)]


def body(
    inputs,
    memory,
    cotangent,
    tgt_lengths,
    src_ids,
    gain_one,
    w_query,
    w_key,
    w_value,
    w_out,
    gain_two,
    w_cross_query,
    w_mem_key,
    w_mem_value,
    w_cross_out,
    gain_three,
    w_up,
    w_down,
):
    nx, ny, nz = (lax.axis_size(a) for a in ("batch", "yy", "head"))
    ix, iy, core, iz = (lax.axis_index(a) for a in ("batch", "yy", "core", "head"))
    rows = inputs.shape[0]
    nxy, place = nx * ny, ix * ny + iy
    chunk = LEN // (2 * ny)

    def part(matrix):
        deep = matrix.shape[0] // 2 // nxy
        return lax.dynamic_slice_in_dim(matrix, (core * nxy + place) * deep, deep, 0)

    def column_parts(*matrices):
        parts = []
        for matrix in matrices:
            wide = matrix.shape[1] // 2
            turned = lax.dynamic_slice_in_dim(matrix, core * wide, wide, 1).T
            parts.append(lax.dynamic_slice_in_dim(turned, place * (wide // nxy), wide // nxy, 0))
        return jnp.concatenate(parts, 0)

    row = iy * nz + iz
    lengths = lax.dynamic_index_in_dim(tgt_lengths, row, 0, keepdims=False)
    source_ids = lax.dynamic_index_in_dim(src_ids, row, 0, keepdims=False)
    index = jnp.arange(LEN, dtype=jnp.int32)
    within = index % (LEN // 2)
    turn = jnp.where(index < LEN // 2, core, 1 - core)
    positions = (2 * (within // chunk) + turn) * chunk + within % chunk
    ends = jnp.cumsum(lengths)
    starts = ends - lengths
    reached = positions[:, None] >= starts[None, :]
    target_ids = jnp.sum(reached.astype(jnp.int32), -1) - 1
    self_start = jnp.max(jnp.where(reached, starts[None, :], 0), -1)
    kinds = jnp.arange(lengths.shape[0], dtype=jnp.int32)
    source_start = jnp.sum((source_ids[None, :] < kinds[:, None]).astype(jnp.int32), -1)
    source_end = jnp.sum((source_ids[None, :] <= kinds[:, None]).astype(jnp.int32), -1) - 1
    mine = target_ids[:, None] == kinds[None, :]
    cross_start = jnp.sum(jnp.where(mine, source_start[None, :], 0), -1)
    cross_end = jnp.sum(jnp.where(mine, source_end[None, :], 0), -1)
    block_positions = positions.reshape(BLOCKS, BLOCK)
    lowest, highest = jnp.min(block_positions, 1), jnp.max(block_positions, 1)

    def tables_of(start, end):
        least = jnp.min(start.reshape(BLOCKS, BLOCK), 1)
        most = jnp.max(end.reshape(BLOCKS, BLOCK), 1)
        some = (least[:, None] <= highest[None, :]) & (most[:, None] >= lowest[None, :])
        last, first = jnp.max(start.reshape(BLOCKS, BLOCK), 1), jnp.min(end.reshape(BLOCKS, BLOCK), 1)
        whole = (last[:, None] <= lowest[None, :]) & (first[:, None] >= highest[None, :])
        need = jnp.where(whole, 2, some.astype(jnp.int32))
        return need.reshape(-1), lowest, jnp.stack([start, end - start], 0)

    self_tables = tables_of(self_start, positions)
    cross_tables = tables_of(cross_start, cross_end)
    heads = Heads(nx, ny, nz, chunk)

    residual = to_row(inputs).astype(F32)
    self_weights = Gather([column_parts(w_query, w_key, w_value)])
    residual = to_row(tied(inputs, self_weights.got))
    self_weights.two()
    residual = meet(residual, self_weights)
    self_weights.three()
    cross_weights = Gather(
        [part(w_out), column_parts(w_mem_key, w_mem_value), column_parts(w_cross_query), part(w_cross_out)],
        residual,
    )
    (normed_one,) = normalize([tied(residual, self_weights.mine, cross_weights.mine)], gain_one)
    normed_one = both(normed_one)
    normed_one = meet(normed_one, self_weights)
    (w_self,) = self_weights.result()
    qkv = dot(w_self, normed_one, 1, 1).astype(BF)
    qkv = meet(qkv, cross_weights)
    cross_weights.two()
    up_weights = Gather([column_parts(w_up)], cross_weights.mine)
    source_own = to_row(tied(memory, up_weights.mine))
    qkv = meet(qkv, cross_weights)
    cross_weights.three()
    qkv = tied(qkv, cross_weights.mine)
    self_mixed, self_lse = heads.attend(self_tables, (qkv,), (3,))
    self_mixed, source_own = meet((self_mixed, source_own), cross_weights, up_weights)
    down_weights = Gather([part(w_down)], up_weights.got)
    up_weights.two()
    self_mixed = tied(self_mixed, up_weights.mine, down_weights.mine)
    w_o, w_mem, w_cq, w_co = cross_weights.result()
    normed_two, after_self = normalize([residual, *own_parts(self_mixed, w_o)], gain_two)
    normed_two, down_weights.got[0] = meet((normed_two, down_weights.got[0]), up_weights)
    up_weights.three()
    normed_two, source_own = tied((normed_two, source_own), up_weights.mine)
    source = both(source_own)
    mkv = dot(w_mem, source, 1, 1).astype(BF)
    normed_two = both(normed_two)
    cq = dot(w_cq, normed_two, 1, 1).astype(BF)
    cq, mkv = meet((cq, mkv), down_weights)
    down_weights.two()
    cq = tied(cq, down_weights.mine)
    cot_own = to_row(tied(cotangent, down_weights.mine))
    cross_mixed, cross_lse = heads.attend(cross_tables, (cq, mkv), (1, 2))
    cross_mixed, cot_own = meet((cross_mixed, cot_own), up_weights, down_weights)
    down_weights.three()
    cross_mixed = tied(cross_mixed, down_weights.mine)
    cot = both(cot_own)
    normed_three, after_cross = normalize([after_self, *own_parts(cross_mixed, w_co)], gain_three)
    normed_three = both(normed_three)
    (w_u,) = up_weights.result()

    def weight_grad(transposed, tokens):
        return dot(transposed, tokens, 1, 0).astype(BF)

    hidden_pre = dot(w_u, normed_three, 1, 1)
    squared = hidden_pre * hidden_pre
    bent = jnp.tanh(GELU_A * hidden_pre * (1.0 + GELU_B * squared))
    gate = 0.5 + 0.5 * bent
    slope = gate + (0.5 * GELU_A) * hidden_pre * (1.0 - bent * bent) * (1.0 + 3.0 * GELU_B * squared)
    hidden_act, slope = lax.optimization_barrier(((hidden_pre * gate).astype(BF), slope.astype(BF)))
    down_sum = Sum([weight_grad(hidden_act, cot)])
    hidden_act = meet(tied(hidden_act, down_sum.mine), down_weights)
    (w_d,) = down_weights.result()
    output = (after_cross + own_sum(hidden_act, w_d)).astype(BF)
    output = from_row(output, rows)

    grad_pre = (slope.astype(F32) * dot(w_d, cot, 1, 1)).astype(BF)
    grad_pre = meet(grad_pre, down_sum)
    down_sum.two()
    third_back = own_parts(tied(grad_pre, down_sum.mine), w_u)
    grad_after_cross, cross_grad, grad_gain_three = normalize_back(after_cross, gain_three, third_back, cot_own)

    cross_grad = both(cross_grad)
    up_sum = Sum([weight_grad(tied(grad_pre, down_sum.mine), normed_three)])
    grad_cross_mixed = dot(w_co, cross_grad, 1, 1).astype(BF)
    grad_cross_mixed = meet(grad_cross_mixed, down_sum)
    down_sum.three()
    grad_cross_mixed = tied(grad_cross_mixed, up_sum.mine, down_sum.mine)
    gcq, gmkv = heads.attend_back(
        cross_tables, (cq, mkv), (1, 2), cross_mixed, grad_cross_mixed, cross_lse
    )
    gcq, gmkv, output = meet((gcq, gmkv, output), up_sum, down_sum)
    up_sum.two()
    down_total = down_sum.result()
    gcq, gmkv = tied((gcq, gmkv), up_sum.mine)
    grad_after_self, self_grad, grad_gain_two = normalize_back(
        after_self, gain_two, own_parts(gcq, w_cq), grad_after_cross
    )
    self_grad = meet(self_grad, up_sum)
    up_sum.three()
    self_grad = both(self_grad)
    g_co = weight_grad(cross_mixed, cross_grad)
    g_cq = weight_grad(gcq, normed_two)
    g_mem = weight_grad(gmkv, source)
    g_o = weight_grad(self_mixed, self_grad)
    cross_sum = Sum([g_co, g_cq, g_mem])
    memory_back = own_sum(gmkv, w_mem).astype(BF)
    grad_self_mixed = dot(w_o, self_grad, 1, 1).astype(BF)
    grad_self_mixed, memory_back, g_o, down_total = meet(
        (grad_self_mixed, memory_back, g_o, down_total), cross_sum
    )
    down_all = gathered(down_total)
    cross_sum.two()
    grad_self_mixed = tied(grad_self_mixed, up_sum.mine, cross_sum.mine)
    grad_memory = from_row(memory_back, rows)
    (gqkv,) = heads.attend_back(self_tables, (qkv,), (3,), self_mixed, grad_self_mixed, self_lse)
    gqkv = meet(gqkv, cross_sum, up_sum)
    g_self = weight_grad(gqkv, normed_one)
    gqkv, g_self, cross_sum.got = lax.optimization_barrier((gqkv, g_self, cross_sum.got))
    self_sum = Sum([g_o, g_self])
    cross_sum.three()
    first_back, grad_memory = lax.optimization_barrier((own_parts(gqkv, w_self), grad_memory))
    _, grad_inputs, grad_gain_one = normalize_back(residual, gain_one, first_back, grad_after_self)
    grad_inputs, up_total = meet((grad_inputs, up_sum.result()), self_sum, cross_sum)
    grad_inputs = from_row(grad_inputs, rows).astype(F32)
    self_sum.two()
    up_all = gathered(up_total)
    gains = jnp.stack([grad_gain_one, grad_gain_two, grad_gain_three])
    for axis in ("core", "yy", "batch"):
        gains = total_of(gains, axis)
    cross_total = meet(cross_sum.result(), self_sum)
    self_sum.three()

    deep = w_query.shape[1] // 2 // nxy
    far = w_up.shape[1] // 2 // nxy
    (grad_down,) = unfold(down_all, [(far, False)])
    (grad_up,) = unfold(up_all, [(far, True)])
    cross_grads = unfold(gathered(cross_total), [(deep, False), (deep, True), (deep, True), (deep, True)])
    grad_memory = grad_memory.astype(F32)
    self_sum.got, grad_down, grad_memory, gains = lax.optimization_barrier(
        (self_sum.got, grad_down, grad_memory, gains)
    )
    gains = total_of(gains, "head")
    self_all, grad_up, (grad_inputs, gains), cross_grads = replicate(
        self_sum.result(), grad_up, (grad_inputs, gains), cross_grads
    )
    grad_co, grad_cq, grad_mk, grad_mv = cross_grads
    grad_o, grad_q, grad_k, grad_v = unfold(
        self_all, [(deep, False), (deep, True), (deep, True), (deep, True)]
    )
    return (
        output,
        grad_inputs,
        grad_memory,
        gains[0],
        grad_q,
        grad_k,
        grad_v,
        grad_o,
        gains[1],
        grad_cq,
        grad_mk,
        grad_mv,
        grad_co,
        gains[2],
        grad_up,
        grad_down,
    )


def solution(mesh):
    nb, ns, nh = (mesh.shape[a] for a in ("batch", "seq", "head"))
    fine = Mesh(mesh.devices.reshape(nb, ns // 2, 2, nh), ("batch", "yy", "core", "head"))
    tokens = P("batch", ("yy", "core", "head"), None)
    ids = P("batch", None)
    wide, tall = P(None, "head"), P("head", None)
    return jax.shard_map(
        body,
        mesh=fine,
        in_specs=(
            tokens, tokens, tokens, ids, ids,
            P(), wide, wide, wide, tall,
            P(), wide, wide, wide, tall,
            P(), wide, tall,
        ),
        out_specs=(
            tokens, tokens, tokens,
            P(), wide, wide, wide, tall,
            P(), wide, wide, wide, tall,
            P(), wide, tall,
        ),
        check_vma=False,
    )
```
